32 devices in a mesh: dp: 8 (over z, core), mp: 4 (over y, x).
Axes of the slice: x: 2, y: 2, z: 4, core: 2. Of those that a mesh axis runs over, the one named last changes fastest.
Arguments:
- frames_in: bfloat16 [16, 1024, 1536], P('dp', 'mp'), may hold values from -6 to 6
- prompt: bfloat16 [16, 128, 768], P('dp'), may hold values from -6 to 6
- lengths: int32 [16], P('dp'), may hold values from 4 to 128, as said below
- tsteps: int32 [16], P('dp'), may hold values from 0 to 999
- table: float32 [1000, 1536], replicated, may hold values from -6 to 6
- gain_one: float32 [1536], replicated, may hold values from 0.25 to 1.75
- shift_one: float32 [1536], replicated, may hold values from -2 to 2
- gain_two: float32 [1536], replicated, may hold values from 0.25 to 1.75
- shift_two: float32 [1536], replicated, may hold values from -2 to 2
- gain_three: float32 [1536], replicated, may hold values from 0.25 to 1.75
- shift_three: float32 [1536], replicated, may hold values from -2 to 2
- w_query: bfloat16 [1536, 1536], P(None, 'mp'), may hold values from -0.15625 to 0.15625
- w_key: bfloat16 [1536, 1536], P(None, 'mp'), may hold values from -0.15625 to 0.15625
- w_value: bfloat16 [1536, 1536], P(None, 'mp'), may hold values from -0.15625 to 0.15625
- w_out: bfloat16 [1536, 1536], P('mp'), may hold values from -2.5 to 2.5
- c_query: bfloat16 [1536, 1536], P(None, 'mp'), may hold values from -0.15625 to 0.15625
- c_key: bfloat16 [768, 1536], P(None, 'mp'), may hold values from -0.21875 to 0.21875
- c_value: bfloat16 [768, 1536], P(None, 'mp'), may hold values from -0.21875 to 0.21875
- c_out: bfloat16 [1536, 1536], P('mp'), may hold values from -0.75 to 0.75
- w_gate: bfloat16 [1536, 6144], P(None, 'mp'), may hold values from -0.15625 to 0.15625
- w_up: bfloat16 [1536, 6144], P(None, 'mp'), may hold values from -0.15625 to 0.15625
- w_down: bfloat16 [6144, 1536], P('mp'), may hold values from -0.078125 to 0.078125
- cotangent: bfloat16 [16, 1024, 1536], P('dp', 'mp'), may hold values from -6 to 6
Outputs:
- output: float32 [16, 1024, 1536], P('dp', 'mp')
- grad_frames: float32 [16, 1024, 1536], P('dp', 'mp')
- grad_table: float32 [1000, 1536], replicated
- grad_gain_one: float32 [1536], replicated
- grad_shift_one: float32 [1536], replicated
- grad_gain_two: float32 [1536], replicated
- grad_shift_two: float32 [1536], replicated
- grad_gain_three: float32 [1536], replicated
- grad_shift_three: float32 [1536], replicated
- grad_w_query: float32 [1536, 1536], P('dp', 'mp')
- grad_w_key: float32 [1536, 1536], P('dp', 'mp')
- grad_w_value: float32 [1536, 1536], P('dp', 'mp')
- grad_w_out: float32 [1536, 1536], P('mp', 'dp')
- grad_c_query: float32 [1536, 1536], P('dp', 'mp')
- grad_c_key: float32 [768, 1536], P('dp', 'mp')
- grad_c_value: float32 [768, 1536], P('dp', 'mp')
- grad_c_out: float32 [1536, 1536], P('mp', 'dp')
- grad_w_gate: float32 [1536, 6144], P('dp', 'mp')
- grad_w_up: float32 [1536, 6144], P('dp', 'mp')
- grad_w_down: float32 [6144, 1536], P('mp', 'dp')
The draws below stay inside these ranges and needn't reach their ends.
Inputs may be any that keep to these rules, and one draw needn't show every extreme that they name: lengths: some clip has all 128 prompt tokens live and another has 4.
All inputs are finite; a program needn't handle non-finite values.
Results may differ from the reference program's by a relative error of at most 0.025.
Values may be sent and summed in bfloat16 or wider, within the bound.
No kernel may reach another device: no remote copies, remote signals or barrier semaphores. Data moves between devices by JAX's collectives and lax.ppermute only.
A program may use at most 384 MiB of HBM per device.

```python
import math
import jax
import jax.numpy as jnp
from jax import lax

HEAD_DIM = 64
D = 1536
FF = 6144
TEXT_DIM = 768
PROMPT = 128
STEPS = 1000
FRAMES = 1024
CLIPS = 16


def draw_lengths(key, part):
    key = jax.random.fold_in(key, 11)
    first_key, second_key, third_key = jax.random.split(key, 3)
    spread = PROMPT - 3
    drawn = jax.random.randint(first_key, (CLIPS,), 0, spread)
    cubed = drawn * drawn // (spread - 1) * drawn // (spread - 1)
    longest = jax.random.randint(second_key, (), 0, CLIPS)
    offset = jax.random.randint(third_key, (), 1, CLIPS)
    shortest = (longest + offset) % CLIPS
    places = jnp.arange(CLIPS)
    result = jnp.where(places == longest, PROMPT, 4 + cubed)
    result = jnp.where(places == shortest, 4, result)
    return result.astype(jnp.int32)


def with_ends(values, stream_key, smallest, top_value):
    longest = values.shape.index(max(values.shape))
    spots = []
    for shift in (0, 1):
        where = [jax.random.randint(jax.random.fold_in(stream_key, axis), (), 0, length) for axis, length in enumerate(values.shape)]
        where[longest] = (where[longest] + shift) % values.shape[longest]
        spots.append(tuple(where))
    return values.at[spots[0]].set(smallest).at[spots[1]].set(top_value)


def steps_of(rng, shape, cuts, low, largest):
    def one(axis_at, blocks):
        draws = jax.random.uniform(jax.random.fold_in(jax.random.fold_in(rng, 6), axis_at), (blocks,), jnp.float32, low / len(cuts), largest / len(cuts))
        return jnp.repeat(jnp.exp(draws), shape[axis_at] // blocks).reshape((-1,) + (1,) * (len(shape) - axis_at - 1))

    loudness = one(*cuts[0])
    for cut in cuts[1:]:
        loudness = loudness * one(*cut)
    return loudness


def noise(key, extent, scale, reach, shards=(), kind=jnp.bfloat16):
    entries = scale * jax.random.normal(key, extent, jnp.float32)
    if shards:
        entries = entries * steps_of(key, extent, shards, -0.22, 0.18)
    return jnp.clip(entries, -reach, reach).astype(kind)


def setup_inputs(seed: int = 0) -> dict:
    key_list = jax.random.split(jax.random.key(seed), 24)
    return {
        "frames_in": noise(key_list[0], (CLIPS, FRAMES, D), 1.0, 6.0, ((0, 8), (1, 4))),
        "prompt": noise(key_list[1], (CLIPS, PROMPT, TEXT_DIM), 1.0, 6.0, ((0, 8),)),
        "lengths": draw_lengths(jax.random.fold_in(key_list[23], 71), 0),
        "tsteps": with_ends(jax.random.randint(key_list[3], (CLIPS,), 0, STEPS), jax.random.fold_in(key_list[3], 1), 0, STEPS - 1).astype(jnp.int32),
        "table": noise(key_list[4], (STEPS, D), 1.0, 6.0, (), jnp.float32),
        "gain_one": jnp.clip(1.0 + 0.15 * jax.random.normal(key_list[5], (D,), jnp.float32), 0.25, 1.75),
        "shift_one": noise(key_list[6], (D,), 0.3, 2.0, (), jnp.float32),
        "gain_two": jnp.clip(1.0 + 0.15 * jax.random.normal(key_list[7], (D,), jnp.float32), 0.25, 1.75),
        "shift_two": noise(key_list[8], (D,), 0.3, 2.0, (), jnp.float32),
        "gain_three": jnp.clip(1.0 + 0.15 * jax.random.normal(key_list[9], (D,), jnp.float32), 0.25, 1.75),
        "shift_three": noise(key_list[10], (D,), 0.3, 2.0, (), jnp.float32),
        "w_query": noise(key_list[11], (D, D), D ** -0.5, 0.15625, ((1, 4),)),
        "w_key": noise(key_list[12], (D, D), D ** -0.5, 0.15625, ((1, 4),)),
        "w_value": noise(key_list[13], (D, D), D ** -0.5, 0.15625, ((1, 4),)),
        "w_out": noise(key_list[14], (D, D), (max(1, 4 * D // FRAMES)) ** -0.5, 2.5, ((0, 4),)),
        "c_query": noise(key_list[15], (D, D), D ** -0.5, 0.15625, ((1, 4),)),
        "c_key": noise(key_list[16], (TEXT_DIM, D), TEXT_DIM ** -0.5, 0.21875, ((1, 4),)),
        "c_value": noise(key_list[17], (TEXT_DIM, D), TEXT_DIM ** -0.5, 0.21875, ((1, 4),)),
        "c_out": noise(key_list[18], (D, D), (max(1, D // 24)) ** -0.5, 0.75, ((0, 4),)),
        "w_gate": noise(key_list[19], (D, FF), D ** -0.5, 0.15625, ((1, 4),)),
        "w_up": noise(key_list[20], (D, FF), D ** -0.5, 0.15625, ((1, 4),)),
        "w_down": noise(key_list[21], (FF, D), FF ** -0.5, 0.078125, ((0, 4),)),
        "cotangent": noise(key_list[22], (CLIPS, FRAMES, D), 1.0, 6.0, ((0, 8), (1, 4))),
    }


@jax.custom_vjp
def low(v):
    return lax.optimization_barrier(v.astype(jnp.bfloat16)).astype(jnp.float32)

@jax.custom_vjp
def low_back(v):
    return v

def low_keep(v):
    return (low(v), None)

def low_pass(kept, grad):
    return (grad,)

def back_keep(v):
    return (v, None)

def back_low(kept, grad):
    return (low(grad),)
low.defvjp(low_keep, low_pass)
low_back.defvjp(back_keep, back_low)
norm_eps = 1e-05
precise = lax.Precision.HIGHEST

def matmul(left, right):
    return jnp.dot(left, right, precision=precise)

def layer_norm(values, gain, shift):
    center = values - lax.optimization_barrier(jnp.mean(values, axis=-1, keepdims=True))
    scale = lax.rsqrt(lax.optimization_barrier(jnp.mean(center * center, axis=-1, keepdims=True)) + norm_eps)
    return center * scale * gain + shift

def turning(count, start):
    half = HEAD_DIM // 2
    places = (jnp.arange(count) + start).astype(jnp.float32)
    rates = jnp.exp(jnp.arange(half).astype(jnp.float32) * (-2.0 * math.log(10000.0) / HEAD_DIM))
    angles = places[:, None] * rates[None, :]
    return (jnp.cos(angles), jnp.sin(angles))

def rotate(values, cosine, sine):
    half = values.shape[-1] // 2
    first_half = values[..., :half]
    second_half = values[..., half:]
    cosine = cosine[:, None, :]
    sine = sine[:, None, :]
    return jnp.concatenate([first_half * cosine - second_half * sine, second_half * cosine + first_half * sine], axis=-1)

def split_heads(values):
    return values.reshape(values.shape[0], -1, HEAD_DIM)

def join_heads(values):
    return values.reshape(values.shape[0], -1)

def clip_layer(frames_in, params, prompt, length, tstep):
    table, gain_one, shift_one, gain_two, shift_two, gain_three, shift_three, w_query, w_key, w_value, w_out, c_query, c_key, c_value, c_out, w_gate, w_up, w_down = params
    frames = frames_in.shape[0]
    factor = 1.0 / math.sqrt(HEAD_DIM)
    picked = lax.dynamic_slice_in_dim(table, tstep.astype(jnp.int32), 1, 0)
    rows_one = jnp.concatenate([picked, frames_in], axis=0)
    normed_one = low(layer_norm(rows_one, gain_one, shift_one))
    cosine, sine = turning(frames + 1, 0)
    queries = low(rotate(split_heads(low_back(matmul(normed_one[1:], w_query))), cosine[1:], sine[1:]))
    keys = low(rotate(split_heads(low_back(matmul(normed_one, w_key))), cosine, sine))
    values = low(split_heads(low_back(matmul(normed_one, w_value))))
    scores = low_back(jnp.einsum('qhd,khd->hqk', queries, keys, precision=precise) * factor)
    self_probs = low(jax.nn.softmax(scores, axis=-1))
    self_mixed = low(low_back(jnp.einsum('hqk,khd->qhd', self_probs, values, precision=precise)))
    first = frames_in + low_back(matmul(join_heads(self_mixed), w_out))
    normed_two = low(layer_norm(first, gain_two, shift_two))
    cross_query = low(split_heads(low_back(matmul(normed_two, c_query))))
    cross_key = low(split_heads(low_back(matmul(prompt, c_key))))
    cross_value = low(split_heads(low_back(matmul(prompt, c_value))))
    live = jnp.arange(prompt.shape[0]) < length
    cross_scores = low_back(jnp.einsum('qhd,khd->hqk', cross_query, cross_key, precision=precise) * factor)
    cross_scores = jnp.where(live[None, None, :], cross_scores, -1e+30)
    cross_probs = low(jax.nn.softmax(cross_scores, axis=-1))
    cross_mixed = low(low_back(jnp.einsum('hqk,khd->qhd', cross_probs, cross_value, precision=precise)))
    second = first + low_back(matmul(join_heads(cross_mixed), c_out))
    normed_three = low(layer_norm(second, gain_three, shift_three))
    gate = low_back(matmul(normed_three, w_gate))
    upper = low_back(matmul(normed_three, w_up))
    hidden = low(jax.nn.silu(gate) * upper)
    return second + low_back(matmul(hidden, w_down))

def reference(frames_in, prompt, lengths, tsteps, table, gain_one, shift_one, gain_two, shift_two, gain_three, shift_three, w_query, w_key, w_value, w_out, c_query, c_key, c_value, c_out, w_gate, w_up, w_down, cotangent):
    params = tuple((member.astype(jnp.float32) for member in (table, gain_one, shift_one, gain_two, shift_two, gain_three, shift_three, w_query, w_key, w_value, w_out, c_query, c_key, c_value, c_out, w_gate, w_up, w_down)))

    def per_clip(totals, inputs):
        clip_frames, clip_prompt, clip_length, clip_step, clip_grad = inputs

        def forward(frames_value, param_value):
            return clip_layer(frames_value, param_value, clip_prompt, clip_length, clip_step)
        result, pullback = jax.vjp(forward, clip_frames, params)
        grad_in, grad_params = pullback(clip_grad)
        totals = jax.tree.map(jnp.add, totals, grad_params)
        return (totals, (result, grad_in))
    zeros = jax.tree.map(jnp.zeros_like, params)
    inputs = (frames_in.astype(jnp.float32), prompt.astype(jnp.float32), lengths.astype(jnp.int32), tsteps.astype(jnp.int32), cotangent.astype(jnp.float32))
    totals, (output, grad_frames) = lax.scan(per_clip, zeros, inputs)
    return (output, grad_frames, totals[0], totals[1], totals[2], totals[3], totals[4], totals[5], totals[6], totals[7], totals[8], totals[9], totals[10], totals[11], totals[12], totals[13], totals[14], totals[15], totals[16], totals[17])
```

```python
import functools
import math

import jax
import jax.numpy as jnp
from jax import lax
from jax.experimental import pallas as pl
from jax.experimental.pallas import tpu as pltpu
from jax.sharding import PartitionSpec as P

HEAD_DIM = 64
HALF = HEAD_DIM // 2
FACTOR = 1.0 / math.sqrt(HEAD_DIM)

norm_eps = 1e-05

f32 = jnp.float32
bf16 = jnp.bfloat16


def dot(left, right, left_axis, right_axis):
    return lax.dot_general(
        left, right, (((left_axis,), (right_axis,)), ((), ())), preferred_element_type=f32
    )


def norm_forward(values, gain, shift):
    center = values - jnp.mean(values, axis=-1, keepdims=True)
    scale = lax.rsqrt(jnp.mean(center * center, axis=-1, keepdims=True) + norm_eps)
    normal = center * scale
    return (normal * gain + shift, normal, scale)


def norm_backward(grad, normal, scale, gain):
    inner = grad * gain
    return scale * (
        inner
        - jnp.mean(inner, axis=-1, keepdims=True)
        - normal * jnp.mean(inner * normal, axis=-1, keepdims=True)
    )


def bits_of(size):
    return [1 << place for place in range(size.bit_length() - 1)]


def swap(values, axis, k):
    return lax.ppermute(values, axis, [(i, i ^ k) for i in range(lax.axis_size(axis))])


def spread(values):
    size = lax.axis_size("mp")
    half = values.shape[0] // 2
    orders = (bits_of(size), bits_of(size)[::-1])
    parts = []
    for piece, order in zip((values[:half], values[half:]), orders):
        have = {0: piece}
        for bit in order:
            for k in list(have):
                have[k ^ bit] = swap(have[k], "mp", bit)
        parts.append(have)
    return [parts[p][k] for k in range(size) for p in (0, 1)]


def trade(blocks):
    return [blocks[0]] + [swap(blocks[k], "mp", k) for k in range(1, len(blocks))]


def settle(blocks):
    got = trade(blocks)
    total = got[0].astype(f32)
    for block in got[1:]:
        total = total + block.astype(f32)
    return total


def all_sum(values):
    for axis in ("mp", "dp"):
        for bit in bits_of(lax.axis_size(axis)):
            values = values + swap(values, axis, bit)
    return values


def whole_rows(shard):
    size = lax.axis_size("mp")
    rows, width = shard.shape
    core = lax.axis_index("dp") & 1
    mine = lax.dynamic_slice_in_dim(shard, core * (rows // 2), rows // 2, 0)
    got = jnp.concatenate(spread(mine)[2:], axis=0).reshape(size - 1, rows // 2, width)
    other = swap(got, "dp", 1)
    low = jnp.where(core == 0, got, other)
    high = jnp.where(core == 0, other, got)
    rest = jnp.concatenate([low, high], axis=1).reshape((size - 1) * rows, width)
    return jnp.concatenate([shard, rest], axis=0)


def whole_columns(shard):
    size = lax.axis_size("mp")
    depth = shard.shape[0] // lax.axis_size("dp")
    mine = lax.dynamic_slice_in_dim(shard, lax.axis_index("dp") * depth, depth, 0)
    wide = jnp.concatenate([mine] + [swap(mine, "mp", k) for k in range(1, size)], axis=1)
    return lax.all_gather(wide, "dp", axis=0, tiled=True)


def self_forward_kernel(block, q_ref, k_ref, v_ref, pk_ref, pv_ref, o_ref, l_ref):
    keys = k_ref[...]
    values = v_ref[...]
    front_key = pk_ref[...].astype(f32)
    front_value = pv_ref[...].astype(f32)
    for start in range(0, q_ref.shape[1], block):
        part = slice(start, start + block)
        queries = q_ref[:, part]
        scores = dot(keys, queries, 0, 0)
        front = jnp.sum(queries.astype(f32) * front_key, axis=0, keepdims=True)
        top = jnp.maximum(jnp.max(scores, axis=0, keepdims=True), front)
        weights = jnp.exp(scores - top)
        front_weight = jnp.exp(front - top)
        total = jnp.sum(weights, axis=0, keepdims=True) + front_weight
        mixed = dot(values, weights.astype(bf16), 1, 0)
        mixed = mixed + front_value * front_weight.astype(bf16).astype(f32)
        o_ref[:, part] = (mixed * (1.0 / total)).astype(bf16)
        l_ref[0, :, part] = top + jnp.log(total)


def self_backward_kernel(
    block,
    q_ref,
    k_ref,
    v_ref,
    g_ref,
    o_ref,
    l_ref,
    pk_ref,
    pv_ref,
    cos_ref,
    sin_ref,
    d_ref,
    dpk_ref,
    dpv_ref,
):
    frames = q_ref.shape[1]
    keys = k_ref[...]
    values = v_ref[...]
    front_key = pk_ref[...].astype(f32)
    front_value = pv_ref[...].astype(f32)
    grad_keys = jnp.zeros((HEAD_DIM, frames), f32)
    grad_values = jnp.zeros((HEAD_DIM, frames), f32)
    grad_front_key = jnp.zeros((HEAD_DIM, 1), f32)
    grad_front_value = jnp.zeros((HEAD_DIM, 1), f32)
    for start in range(0, frames, block):
        part = slice(start, start + block)
        queries = q_ref[:, part]
        grads = g_ref[:, part]
        wide_queries = queries.astype(f32)
        wide_grads = grads.astype(f32)
        logsum = l_ref[0, :, part]
        mixsum = jnp.sum(o_ref[:, part].astype(f32) * wide_grads, axis=0, keepdims=True)
        probs = jnp.exp(dot(keys, queries, 0, 0) - logsum)
        grad_probs = dot(values, grads, 0, 0)
        grad_scores = (probs * (grad_probs - mixsum)).astype(bf16)
        grad_values = grad_values + dot(grads, probs.astype(bf16), 1, 1)
        grad_keys = grad_keys + dot(queries, grad_scores, 1, 1)
        grad_queries = dot(keys, grad_scores, 1, 0)
        front = jnp.exp(jnp.sum(wide_queries * front_key, axis=0, keepdims=True) - logsum)
        grad_front = jnp.sum(wide_grads * front_value, axis=0, keepdims=True)
        grad_front = (front * (grad_front - mixsum)).astype(bf16).astype(f32)
        front = front.astype(bf16).astype(f32)
        grad_front_key += jnp.sum(wide_queries * grad_front, axis=1, keepdims=True)
        grad_front_value += jnp.sum(wide_grads * front, axis=1, keepdims=True)
        grad_queries = (grad_queries + front_key * grad_front) * FACTOR
        cosine = cos_ref[:, part]
        sine = sin_ref[:, part]
        upper, lower = grad_queries[:HALF], grad_queries[HALF:]
        d_ref[0, :HALF, part] = (upper * cosine + lower * sine).astype(bf16)
        d_ref[0, HALF:, part] = (lower * cosine - upper * sine).astype(bf16)
    cosine = cos_ref[...]
    sine = sin_ref[...]
    upper, lower = grad_keys[:HALF], grad_keys[HALF:]
    d_ref[1, :HALF, :] = (upper * cosine + lower * sine).astype(bf16)
    d_ref[1, HALF:, :] = (lower * cosine - upper * sine).astype(bf16)
    d_ref[2] = grad_values.astype(bf16)
    dpk_ref[...] = grad_front_key.astype(bf16)
    dpv_ref[...] = grad_front_value.astype(bf16)


def cross_forward_kernel(clip, heads, n_ref, q_ref, k_ref, v_ref, o_ref, l_ref):
    live = lax.broadcasted_iota(jnp.int32, (k_ref.shape[1], 1), 0) < n_ref[clip]
    for head in range(heads):
        part = slice(head * HEAD_DIM, (head + 1) * HEAD_DIM)
        scores = jnp.where(live, dot(k_ref[part], q_ref[part], 0, 0), -1e30)
        top = jnp.max(scores, axis=0, keepdims=True)
        weights = jnp.exp(scores - top)
        total = jnp.sum(weights, axis=0, keepdims=True)
        mixed = dot(v_ref[part], weights.astype(bf16), 1, 0)
        o_ref[part] = (mixed * (1.0 / total)).astype(bf16)
        l_ref[head] = top + jnp.log(total)


def cross_backward_kernel(
    clip, heads, n_ref, q_ref, k_ref, v_ref, g_ref, o_ref, l_ref, dq_ref, dk_ref, dv_ref
):
    live = lax.broadcasted_iota(jnp.int32, (k_ref.shape[1], 1), 0) < n_ref[clip]
    for head in range(heads):
        part = slice(head * HEAD_DIM, (head + 1) * HEAD_DIM)
        queries = q_ref[part]
        keys = k_ref[part]
        grads = g_ref[part]
        mixsum = jnp.sum(o_ref[part].astype(f32) * grads.astype(f32), axis=0, keepdims=True)
        scores = jnp.where(live, dot(keys, queries, 0, 0), -1e30)
        probs = jnp.exp(scores - l_ref[head])
        grad_scores = (probs * (dot(v_ref[part], grads, 0, 0) - mixsum)).astype(bf16)
        dq_ref[part] = (dot(keys, grad_scores, 1, 0) * FACTOR).astype(bf16)
        dk_ref[part] = dot(queries, grad_scores, 1, 1).astype(bf16)
        dv_ref[part] = dot(grads, probs.astype(bf16), 1, 1).astype(bf16)


def shape_of(shape, kind):
    return jax.ShapeDtypeStruct(shape, kind)


def params():
    return pltpu.CompilerParams(vmem_limit_bytes=40 * 2**20)


def self_cost(heads, frames, products):
    return pl.CostEstimate(
        flops=products * 2 * heads * frames * frames * HEAD_DIM * 4,
        bytes_accessed=products * 2 * heads * frames * HEAD_DIM * 2,
        transcendentals=heads * frames * frames,
    )


def self_forward(turned, front_keys, front_values):
    heads = front_keys.shape[0] // HEAD_DIM
    frames = turned.shape[1]

    def at(third):
        return pl.BlockSpec((HEAD_DIM, frames), lambda h: (third * heads + h, 0))

    column = pl.BlockSpec((HEAD_DIM, 1), lambda h: (h, 0))
    return pl.pallas_call(
        functools.partial(self_forward_kernel, frames),
        grid=(heads,),
        in_specs=[at(0), at(1), at(2), column, column],
        out_specs=[at(0), pl.BlockSpec((1, 1, frames), lambda h: (h, 0, 0))],
        out_shape=[
            shape_of((heads * HEAD_DIM, frames), bf16),
            shape_of((heads, 1, frames), f32),
        ],
        compiler_params=params(),
        cost_estimate=self_cost(heads, frames, 2),
        name="self_forward",
    )(turned, turned, turned, front_keys, front_values)


def self_backward(turned, grads, mixed, logsum, front_keys, front_values, cosine, sine):
    heads = front_keys.shape[0] // HEAD_DIM
    frames = turned.shape[1]

    def at(third):
        return pl.BlockSpec((HEAD_DIM, frames), lambda h: (third * heads + h, 0))

    column = pl.BlockSpec((HEAD_DIM, 1), lambda h: (h, 0))
    angles = pl.BlockSpec((HALF, frames), lambda h: (0, 0))
    return pl.pallas_call(
        functools.partial(self_backward_kernel, min(256, frames)),
        grid=(heads,),
        in_specs=[
            at(0),
            at(1),
            at(2),
            at(0),
            at(0),
            pl.BlockSpec((1, 1, frames), lambda h: (h, 0, 0)),
            column,
            column,
            angles,
            angles,
        ],
        out_specs=[
            pl.BlockSpec((3, HEAD_DIM, frames), lambda h: (0, h, 0)),
            column,
            column,
        ],
        out_shape=[
            shape_of((3, heads * HEAD_DIM, frames), bf16),
            shape_of((heads * HEAD_DIM, 1), bf16),
            shape_of((heads * HEAD_DIM, 1), bf16),
        ],
        compiler_params=params(),
        cost_estimate=self_cost(heads, frames, 5),
        name="self_backward",
    )(turned, turned, turned, grads, mixed, logsum, front_keys, front_values, cosine, sine)


def cross_specs(groups, heads, frames, slots):
    at_frames = pl.BlockSpec((heads * HEAD_DIM, frames), lambda h: (h, 0))
    at_slots = pl.BlockSpec((heads * HEAD_DIM, slots), lambda h: (h, 0))
    at_sums = pl.BlockSpec((heads, 1, frames), lambda h: (h, 0, 0))
    return (at_frames, at_slots, at_sums)


def cross_cost(rows, frames, slots, products):
    return pl.CostEstimate(
        flops=products * 2 * rows * frames * slots * 4,
        bytes_accessed=products * 2 * rows * frames,
        transcendentals=rows // HEAD_DIM * frames * slots,
    )


def cross_forward(clip, groups, lengths, queries, keys, values):
    rows, frames = queries.shape
    heads = rows // HEAD_DIM // groups
    slots = keys.shape[1]
    at_frames, at_slots, at_sums = cross_specs(groups, heads, frames, slots)
    return pl.pallas_call(
        functools.partial(cross_forward_kernel, clip, heads),
        grid=(groups,),
        in_specs=[pl.BlockSpec(memory_space=pltpu.SMEM), at_frames, at_slots, at_slots],
        out_specs=[at_frames, at_sums],
        out_shape=[
            shape_of((rows, frames), bf16),
            shape_of((rows // HEAD_DIM, 1, frames), f32),
        ],
        compiler_params=params(),
        cost_estimate=cross_cost(rows, frames, slots, 2),
        name="cross_forward",
    )(lengths, queries, keys, values)


def cross_backward(clip, groups, lengths, queries, keys, values, grads, mixed, logsum):
    rows, frames = queries.shape
    heads = rows // HEAD_DIM // groups
    slots = keys.shape[1]
    at_frames, at_slots, at_sums = cross_specs(groups, heads, frames, slots)
    return pl.pallas_call(
        functools.partial(cross_backward_kernel, clip, heads),
        grid=(groups,),
        in_specs=[
            pl.BlockSpec(memory_space=pltpu.SMEM),
            at_frames,
            at_slots,
            at_slots,
            at_frames,
            at_frames,
            at_sums,
        ],
        out_specs=[at_frames, at_slots, at_slots],
        out_shape=[
            shape_of((rows, frames), bf16),
            shape_of((rows, slots), bf16),
            shape_of((rows, slots), bf16),
        ],
        compiler_params=params(),
        cost_estimate=cross_cost(rows, frames, slots, 5),
        name="cross_backward",
    )(lengths, queries, keys, values, grads, mixed, logsum)


def turning(rows):
    size = lax.axis_size("mp")
    me = lax.axis_index("mp")
    starts = jnp.stack([(me ^ k) * rows for k in range(size)])
    places = (starts[:, None] + jnp.arange(rows)[None, :] + 1).reshape(-1).astype(f32)
    rates = jnp.exp(jnp.arange(HALF).astype(f32) * (-2.0 * math.log(10000.0) / HEAD_DIM))
    angles = rates[:, None] * places[None, :]
    return (jnp.cos(angles), jnp.sin(angles))


def turn(values, cosine, sine):
    pairs = values.reshape(-1, 2, HALF, values.shape[-1])
    upper, lower = pairs[:, 0], pairs[:, 1]
    return jnp.stack([upper * cosine - lower * sine, lower * cosine + upper * sine], axis=1).reshape(
        values.shape
    )


def row_blocks(values, count):
    return jnp.split(values, count, axis=0)


def sum_over_clips(values, axis):
    return lax.psum_scatter(values.astype(bf16), "dp", scatter_dimension=axis, tiled=True)


def shards(
    frames_in,
    prompt,
    lengths,
    tsteps,
    table,
    gain_one,
    shift_one,
    gain_two,
    shift_two,
    gain_three,
    shift_three,
    w_query,
    w_key,
    w_value,
    w_out,
    c_query,
    c_key,
    c_value,
    c_out,
    w_gate,
    w_up,
    w_down,
    cotangent,
):
    size = lax.axis_size("mp")
    count, rows, width = frames_in.shape
    clips = range(count)
    local = w_query.shape[1]

    resid = [frames_in[b].astype(f32) for b in clips]
    ones = [norm_forward(resid[b], gain_one, shift_one) for b in clips]
    whole_one = [jnp.concatenate(spread(ones[b][0].astype(bf16)), axis=0) for b in clips]

    picked = jnp.take(table, tsteps, axis=0)
    prefix_normed, prefix_normal, prefix_scale = norm_forward(picked, gain_one, shift_one)
    prefix_low = prefix_normed.astype(bf16)
    cosine, sine = turning(rows)

    w_self = jnp.concatenate([w_query, w_key, w_value], axis=1)
    front = dot(w_self[:, local:], prefix_low, 0, 1).astype(bf16)
    front_keys = [front[:local, b : b + 1] for b in clips]
    front_values = [front[local:, b : b + 1] for b in clips]

    out_all = whole_rows(w_out)
    c_out_all = whole_rows(c_out)
    c_query_all = whole_columns(c_query)

    memory = jnp.concatenate([c_key, c_value], axis=1)
    memory = jnp.stack([dot(memory, prompt[b], 0, 1).astype(bf16) for b in clips])
    memory = jnp.stack([memory] + [swap(memory, "mp", k) for k in range(1, size)], axis=1)
    cross_keys = [memory[b, :, :local].reshape(size * local, -1) for b in clips]
    cross_values = [memory[b, :, local:].reshape(size * local, -1) for b in clips]

    turned, mixed_part, logsum, mixed = [], [], [], []
    for b in clips:
        raw = dot(w_self, whole_one[b], 0, 1)
        queries = (turn(raw[:local], cosine, sine) * FACTOR).astype(bf16)
        keys = turn(raw[local : 2 * local], cosine, sine).astype(bf16)
        turned.append(jnp.concatenate([queries, keys, raw[2 * local :].astype(bf16)], axis=0))
        out, sums = self_forward(turned[b], front_keys[b], front_values[b])
        mixed_part.append(out)
        logsum.append(sums)
        mixed.append(jnp.concatenate(trade(jnp.split(out, size, axis=1)), axis=0))

    first, twos, normed_two, cross_query, cross_sums, cross_mixed = [], [], [], [], [], []
    second, threes, whole_three = [], [], []
    for b in clips:
        first.append(resid[b] + dot(mixed[b], out_all, 0, 0))
        twos.append(norm_forward(first[b], gain_two, shift_two))
        normed_two.append(twos[b][0].astype(bf16))
        cross_query.append((dot(c_query_all, normed_two[b], 0, 1) * FACTOR).astype(bf16))
        out, sums = cross_forward(
            b, size, lengths, cross_query[b], cross_keys[b], cross_values[b]
        )
        cross_mixed.append(out)
        cross_sums.append(sums)
        second.append(first[b] + dot(out, c_out_all, 0, 0))
        threes.append(norm_forward(second[b], gain_three, shift_three))
        whole_three.append(jnp.concatenate(spread(threes[b][0].astype(bf16)), axis=0))

    down_in = [jnp.concatenate(spread(cotangent[b]), axis=0) for b in clips]
    hidden, grad_gate, grad_upper, back_three, output = [], [], [], [], []
    for b in clips:
        grad_hidden = dot(down_in[b], w_down, 1, 1)
        gate = dot(whole_three[b], w_gate, 1, 0)
        upper = dot(whole_three[b], w_up, 1, 0)
        sigma = jax.nn.sigmoid(gate)
        hidden.append((gate * sigma * upper).astype(bf16))
        grad_gate.append(
            (grad_hidden * upper * sigma * (1.0 + gate * (1.0 - sigma))).astype(bf16)
        )
        grad_upper.append((grad_hidden * gate * sigma).astype(bf16))
        back = dot(grad_gate[b], w_gate, 1, 1) + dot(grad_upper[b], w_up, 1, 1)
        back_three.append(settle(row_blocks(back.astype(bf16), size)))
        branch = dot(hidden[b], w_down, 1, 0)
        output.append(second[b] + settle(row_blocks(branch.astype(bf16), size)))

    grad_two, grad_one, cross_in, self_in = [], [], [], []
    grad_cross_query, grad_memory, grad_mixed, back_two = [], [], [], []
    for b in clips:
        cot = cotangent[b].astype(f32)
        grad_two.append(cot + norm_backward(back_three[b], threes[b][1], threes[b][2], gain_three))
        cross_in.append(grad_two[b].astype(bf16))
        grads = dot(c_out_all, cross_in[b], 1, 1).astype(bf16)
        grad_queries, grad_keys, grad_values = cross_backward(
            b,
            size,
            lengths,
            cross_query[b],
            cross_keys[b],
            cross_values[b],
            grads,
            cross_mixed[b],
            cross_sums[b],
        )
        grad_cross_query.append(grad_queries)
        grad_memory.append(
            jnp.concatenate(
                [grad_keys.reshape(size, local, -1), grad_values.reshape(size, local, -1)], axis=1
            )
        )
        back_two.append(dot(grad_queries, c_query_all, 0, 1))
        grad_one.append(
            grad_two[b] + norm_backward(back_two[b], twos[b][1], twos[b][2], gain_two)
        )
        self_in.append(grad_one[b].astype(bf16))
        grads = dot(out_all, self_in[b], 1, 1).astype(bf16)
        grad_mixed.append(jnp.concatenate(trade(row_blocks(grads, size)), axis=1))

    grad_self, grad_front, back_one = [], [], []
    for b in clips:
        grads, grad_front_key, grad_front_value = self_backward(
            turned[b],
            grad_mixed[b],
            mixed_part[b],
            logsum[b],
            front_keys[b],
            front_values[b],
            cosine,
            sine,
        )
        grad_self.append(grads.reshape(3 * local, -1))
        grad_front.append(jnp.concatenate([grad_front_key, grad_front_value], axis=0))
        back = dot(grad_self[b], w_self, 0, 1).astype(bf16)
        back_one.append(settle(row_blocks(back, size)))
    grad_frames = [
        grad_one[b] + norm_backward(back_one[b], ones[b][1], ones[b][2], gain_one) for b in clips
    ]

    def joined(parts, axis):
        return jnp.concatenate(parts, axis=axis)

    hidden_all = joined(hidden, 0)
    three_all = joined(whole_three, 0)
    grad_w_down = sum_over_clips(dot(hidden_all, joined(down_in, 0), 0, 0), 1)
    grad_w_gate = sum_over_clips(dot(three_all, joined(grad_gate, 0), 0, 0), 0)
    grad_w_up = sum_over_clips(dot(three_all, joined(grad_upper, 0), 0, 0), 0)

    def from_rows(grad):
        return settle(row_blocks(sum_over_clips(grad, 1), size))

    grad_c_out = from_rows(dot(joined(cross_mixed, 1), joined(cross_in, 0), 1, 0))
    grad_w_out = from_rows(dot(joined(mixed, 1), joined(self_in, 0), 1, 0))
    grad_c_query = dot(joined(normed_two, 0), joined(grad_cross_query, 1), 0, 1)
    grad_c_query = settle(jnp.split(sum_over_clips(grad_c_query, 0), size, axis=1))

    grad_memory = jnp.stack(grad_memory)
    grad_memory = settle([grad_memory[:, k] for k in range(size)]).astype(bf16)
    grad_memory = joined([grad_memory[b] for b in clips], 1)
    grad_c_memory = dot(prompt.reshape(-1, prompt.shape[-1]), grad_memory, 0, 1)
    grad_c_memory = sum_over_clips(grad_c_memory, 0)

    grad_front = joined(grad_front, 1)
    grad_w_self = dot(joined(whole_one, 0), joined(grad_self, 1), 0, 1)
    grad_w_front = dot(prefix_low, grad_front, 0, 1)
    grad_w_self = joined(
        [grad_w_self[:, :local], grad_w_self[:, local:] + grad_w_front], 1
    )
    grad_w_self = sum_over_clips(grad_w_self, 0)

    early = []
    for back, kept in ((back_two, twos), (back_three, threes)):
        early.append(sum(jnp.sum(back[b] * kept[b][1], axis=0) for b in clips))
        early.append(sum(jnp.sum(back[b], axis=0) for b in clips))
    early = all_sum(jnp.stack(early))

    back_prefix = dot(grad_front, w_self[:, local:], 0, 1)
    grad_picked = norm_backward(back_prefix, prefix_normal, prefix_scale, gain_one)
    groups = lax.axis_size("dp")
    spots = jnp.arange(groups)[:, None, None] == lax.axis_index("dp")
    spots = jnp.where(spots, grad_picked[None], 0.0).reshape(groups * count, width)
    gain_term = jnp.sum(back_prefix * prefix_normal, axis=0)
    shift_term = jnp.sum(back_prefix, axis=0)
    for b in clips:
        gain_term = gain_term + jnp.sum(back_one[b] * ones[b][1], axis=0)
        shift_term = shift_term + jnp.sum(back_one[b], axis=0)
    late = all_sum(jnp.concatenate([gain_term[None], shift_term[None], spots], axis=0))
    all_steps = lax.all_gather(tsteps, "dp", axis=0, tiled=True)
    matches = (jnp.arange(table.shape[0])[:, None] == all_steps[None, :]).astype(f32)
    grad_table = jnp.dot(matches, late[2:], precision=lax.Precision.HIGHEST)

    wide = lambda value: value.astype(f32)
    return (
        jnp.stack(output),
        jnp.stack(grad_frames),
        grad_table,
        late[0],
        late[1],
        early[0],
        early[1],
        early[2],
        early[3],
        wide(grad_w_self[:, :local]),
        wide(grad_w_self[:, local : 2 * local]),
        wide(grad_w_self[:, 2 * local :]),
        grad_w_out,
        grad_c_query,
        wide(grad_c_memory[:, :local]),
        wide(grad_c_memory[:, local:]),
        grad_c_out,
        wide(grad_w_gate),
        wide(grad_w_up),
        wide(grad_w_down),
    )


def solution(mesh):
    placed = (
        P("dp", "mp", None),
        P("dp", None, None),
        P("dp"),
        P("dp"),
        P(),
        P(),
        P(),
        P(),
        P(),
        P(),
        P(),
        P(None, "mp"),
        P(None, "mp"),
        P(None, "mp"),
        P("mp", None),
        P(None, "mp"),
        P(None, "mp"),
        P(None, "mp"),
        P("mp", None),
        P(None, "mp"),
        P(None, "mp"),
        P("mp", None),
        P("dp", "mp", None),
    )
    return jax.shard_map(
        shards,
        mesh=mesh,
        in_specs=placed,
        out_specs=(
            P("dp", "mp", None),
            P("dp", "mp", None),
            P(),
            P(),
            P(),
            P(),
            P(),
            P(),
            P(),
            P("dp", "mp"),
            P("dp", "mp"),
            P("dp", "mp"),
            P("mp", "dp"),
            P("dp", "mp"),
            P("dp", "mp"),
            P("dp", "mp"),
            P("mp", "dp"),
            P("dp", "mp"),
            P("dp", "mp"),
            P("mp", "dp"),
        ),
        check_vma=False,
    )
```

```python
import functools
import math

import jax
import jax.numpy as jnp
from jax import lax
from jax.experimental import pallas as pl
from jax.experimental.pallas import tpu as pltpu
from jax.sharding import PartitionSpec as P

HEAD_DIM = 64
HALF = HEAD_DIM // 2
FACTOR = 1.0 / math.sqrt(HEAD_DIM)

norm_eps = 1e-05

f32 = jnp.float32
bf16 = jnp.bfloat16


def dot(left, right, left_axis, right_axis):
    return lax.dot_general(
        left, right, (((left_axis,), (right_axis,)), ((), ())), preferred_element_type=f32
    )


def norm_forward(values, gain, shift):
    center = values - jnp.mean(values, axis=-1, keepdims=True)
    scale = lax.rsqrt(jnp.mean(center * center, axis=-1, keepdims=True) + norm_eps)
    normal = center * scale
    return (normal * gain + shift, normal, scale)


def norm_backward(grad, normal, scale, gain):
    inner = grad * gain
    return scale * (
        inner
        - jnp.mean(inner, axis=-1, keepdims=True)
        - normal * jnp.mean(inner * normal, axis=-1, keepdims=True)
    )


def bits_of(size):
    return [1 << place for place in range(size.bit_length() - 1)]


def swap(values, axis, k):
    return lax.ppermute(values, axis, [(i, i ^ k) for i in range(lax.axis_size(axis))])


def after(values, *others):
    return lax.optimization_barrier((values,) + others)[0]


def spread(values):
    size = lax.axis_size("mp")
    if size != 4:
        pieces = [values] + [swap(values, "mp", k) for k in range(1, size)]
        return (pieces, tuple(pieces[1:2]))
    half = values.shape[0] // 2
    one = swap(values, "mp", 1)
    two = swap(values, "mp", 2)
    pieces = [values, one, two, swap(one[:half], "mp", 2), swap(two[half:], "mp", 1)]
    return (pieces, (one, two))


def trade(blocks):
    return [blocks[0]] + [swap(blocks[k], "mp", k) for k in range(1, len(blocks))]


def settle(blocks):
    if len(blocks) != 4:
        return trade(blocks)
    half = blocks[0].shape[0] // 2
    high = swap(blocks[3][:half], "mp", 2)
    low = swap(blocks[3][half:], "mp", 1)
    one = jnp.concatenate([plus(blocks[1][:half], high), blocks[1][half:]], axis=0)
    two = jnp.concatenate([blocks[2][:half], plus(blocks[2][half:], low)], axis=0)
    return [blocks[0], swap(one, "mp", 1), swap(two, "mp", 2)]


def plus(left, right):
    return (left.astype(f32) + right.astype(f32)).astype(bf16)


def total(terms):
    result = terms[0].astype(f32)
    for term in terms[1:]:
        result = result + term.astype(f32)
    return result


def all_sum(values):
    for axis in ("mp", "dp"):
        for bit in bits_of(lax.axis_size(axis)):
            values = values + swap(values, axis, bit)
    return values


def core_half(blocks):
    core = lax.axis_index("dp") & 1
    pairs = blocks.reshape((blocks.shape[0] // 2, 2) + blocks.shape[1:])
    mine = lax.dynamic_index_in_dim(pairs, core, 1, False)
    other = lax.dynamic_index_in_dim(pairs, 1 - core, 1, False)
    return (mine, swap(other, "dp", 1))


def chips_sum(blocks):
    here = lax.axis_index("dp") >> 1
    mine = [
        lax.dynamic_index_in_dim(blocks, here ^ k, 0, False) for k in range(blocks.shape[0])
    ]
    return total([mine[0]] + [swap(mine[k], "dp", 2 * k) for k in range(1, len(mine))])


def whole_rows(shard):
    size = lax.axis_size("mp")
    rows, width = shard.shape
    core = lax.axis_index("dp") & 1
    mine = lax.dynamic_slice_in_dim(shard, core * (rows // 2), rows // 2, 0)
    got = jnp.concatenate(spread(mine)[0][1:], axis=0).reshape(size - 1, rows // 2, width)
    other = swap(got, "dp", 1)
    low = jnp.where(core == 0, got, other)
    high = jnp.where(core == 0, other, got)
    rest = jnp.concatenate([low, high], axis=1).reshape((size - 1) * rows, width)
    return jnp.concatenate([shard, rest], axis=0)


def whole_columns(shard):
    size = lax.axis_size("mp")
    depth = shard.shape[0] // lax.axis_size("dp")
    mine = lax.dynamic_slice_in_dim(shard, lax.axis_index("dp") * depth, depth, 0)
    wide = jnp.concatenate([mine] + [swap(mine, "mp", k) for k in range(1, size)], axis=1)
    return (wide, lax.all_gather(wide, "dp", axis=0, tiled=True))


def self_forward_kernel(block, q_ref, k_ref, v_ref, pk_ref, pv_ref, o_ref, l_ref):
    keys = k_ref[...]
    values = v_ref[...]
    front_key = pk_ref[...].astype(f32)
    front_value = pv_ref[...].astype(f32)
    for start in range(0, q_ref.shape[1], block):
        part = slice(start, start + block)
        queries = q_ref[:, part]
        scores = dot(keys, queries, 0, 0)
        front = jnp.sum(queries.astype(f32) * front_key, axis=0, keepdims=True)
        top = jnp.maximum(jnp.max(scores, axis=0, keepdims=True), front)
        weights = jnp.exp(scores - top)
        front_weight = jnp.exp(front - top)
        total = jnp.sum(weights, axis=0, keepdims=True) + front_weight
        mixed = dot(values, weights.astype(bf16), 1, 0)
        mixed = mixed + front_value * front_weight.astype(bf16).astype(f32)
        o_ref[:, part] = (mixed * (1.0 / total)).astype(bf16)
        l_ref[0, :, part] = top + jnp.log(total)


def self_backward_kernel(
    block,
    q_ref,
    k_ref,
    v_ref,
    g_ref,
    o_ref,
    l_ref,
    pk_ref,
    pv_ref,
    cos_ref,
    sin_ref,
    d_ref,
    dpk_ref,
    dpv_ref,
):
    frames = q_ref.shape[1]
    keys = k_ref[...]
    values = v_ref[...]
    front_key = pk_ref[...].astype(f32)
    front_value = pv_ref[...].astype(f32)
    grad_keys = jnp.zeros((HEAD_DIM, frames), f32)
    grad_values = jnp.zeros((HEAD_DIM, frames), f32)
    grad_front_key = jnp.zeros((HEAD_DIM, 1), f32)
    grad_front_value = jnp.zeros((HEAD_DIM, 1), f32)
    for start in range(0, frames, block):
        part = slice(start, start + block)
        queries = q_ref[:, part]
        grads = g_ref[:, part]
        wide_queries = queries.astype(f32)
        wide_grads = grads.astype(f32)
        logsum = l_ref[0, :, part]
        mixsum = jnp.sum(o_ref[:, part].astype(f32) * wide_grads, axis=0, keepdims=True)
        probs = jnp.exp(dot(keys, queries, 0, 0) - logsum)
        grad_probs = dot(values, grads, 0, 0)
        grad_scores = (probs * (grad_probs - mixsum)).astype(bf16)
        grad_values = grad_values + dot(grads, probs.astype(bf16), 1, 1)
        grad_keys = grad_keys + dot(queries, grad_scores, 1, 1)
        grad_queries = dot(keys, grad_scores, 1, 0)
        front = jnp.exp(jnp.sum(wide_queries * front_key, axis=0, keepdims=True) - logsum)
        grad_front = jnp.sum(wide_grads * front_value, axis=0, keepdims=True)
        grad_front = (front * (grad_front - mixsum)).astype(bf16).astype(f32)
        front = front.astype(bf16).astype(f32)
        grad_front_key += jnp.sum(wide_queries * grad_front, axis=1, keepdims=True)
        grad_front_value += jnp.sum(wide_grads * front, axis=1, keepdims=True)
        grad_queries = (grad_queries + front_key * grad_front) * FACTOR
        cosine = cos_ref[:, part]
        sine = sin_ref[:, part]
        upper, lower = grad_queries[:HALF], grad_queries[HALF:]
        d_ref[0, :HALF, part] = (upper * cosine + lower * sine).astype(bf16)
        d_ref[0, HALF:, part] = (lower * cosine - upper * sine).astype(bf16)
    cosine = cos_ref[...]
    sine = sin_ref[...]
    upper, lower = grad_keys[:HALF], grad_keys[HALF:]
    d_ref[1, :HALF, :] = (upper * cosine + lower * sine).astype(bf16)
    d_ref[1, HALF:, :] = (lower * cosine - upper * sine).astype(bf16)
    d_ref[2] = grad_values.astype(bf16)
    dpk_ref[...] = grad_front_key.astype(bf16)
    dpv_ref[...] = grad_front_value.astype(bf16)


def cross_forward_kernel(clip, heads, n_ref, q_ref, k_ref, v_ref, o_ref, l_ref):
    live = lax.broadcasted_iota(jnp.int32, (k_ref.shape[1], 1), 0) < n_ref[clip]
    for head in range(heads):
        part = slice(head * HEAD_DIM, (head + 1) * HEAD_DIM)
        scores = jnp.where(live, dot(k_ref[part], q_ref[part], 0, 0), -1e30)
        top = jnp.max(scores, axis=0, keepdims=True)
        weights = jnp.exp(scores - top)
        total = jnp.sum(weights, axis=0, keepdims=True)
        mixed = dot(v_ref[part], weights.astype(bf16), 1, 0)
        o_ref[part] = (mixed * (1.0 / total)).astype(bf16)
        l_ref[head] = top + jnp.log(total)


def cross_backward_kernel(
    clip, heads, n_ref, q_ref, k_ref, v_ref, g_ref, o_ref, l_ref, dq_ref, dk_ref, dv_ref
):
    live = lax.broadcasted_iota(jnp.int32, (k_ref.shape[1], 1), 0) < n_ref[clip]
    for head in range(heads):
        part = slice(head * HEAD_DIM, (head + 1) * HEAD_DIM)
        queries = q_ref[part]
        keys = k_ref[part]
        grads = g_ref[part]
        mixsum = jnp.sum(o_ref[part].astype(f32) * grads.astype(f32), axis=0, keepdims=True)
        scores = jnp.where(live, dot(keys, queries, 0, 0), -1e30)
        probs = jnp.exp(scores - l_ref[head])
        grad_scores = (probs * (dot(v_ref[part], grads, 0, 0) - mixsum)).astype(bf16)
        dq_ref[part] = (dot(keys, grad_scores, 1, 0) * FACTOR).astype(bf16)
        dk_ref[part] = dot(queries, grad_scores, 1, 1).astype(bf16)
        dv_ref[part] = dot(grads, probs.astype(bf16), 1, 1).astype(bf16)


def shape_of(shape, kind):
    return jax.ShapeDtypeStruct(shape, kind)


def params():
    return pltpu.CompilerParams(vmem_limit_bytes=40 * 2**20)


def self_cost(heads, frames, products):
    return pl.CostEstimate(
        flops=products * 2 * heads * frames * frames * HEAD_DIM * 4,
        bytes_accessed=products * 2 * heads * frames * HEAD_DIM * 2,
        transcendentals=heads * frames * frames,
    )


def self_forward(turned, front_keys, front_values):
    heads = front_keys.shape[0] // HEAD_DIM
    frames = turned.shape[1]

    def at(third):
        return pl.BlockSpec((HEAD_DIM, frames), lambda h: (third * heads + h, 0))

    column = pl.BlockSpec((HEAD_DIM, 1), lambda h: (h, 0))
    return pl.pallas_call(
        functools.partial(self_forward_kernel, frames),
        grid=(heads,),
        in_specs=[at(0), at(1), at(2), column, column],
        out_specs=[at(0), pl.BlockSpec((1, 1, frames), lambda h: (h, 0, 0))],
        out_shape=[
            shape_of((heads * HEAD_DIM, frames), bf16),
            shape_of((heads, 1, frames), f32),
        ],
        compiler_params=params(),
        cost_estimate=self_cost(heads, frames, 2),
        name="self_forward",
    )(turned, turned, turned, front_keys, front_values)


def self_backward(turned, grads, mixed, logsum, front_keys, front_values, cosine, sine):
    heads = front_keys.shape[0] // HEAD_DIM
    frames = turned.shape[1]

    def at(third):
        return pl.BlockSpec((HEAD_DIM, frames), lambda h: (third * heads + h, 0))

    column = pl.BlockSpec((HEAD_DIM, 1), lambda h: (h, 0))
    angles = pl.BlockSpec((HALF, frames), lambda h: (0, 0))
    return pl.pallas_call(
        functools.partial(self_backward_kernel, min(256, frames)),
        grid=(heads,),
        in_specs=[
            at(0),
            at(1),
            at(2),
            at(0),
            at(0),
            pl.BlockSpec((1, 1, frames), lambda h: (h, 0, 0)),
            column,
            column,
            angles,
            angles,
        ],
        out_specs=[
            pl.BlockSpec((3, HEAD_DIM, frames), lambda h: (0, h, 0)),
            column,
            column,
        ],
        out_shape=[
            shape_of((3, heads * HEAD_DIM, frames), bf16),
            shape_of((heads * HEAD_DIM, 1), bf16),
            shape_of((heads * HEAD_DIM, 1), bf16),
        ],
        compiler_params=params(),
        cost_estimate=self_cost(heads, frames, 5),
        name="self_backward",
    )(turned, turned, turned, grads, mixed, logsum, front_keys, front_values, cosine, sine)


def cross_specs(groups, heads, frames, slots):
    at_frames = pl.BlockSpec((heads * HEAD_DIM, frames), lambda h: (h, 0))
    at_slots = pl.BlockSpec((heads * HEAD_DIM, slots), lambda h: (h, 0))
    at_sums = pl.BlockSpec((heads, 1, frames), lambda h: (h, 0, 0))
    return (at_frames, at_slots, at_sums)


def cross_cost(rows, frames, slots, products):
    return pl.CostEstimate(
        flops=products * 2 * rows * frames * slots * 4,
        bytes_accessed=products * 2 * rows * frames,
        transcendentals=rows // HEAD_DIM * frames * slots,
    )


def cross_forward(clip, groups, lengths, queries, keys, values):
    rows, frames = queries.shape
    heads = rows // HEAD_DIM // groups
    slots = keys.shape[1]
    at_frames, at_slots, at_sums = cross_specs(groups, heads, frames, slots)
    return pl.pallas_call(
        functools.partial(cross_forward_kernel, clip, heads),
        grid=(groups,),
        in_specs=[pl.BlockSpec(memory_space=pltpu.SMEM), at_frames, at_slots, at_slots],
        out_specs=[at_frames, at_sums],
        out_shape=[
            shape_of((rows, frames), bf16),
            shape_of((rows // HEAD_DIM, 1, frames), f32),
        ],
        compiler_params=params(),
        cost_estimate=cross_cost(rows, frames, slots, 2),
        name="cross_forward",
    )(lengths, queries, keys, values)


def cross_backward(clip, groups, lengths, queries, keys, values, grads, mixed, logsum):
    rows, frames = queries.shape
    heads = rows // HEAD_DIM // groups
    slots = keys.shape[1]
    at_frames, at_slots, at_sums = cross_specs(groups, heads, frames, slots)
    return pl.pallas_call(
        functools.partial(cross_backward_kernel, clip, heads),
        grid=(groups,),
        in_specs=[
            pl.BlockSpec(memory_space=pltpu.SMEM),
            at_frames,
            at_slots,
            at_slots,
            at_frames,
            at_frames,
            at_sums,
        ],
        out_specs=[at_frames, at_slots, at_slots],
        out_shape=[
            shape_of((rows, frames), bf16),
            shape_of((rows, slots), bf16),
            shape_of((rows, slots), bf16),
        ],
        compiler_params=params(),
        cost_estimate=cross_cost(rows, frames, slots, 5),
        name="cross_backward",
    )(lengths, queries, keys, values, grads, mixed, logsum)


def glu_kernel(block, x_ref, c_ref, gate_ref, up_ref, down_ref, h_ref, dg_ref, du_ref):
    for start in range(0, x_ref.shape[0], block):
        part = slice(start, start + block)
        gate = dot(x_ref[part], gate_ref[...], 1, 0)
        upper = dot(x_ref[part], up_ref[...], 1, 0)
        grad_hidden = dot(c_ref[part], down_ref[...], 1, 1)
        sigma = 1.0 / (1.0 + jnp.exp(-gate))
        silu = gate * sigma
        h_ref[part] = (silu * upper).astype(bf16)
        dg_ref[part] = (grad_hidden * upper * (sigma + silu * (1.0 - sigma))).astype(bf16)
        du_ref[part] = (grad_hidden * silu).astype(bf16)


def glu(frames, grads, w_gate, w_up, w_down):
    rows, width = frames.shape
    hidden = w_gate.shape[1]
    block = 256
    whole = pl.BlockSpec((rows, width), lambda j: (0, 0))
    columns = pl.BlockSpec((width, block), lambda j: (0, j))
    out = pl.BlockSpec((rows, block), lambda j: (0, j))
    return pl.pallas_call(
        functools.partial(glu_kernel, 256),
        grid=(hidden // block,),
        in_specs=[whole, whole, columns, columns, pl.BlockSpec((block, width), lambda j: (j, 0))],
        out_specs=[out, out, out],
        out_shape=[shape_of((rows, hidden), bf16)] * 3,
        compiler_params=params(),
        cost_estimate=pl.CostEstimate(
            flops=6 * rows * width * hidden,
            bytes_accessed=4 * rows * width + 6 * width * hidden + 6 * rows * hidden,
            transcendentals=rows * hidden,
        ),
        name="glu",
    )(frames, grads, w_gate, w_up, w_down)


def glu_back_kernel(block, dg_ref, du_ref, gate_ref, up_ref, o_ref):
    for start in range(0, dg_ref.shape[0], block):
        part = slice(start, start + block)
        back = dot(dg_ref[part], gate_ref[...], 1, 1) + dot(du_ref[part], up_ref[...], 1, 1)
        o_ref[part] = back.astype(bf16)


def glu_back(grad_gate, grad_upper, w_gate, w_up):
    rows, hidden = grad_gate.shape
    width = w_gate.shape[0]
    block = 256
    whole = pl.BlockSpec((rows, hidden), lambda j: (0, 0))
    part = pl.BlockSpec((block, hidden), lambda j: (j, 0))
    return pl.pallas_call(
        functools.partial(glu_back_kernel, 256),
        grid=(width // block,),
        in_specs=[whole, whole, part, part],
        out_specs=pl.BlockSpec((rows, block), lambda j: (0, j)),
        out_shape=shape_of((rows, width), bf16),
        compiler_params=params(),
        cost_estimate=pl.CostEstimate(
            flops=4 * rows * width * hidden,
            bytes_accessed=4 * rows * hidden + 4 * width * hidden + 2 * rows * width,
            transcendentals=0,
        ),
        name="glu_back",
    )(grad_gate, grad_upper, w_gate, w_up)


def turning(rows):
    size = lax.axis_size("mp")
    me = lax.axis_index("mp")
    starts = jnp.stack([(me ^ k) * rows for k in range(size)])
    places = (starts[:, None] + jnp.arange(rows)[None, :] + 1).reshape(-1).astype(f32)
    rates = jnp.exp(jnp.arange(HALF).astype(f32) * (-2.0 * math.log(10000.0) / HEAD_DIM))
    angles = rates[:, None] * places[None, :]
    return (jnp.cos(angles), jnp.sin(angles))


def turn(values, cosine, sine):
    pairs = values.reshape(-1, 2, HALF, values.shape[-1])
    upper, lower = pairs[:, 0], pairs[:, 1]
    return jnp.stack([upper * cosine - lower * sine, lower * cosine + upper * sine], axis=1).reshape(
        values.shape
    )


def row_blocks(values, count):
    return jnp.split(values, count, axis=0)


def sum_over_clips(values, axis):
    return lax.psum_scatter(values.astype(bf16), "dp", scatter_dimension=axis, tiled=True)


def shards(
    frames_in,
    prompt,
    lengths,
    tsteps,
    table,
    gain_one,
    shift_one,
    gain_two,
    shift_two,
    gain_three,
    shift_three,
    w_query,
    w_key,
    w_value,
    w_out,
    c_query,
    c_key,
    c_value,
    c_out,
    w_gate,
    w_up,
    w_down,
    cotangent,
):
    size = lax.axis_size("mp")
    groups = lax.axis_size("dp")
    count, rows, width = frames_in.shape
    clips = range(count)
    last = count - 1
    local = w_query.shape[1]

    def joined(parts, axis):
        return jnp.concatenate(parts, axis=axis)

    resid = [frames_in[b].astype(f32) for b in clips]
    ones = [norm_forward(resid[b], gain_one, shift_one) for b in clips]
    whole_one = []
    held = ()
    for b in clips:
        pieces, held = spread(after(ones[b][0].astype(bf16), *held))
        whole_one.append(joined(pieces, 0))
        if b == 0:
            seen = held
    c_query_wide, c_query_all = whole_columns(c_query)
    c_out_side, c_query_side = after((c_out.T, c_query_all), *seen)
    c_out_wide, c_out_all = whole_columns(c_out_side)
    out_all = whole_rows(after(w_out, whole_one[0]))

    memory = joined([c_key, c_value], 1)
    memory = jnp.stack([dot(memory, prompt[b], 0, 1).astype(bf16) for b in clips])
    memory = after(memory, *held)
    memory = jnp.stack([memory] + [swap(memory, "mp", k) for k in range(1, size)], axis=1)
    cross_keys = [memory[b, :, :local].reshape(size * local, -1) for b in clips]
    cross_values = [memory[b, :, local:].reshape(size * local, -1) for b in clips]

    picked = jnp.take(table, tsteps, axis=0)
    prefix_normed, prefix_normal, prefix_scale = norm_forward(picked, gain_one, shift_one)
    prefix_low = prefix_normed.astype(bf16)
    cosine, sine = turning(rows)
    w_self = joined([w_query, w_key, w_value], 1)
    front = dot(w_self[:, local:], prefix_low, 0, 1).astype(bf16)
    front_keys = [front[:local, b : b + 1] for b in clips]
    front_values = [front[local:, b : b + 1] for b in clips]

    turned, mixed_part, logsum, mixed = [], [], [], []
    for b in clips:
        raw = dot(w_self, whole_one[b], 0, 1)
        queries = (turn(raw[:local], cosine, sine) * FACTOR).astype(bf16)
        keys = turn(raw[local : 2 * local], cosine, sine).astype(bf16)
        turned.append(joined([queries, keys, raw[2 * local :].astype(bf16)], 0))
        out, sums = self_forward(turned[b], front_keys[b], front_values[b])
        mixed_part.append(out)
        logsum.append(sums)
        mixed.append(joined(trade(jnp.split(out, size, axis=1)), 0))

    first, twos, normed_two, cross_query, cross_sums, cross_mixed = [], [], [], [], [], []
    second, threes, whole_three, down_in = [], [], [], []
    held = (whole_one[last],)
    for b in clips:
        pieces, held = spread(after(cotangent[b], *held))
        down_in.append(joined(pieces, 0))
        first.append(resid[b] + dot(mixed[b], out_all, 0, 0))
        twos.append(norm_forward(first[b], gain_two, shift_two))
        normed_two.append(twos[b][0].astype(bf16))
        cross_query.append((dot(c_query_all, normed_two[b], 0, 1) * FACTOR).astype(bf16))
        out, sums = cross_forward(
            b, size, lengths, cross_query[b], cross_keys[b], cross_values[b]
        )
        cross_mixed.append(out)
        cross_sums.append(sums)
        second.append(first[b] + dot(out, c_out_all, 0, 1))
        threes.append(norm_forward(second[b], gain_three, shift_three))
        pieces, held = spread(threes[b][0].astype(bf16))
        whole_three.append(joined(pieces, 0))

    hidden, grad_gate, grad_upper, back_three, branch = [], [], [], [], []
    done = ()
    for b in clips:
        parts = glu(after(whole_three[b], *done), down_in[b], w_gate, w_up, w_down)
        hidden.append(parts[0])
        grad_gate.append(parts[1])
        grad_upper.append(parts[2])
        back = glu_back(grad_gate[b], grad_upper[b], w_gate, w_up)
        back_three.append(settle(row_blocks(back, size)))
        if b < last:
            branch.append(dot(after(hidden[b], back), w_down, 1, 0).astype(bf16))
            done = (branch[b],)
        else:
            done = (back,)

    hidden_all = joined(hidden, 0)
    three_all = joined(whole_three, 0)
    raw_w_down = dot(after(hidden_all, *done), joined(down_in, 0), 0, 0).astype(bf16)
    grad_w_down = sum_over_clips(raw_w_down, 1)
    done = (raw_w_down,)

    grad_two, grad_one, cross_in, self_in = [], [], [], []
    grad_cross_query, grad_memory, grad_mixed, back_two = [], [], [], []
    for b in clips:
        back_three[b] = total(after(back_three[b], *done))
        cot = cotangent[b].astype(f32)
        grad_two.append(cot + norm_backward(back_three[b], threes[b][1], threes[b][2], gain_three))
        cross_in.append(grad_two[b].astype(bf16))
        grads = dot(c_out_all, cross_in[b], 0, 1).astype(bf16)
        grad_queries, grad_keys, grad_values = cross_backward(
            b,
            size,
            lengths,
            cross_query[b],
            cross_keys[b],
            cross_values[b],
            grads,
            cross_mixed[b],
            cross_sums[b],
        )
        grad_cross_query.append(grad_queries)
        grad_memory.append(
            joined([grad_keys.reshape(size, local, -1), grad_values.reshape(size, local, -1)], 1)
        )
        back_two.append(dot(grad_queries, c_query_all, 0, 1))
        grad_one.append(
            grad_two[b] + norm_backward(back_two[b], twos[b][1], twos[b][2], gain_two)
        )
        self_in.append(grad_one[b].astype(bf16))
        grads = dot(out_all, self_in[b], 1, 1).astype(bf16)
        grad_mixed.append(joined(trade(row_blocks(grads, size)), 1))
        done = (grads,)

    branch.append(dot(after(hidden[last], *done), w_down, 1, 0).astype(bf16))
    raw_w_gate = dot(after(three_all, branch[last]), joined(grad_gate, 0), 0, 0).astype(bf16)
    grad_w_gate = sum_over_clips(raw_w_gate, 0)
    done = (raw_w_gate,)
    output = [
        second[b] + total(settle(row_blocks(branch[b], size))) for b in clips
    ]

    grad_self, grad_front, back_one = [], [], []
    for b in clips:
        grads, grad_front_key, grad_front_value = self_backward(
            turned[b],
            after(grad_mixed[b], *done),
            mixed_part[b],
            logsum[b],
            front_keys[b],
            front_values[b],
            cosine,
            sine,
        )
        grad_self.append(grads.reshape(3 * local, -1))
        grad_front.append(joined([grad_front_key, grad_front_value], 0))
        back = dot(grad_self[b], w_self, 0, 1).astype(bf16)
        done = (back,)
        back_one.append(total(settle(row_blocks(back, size))))
    grad_frames = [
        grad_one[b] + norm_backward(back_one[b], ones[b][1], ones[b][2], gain_one) for b in clips
    ]

    grad_front = joined(grad_front, 1)
    turned_grads = after(joined(grad_self, 1), *done)
    raw_w_self = dot(joined(whole_one, 0), turned_grads, 0, 1)
    raw_w_front = dot(prefix_low, grad_front, 0, 1)
    raw_w_self = joined([raw_w_self[:, :local], raw_w_self[:, local:] + raw_w_front], 1)
    low_w_self = raw_w_self.astype(bf16).reshape(groups, -1, 3 * local)
    grad_w_self = chips_sum(plus(*core_half(low_w_self)))

    raw_w_up = dot(after(three_all, raw_w_self), joined(grad_upper, 0), 0, 0).astype(bf16)
    grad_w_up = sum_over_clips(raw_w_up, 0)

    cross_all = after(joined(cross_in, 0), raw_w_up)
    raws = [
        dot(joined(normed_two, 0), joined(grad_cross_query, 1), 0, 1),
        dot(cross_all, joined(cross_mixed, 1), 0, 1),
        dot(joined(self_in, 0), joined(mixed, 1), 0, 1),
    ]
    raws = joined([raw.astype(bf16).reshape(groups, -1, size, local) for raw in raws], 3)
    mine, other = core_half(raws)
    raws = [plus(mine[:, :, k], other[:, :, k]).reshape(-1, 3 * local) for k in range(size)]
    raws = total(settle(raws)).astype(bf16).reshape(groups // 2, -1, 3 * local)
    raws = chips_sum(raws)

    grad_memory = jnp.stack(grad_memory)
    grad_memory = total(trade([grad_memory[:, k] for k in range(size)])).astype(bf16)
    grad_memory = joined([grad_memory[b] for b in clips], 1)
    grad_c_memory = dot(prompt.reshape(-1, prompt.shape[-1]), grad_memory, 0, 1)
    grad_c_memory = sum_over_clips(grad_c_memory, 0)

    small = []
    wide_w_self = w_self.astype(f32)
    sums = jnp.sum(turned_grads.astype(f32), axis=1)
    front_sums = jnp.sum(grad_front.astype(f32), axis=1)
    sums = joined([sums[:local], sums[local:] + front_sums], 0)
    shift_term = jnp.sum(wide_w_self * sums[None, :], axis=1)
    gain_term = jnp.sum(wide_w_self * raw_w_self, axis=1)
    small.append((gain_term - shift_one * shift_term) / gain_one)
    small.append(shift_term)
    for back, kept in ((back_two, twos), (back_three, threes)):
        small.append(sum(jnp.sum(back[b] * kept[b][1], axis=0) for b in clips))
        small.append(sum(jnp.sum(back[b], axis=0) for b in clips))

    me = lax.axis_index("dp")
    steps = jnp.where(lax.axis_index("mp") == 0, tsteps, 0).astype(f32)
    steps = lax.dynamic_update_slice(jnp.zeros((width,), f32), steps, (me * count,))
    small.append(steps)

    back_prefix = dot(grad_front, w_self[:, local:], 0, 1)
    grad_picked = norm_backward(back_prefix, prefix_normal, prefix_scale, gain_one)
    spots = jnp.arange(groups)[:, None, None] == me
    spots = jnp.where(spots, grad_picked[None], 0.0).reshape(groups * count, width)
    small = all_sum(joined([jnp.stack(small), spots], 0))
    all_steps = small[6, : groups * count]
    matches = jnp.arange(table.shape[0])[:, None].astype(f32) == all_steps[None, :]
    grad_table = jnp.dot(matches.astype(f32), small[7:], precision=lax.Precision.HIGHEST)

    def wide(value):
        return value.astype(f32)

    return (
        jnp.stack(output),
        jnp.stack(grad_frames),
        grad_table,
        small[0],
        small[1],
        small[2],
        small[3],
        small[4],
        small[5],
        grad_w_self[:, :local],
        grad_w_self[:, local : 2 * local],
        grad_w_self[:, 2 * local :],
        raws[:, 2 * local :].T,
        raws[:, :local],
        wide(grad_c_memory[:, :local]),
        wide(grad_c_memory[:, local:]),
        raws[:, local : 2 * local].T,
        wide(grad_w_gate),
        wide(grad_w_up),
        wide(grad_w_down),
    )


def solution(mesh):
    placed = (
        P("dp", "mp", None),
        P("dp", None, None),
        P("dp"),
        P("dp"),
        P(),
        P(),
        P(),
        P(),
        P(),
        P(),
        P(),
        P(None, "mp"),
        P(None, "mp"),
        P(None, "mp"),
        P("mp", None),
        P(None, "mp"),
        P(None, "mp"),
        P(None, "mp"),
        P("mp", None),
        P(None, "mp"),
        P(None, "mp"),
        P("mp", None),
        P("dp", "mp", None),
    )
    return jax.shard_map(
        shards,
        mesh=mesh,
        in_specs=placed,
        out_specs=(
            P("dp", "mp", None),
            P("dp", "mp", None),
            P(),
            P(),
            P(),
            P(),
            P(),
            P(),
            P(),
            P("dp", "mp"),
            P("dp", "mp"),
            P("dp", "mp"),
            P("mp", "dp"),
            P("dp", "mp"),
            P("dp", "mp"),
            P("dp", "mp"),
            P("mp", "dp"),
            P("dp", "mp"),
            P("dp", "mp"),
            P("mp", "dp"),
        ),
        check_vma=False,
    )
```

```python
import functools
import math

import jax
import jax.numpy as jnp
from jax import lax
from jax.experimental import pallas as pl
from jax.experimental.pallas import tpu as pltpu
from jax.sharding import PartitionSpec as P

HEAD_DIM = 64
HALF = HEAD_DIM // 2
FACTOR = 1.0 / math.sqrt(HEAD_DIM)

norm_eps = 1e-05

f32 = jnp.float32
bf16 = jnp.bfloat16


def dot(left, right, left_axis, right_axis):
    return lax.dot_general(
        left, right, (((left_axis,), (right_axis,)), ((), ())), preferred_element_type=f32
    )


def norm_forward(values, gain, shift):
    center = values - jnp.mean(values, axis=-1, keepdims=True)
    scale = lax.rsqrt(jnp.mean(center * center, axis=-1, keepdims=True) + norm_eps)
    normal = center * scale
    return (normal * gain + shift, normal, scale)


def norm_backward(grad, normal, scale, gain):
    inner = grad * gain
    return scale * (
        inner
        - jnp.mean(inner, axis=-1, keepdims=True)
        - normal * jnp.mean(inner * normal, axis=-1, keepdims=True)
    )


def bits_of(size):
    return [1 << place for place in range(size.bit_length() - 1)]


def swap(values, axis, k):
    return lax.ppermute(values, axis, [(i, i ^ k) for i in range(lax.axis_size(axis))])


def after(values, *others):
    return lax.optimization_barrier((values,) + others)[0]


class Spread:
    def __init__(self, values):
        self.values = values
        if lax.axis_size("mp") == 4:
            self.first = (swap(values, "mp", 1), swap(values, "mp", 2))
        else:
            self.first = tuple(swap(values, "mp", k) for k in range(1, lax.axis_size("mp")))
        self.last = ()

    def second_step(self):
        if lax.axis_size("mp") == 4:
            half = self.values.shape[0] // 2
            one, two = self.first
            self.last = (swap(one[:half], "mp", 2), swap(two[half:], "mp", 1))

    def pieces(self):
        return [self.values, *self.first, *self.last]


def trade(blocks):
    return [blocks[0]] + [swap(blocks[k], "mp", k) for k in range(1, len(blocks))]


def cut(values):
    size = lax.axis_size("mp")
    blocks = jnp.split(values, size, axis=0)
    return blocks[:3] + jnp.split(blocks[3], 2, axis=0) if size == 4 else blocks


def settle_first(pieces):
    if lax.axis_size("mp") != 4:
        return ()
    return (swap(pieces[3], "mp", 2), swap(pieces[4], "mp", 1))


def settle_last(pieces, came):
    if lax.axis_size("mp") != 4:
        return trade(pieces)
    high, low = came
    half = high.shape[0]
    one = jnp.concatenate([plus(pieces[1][:half], high), pieces[1][half:]], axis=0)
    two = jnp.concatenate([pieces[2][:half], plus(pieces[2][half:], low)], axis=0)
    return [pieces[0], swap(one, "mp", 1), swap(two, "mp", 2)]


class Chain:
    def __init__(self):
        self.last = ()

    def hold(self, values):
        return after(values, *self.last) if self.last else values

    def mark(self, *values):
        self.last = values

    def arrive(self, values):
        values = self.hold(values)
        self.mark(values)
        return values


def plus(left, right):
    return (left.astype(f32) + right.astype(f32)).astype(bf16)


def total(terms):
    result = terms[0].astype(f32)
    for term in terms[1:]:
        result = result + term.astype(f32)
    return result


def all_sum(values):
    for axis in ("mp", "dp"):
        for bit in bits_of(lax.axis_size(axis)):
            values = values + swap(values, axis, bit)
    return values


def core_half(blocks):
    core = lax.axis_index("dp") & 1
    pairs = blocks.reshape((blocks.shape[0] // 2, 2) + blocks.shape[1:])
    mine = lax.dynamic_index_in_dim(pairs, core, 1, False)
    other = lax.dynamic_index_in_dim(pairs, 1 - core, 1, False)
    return (mine, swap(other, "dp", 1))


def chips_sum(blocks):
    here = lax.axis_index("dp") >> 1
    mine = [
        lax.dynamic_index_in_dim(blocks, here ^ k, 0, False) for k in range(blocks.shape[0])
    ]
    return total([mine[0]] + [swap(mine[k], "dp", 2 * k) for k in range(1, len(mine))])


def self_forward_kernel(block, q_ref, k_ref, v_ref, pk_ref, pv_ref, o_ref, l_ref):
    keys = k_ref[...]
    values = v_ref[...]
    front_key = pk_ref[...].astype(f32)
    front_value = pv_ref[...].astype(f32)
    for start in range(0, q_ref.shape[1], block):
        part = slice(start, start + block)
        queries = q_ref[:, part]
        scores = dot(keys, queries, 0, 0)
        front = jnp.sum(queries.astype(f32) * front_key, axis=0, keepdims=True)
        top = jnp.maximum(jnp.max(scores, axis=0, keepdims=True), front)
        weights = jnp.exp(scores - top)
        front_weight = jnp.exp(front - top)
        total = jnp.sum(weights, axis=0, keepdims=True) + front_weight
        mixed = dot(values, weights.astype(bf16), 1, 0)
        mixed = mixed + front_value * front_weight.astype(bf16).astype(f32)
        o_ref[:, part] = (mixed * (1.0 / total)).astype(bf16)
        l_ref[0, :, part] = top + jnp.log(total)


def self_backward_kernel(
    block,
    q_ref,
    k_ref,
    v_ref,
    g_ref,
    o_ref,
    l_ref,
    pk_ref,
    pv_ref,
    cos_ref,
    sin_ref,
    d_ref,
    dpk_ref,
    dpv_ref,
):
    frames = q_ref.shape[1]
    keys = k_ref[...]
    values = v_ref[...]
    front_key = pk_ref[...].astype(f32)
    front_value = pv_ref[...].astype(f32)
    grad_keys = jnp.zeros((HEAD_DIM, frames), f32)
    grad_values = jnp.zeros((HEAD_DIM, frames), f32)
    grad_front_key = jnp.zeros((HEAD_DIM, 1), f32)
    grad_front_value = jnp.zeros((HEAD_DIM, 1), f32)
    for start in range(0, frames, block):
        part = slice(start, start + block)
        queries = q_ref[:, part]
        grads = g_ref[:, part]
        wide_queries = queries.astype(f32)
        wide_grads = grads.astype(f32)
        logsum = l_ref[0, :, part]
        mixsum = jnp.sum(o_ref[:, part].astype(f32) * wide_grads, axis=0, keepdims=True)
        probs = jnp.exp(dot(keys, queries, 0, 0) - logsum)
        grad_probs = dot(values, grads, 0, 0)
        grad_scores = (probs * (grad_probs - mixsum)).astype(bf16)
        grad_values = grad_values + dot(grads, probs.astype(bf16), 1, 1)
        grad_keys = grad_keys + dot(queries, grad_scores, 1, 1)
        grad_queries = dot(keys, grad_scores, 1, 0)
        front = jnp.exp(jnp.sum(wide_queries * front_key, axis=0, keepdims=True) - logsum)
        grad_front = jnp.sum(wide_grads * front_value, axis=0, keepdims=True)
        grad_front = (front * (grad_front - mixsum)).astype(bf16).astype(f32)
        front = front.astype(bf16).astype(f32)
        grad_front_key += jnp.sum(wide_queries * grad_front, axis=1, keepdims=True)
        grad_front_value += jnp.sum(wide_grads * front, axis=1, keepdims=True)
        grad_queries = (grad_queries + front_key * grad_front) * FACTOR
        cosine = cos_ref[:, part]
        sine = sin_ref[:, part]
        upper, lower = grad_queries[:HALF], grad_queries[HALF:]
        d_ref[0, :HALF, part] = (upper * cosine + lower * sine).astype(bf16)
        d_ref[0, HALF:, part] = (lower * cosine - upper * sine).astype(bf16)
    cosine = cos_ref[...]
    sine = sin_ref[...]
    upper, lower = grad_keys[:HALF], grad_keys[HALF:]
    d_ref[1, :HALF, :] = (upper * cosine + lower * sine).astype(bf16)
    d_ref[1, HALF:, :] = (lower * cosine - upper * sine).astype(bf16)
    d_ref[2] = grad_values.astype(bf16)
    dpk_ref[...] = grad_front_key.astype(bf16)
    dpv_ref[...] = grad_front_value.astype(bf16)


def cross_forward_kernel(clip, heads, n_ref, q_ref, k_ref, v_ref, o_ref, l_ref):
    live = lax.broadcasted_iota(jnp.int32, (k_ref.shape[1], 1), 0) < n_ref[clip]
    for head in range(heads):
        part = slice(head * HEAD_DIM, (head + 1) * HEAD_DIM)
        scores = jnp.where(live, dot(k_ref[part], q_ref[part], 0, 0), -1e30)
        top = jnp.max(scores, axis=0, keepdims=True)
        weights = jnp.exp(scores - top)
        total = jnp.sum(weights, axis=0, keepdims=True)
        mixed = dot(v_ref[part], weights.astype(bf16), 1, 0)
        o_ref[part] = (mixed * (1.0 / total)).astype(bf16)
        l_ref[head] = top + jnp.log(total)


def cross_backward_kernel(
    clip, heads, n_ref, q_ref, k_ref, v_ref, g_ref, o_ref, l_ref, dq_ref, dk_ref, dv_ref
):
    live = lax.broadcasted_iota(jnp.int32, (k_ref.shape[1], 1), 0) < n_ref[clip]
    for head in range(heads):
        part = slice(head * HEAD_DIM, (head + 1) * HEAD_DIM)
        queries = q_ref[part]
        keys = k_ref[part]
        grads = g_ref[part]
        mixsum = jnp.sum(o_ref[part].astype(f32) * grads.astype(f32), axis=0, keepdims=True)
        scores = jnp.where(live, dot(keys, queries, 0, 0), -1e30)
        probs = jnp.exp(scores - l_ref[head])
        grad_scores = (probs * (dot(v_ref[part], grads, 0, 0) - mixsum)).astype(bf16)
        dq_ref[part] = (dot(keys, grad_scores, 1, 0) * FACTOR).astype(bf16)
        dk_ref[part] = dot(queries, grad_scores, 1, 1).astype(bf16)
        dv_ref[part] = dot(grads, probs.astype(bf16), 1, 1).astype(bf16)


def shape_of(shape, kind):
    return jax.ShapeDtypeStruct(shape, kind)


def params():
    return pltpu.CompilerParams(vmem_limit_bytes=40 * 2**20)


def self_cost(heads, frames, products):
    return pl.CostEstimate(
        flops=products * 2 * heads * frames * frames * HEAD_DIM * 4,
        bytes_accessed=products * 2 * heads * frames * HEAD_DIM * 2,
        transcendentals=heads * frames * frames,
    )


def self_forward(turned, front_keys, front_values):
    heads = front_keys.shape[0] // HEAD_DIM
    frames = turned.shape[1]

    def at(third):
        return pl.BlockSpec((HEAD_DIM, frames), lambda h: (third * heads + h, 0))

    column = pl.BlockSpec((HEAD_DIM, 1), lambda h: (h, 0))
    return pl.pallas_call(
        functools.partial(self_forward_kernel, frames),
        grid=(heads,),
        in_specs=[at(0), at(1), at(2), column, column],
        out_specs=[at(0), pl.BlockSpec((1, 1, frames), lambda h: (h, 0, 0))],
        out_shape=[
            shape_of((heads * HEAD_DIM, frames), bf16),
            shape_of((heads, 1, frames), f32),
        ],
        compiler_params=params(),
        cost_estimate=self_cost(heads, frames, 2),
        name="self_forward",
    )(turned, turned, turned, front_keys, front_values)


def self_backward(turned, grads, mixed, logsum, front_keys, front_values, cosine, sine):
    heads = front_keys.shape[0] // HEAD_DIM
    frames = turned.shape[1]

    def at(third):
        return pl.BlockSpec((HEAD_DIM, frames), lambda h: (third * heads + h, 0))

    column = pl.BlockSpec((HEAD_DIM, 1), lambda h: (h, 0))
    angles = pl.BlockSpec((HALF, frames), lambda h: (0, 0))
    return pl.pallas_call(
        functools.partial(self_backward_kernel, min(256, frames)),
        grid=(heads,),
        in_specs=[
            at(0),
            at(1),
            at(2),
            at(0),
            at(0),
            pl.BlockSpec((1, 1, frames), lambda h: (h, 0, 0)),
            column,
            column,
            angles,
            angles,
        ],
        out_specs=[
            pl.BlockSpec((3, HEAD_DIM, frames), lambda h: (0, h, 0)),
            column,
            column,
        ],
        out_shape=[
            shape_of((3, heads * HEAD_DIM, frames), bf16),
            shape_of((heads * HEAD_DIM, 1), bf16),
            shape_of((heads * HEAD_DIM, 1), bf16),
        ],
        compiler_params=params(),
        cost_estimate=self_cost(heads, frames, 5),
        name="self_backward",
    )(turned, turned, turned, grads, mixed, logsum, front_keys, front_values, cosine, sine)


def cross_specs(groups, heads, frames, slots):
    at_frames = pl.BlockSpec((heads * HEAD_DIM, frames), lambda h: (h, 0))
    at_slots = pl.BlockSpec((heads * HEAD_DIM, slots), lambda h: (h, 0))
    at_sums = pl.BlockSpec((heads, 1, frames), lambda h: (h, 0, 0))
    return (at_frames, at_slots, at_sums)


def cross_cost(rows, frames, slots, products):
    return pl.CostEstimate(
        flops=products * 2 * rows * frames * slots * 4,
        bytes_accessed=products * 2 * rows * frames,
        transcendentals=rows // HEAD_DIM * frames * slots,
    )


def cross_forward(clip, groups, lengths, queries, keys, values):
    rows, frames = queries.shape
    heads = rows // HEAD_DIM // groups
    slots = keys.shape[1]
    at_frames, at_slots, at_sums = cross_specs(groups, heads, frames, slots)
    return pl.pallas_call(
        functools.partial(cross_forward_kernel, clip, heads),
        grid=(groups,),
        in_specs=[pl.BlockSpec(memory_space=pltpu.SMEM), at_frames, at_slots, at_slots],
        out_specs=[at_frames, at_sums],
        out_shape=[
            shape_of((rows, frames), bf16),
            shape_of((rows // HEAD_DIM, 1, frames), f32),
        ],
        compiler_params=params(),
        cost_estimate=cross_cost(rows, frames, slots, 2),
        name="cross_forward",
    )(lengths, queries, keys, values)


def cross_backward(clip, groups, lengths, queries, keys, values, grads, mixed, logsum):
    rows, frames = queries.shape
    heads = rows // HEAD_DIM // groups
    slots = keys.shape[1]
    at_frames, at_slots, at_sums = cross_specs(groups, heads, frames, slots)
    return pl.pallas_call(
        functools.partial(cross_backward_kernel, clip, heads),
        grid=(groups,),
        in_specs=[
            pl.BlockSpec(memory_space=pltpu.SMEM),
            at_frames,
            at_slots,
            at_slots,
            at_frames,
            at_frames,
            at_sums,
        ],
        out_specs=[at_frames, at_slots, at_slots],
        out_shape=[
            shape_of((rows, frames), bf16),
            shape_of((rows, slots), bf16),
            shape_of((rows, slots), bf16),
        ],
        compiler_params=params(),
        cost_estimate=cross_cost(rows, frames, slots, 5),
        name="cross_backward",
    )(lengths, queries, keys, values, grads, mixed, logsum)


def block_refs(refs, size):
    return [refs[0:1], refs[1:2], refs[2:3], refs[3:5]] if size == 4 else [[r] for r in refs]


def block_value(refs):
    parts = [ref[...] for ref in refs]
    return parts[0] if len(parts) == 1 else jnp.concatenate(parts, axis=0)


def whole_specs(pieces):
    return [pl.BlockSpec(piece.shape, lambda j: (0, 0)) for piece in pieces]


def project_kernel(size, heads, w_ref, cos_ref, sin_ref, *refs):
    d_ref, x_ref = refs[-2:]
    blocks = block_refs(refs[: 5 if size == 4 else size], size)
    for k in range(size):

        @pl.when(pl.program_id(0) == k)
        def _(k=k):
            frames = block_value(blocks[k])
            x_ref[0] = frames
            raw = dot(w_ref[...], frames, 1, 1)
            cosine = cos_ref[...]
            sine = sin_ref[...]
            for head in range(2 * heads):
                at = head * HEAD_DIM
                upper = raw[at : at + HALF]
                lower = raw[at + HALF : at + HEAD_DIM]
                first = upper * cosine - lower * sine
                second = lower * cosine + upper * sine
                if head < heads:
                    first, second = first * FACTOR, second * FACTOR
                d_ref[at : at + HALF] = first.astype(bf16)
                d_ref[at + HALF : at + HEAD_DIM] = second.astype(bf16)
            at = 2 * heads * HEAD_DIM
            d_ref[at:] = raw[at:].astype(bf16)


def project(clip, count, pieces, w_turned, cosine, sine, earlier):
    size = lax.axis_size("mp")
    depth, width = w_turned.shape
    rows = pieces[0].shape[0]
    angles = pl.BlockSpec((HALF, rows), lambda k: (0, k))
    return pl.pallas_call(
        functools.partial(project_kernel, size, depth // 3 // HEAD_DIM),
        grid=(size,),
        in_specs=[pl.BlockSpec((depth, width), lambda k: (0, 0)), angles, angles]
        + whole_specs(pieces)
        + [pl.BlockSpec(memory_space=pl.ANY)] * len(earlier),
        out_specs=[
            pl.BlockSpec((depth, rows), lambda k: (0, k)),
            pl.BlockSpec((1, rows, width), lambda k: (clip, k, 0)),
        ],
        out_shape=[
            shape_of((depth, size * rows), bf16),
            shape_of((count, size * rows, width), bf16),
        ],
        input_output_aliases={3 + len(pieces): 1} if earlier else {},
        compiler_params=params(),
        cost_estimate=pl.CostEstimate(
            flops=2 * depth * width * size * rows,
            bytes_accessed=4 * size * rows * width + 2 * depth * (width + size * rows),
            transcendentals=0,
        ),
        name="project",
    )(w_turned, cosine, sine, *pieces, *earlier)


def glu_kernel(size, given, n_ref, gate_ref, up_ref, down_ref, c_ref, *refs):
    h_ref, dg_ref, du_ref, x_ref = refs[-4:]
    blocks = block_refs(refs[:given], size)
    rows = h_ref.shape[1] // size

    @pl.when(pl.program_id(0) == 0)
    def _():
        for k in range(size):
            x_ref[0, k * rows : (k + 1) * rows] = block_value(blocks[k])

    for k in range(size):
        frames = block_value(blocks[k])
        part = slice(k * rows, (k + 1) * rows)
        there = pl.ds(pl.multiple_of(n_ref[k] * rows, rows), rows)
        gate = dot(frames, gate_ref[...], 1, 0)
        upper = dot(frames, up_ref[...], 1, 0)
        grad_hidden = dot(c_ref[0, there], down_ref[...], 1, 1)
        sigma = 1.0 / (1.0 + jnp.exp(-gate))
        silu = gate * sigma
        h_ref[0, there] = (silu * upper).astype(bf16)
        dg_ref[0, part] = (grad_hidden * upper * (sigma + silu * (1.0 - sigma))).astype(bf16)
        du_ref[0, part] = (grad_hidden * silu).astype(bf16)


def glu(clip, order, pieces, grads, w_gate, w_up, w_down, earlier):
    size = lax.axis_size("mp")
    count, rows, width = grads.shape
    hidden = w_gate.shape[1]
    block = 256
    columns = pl.BlockSpec((width, block), lambda j: (0, j))
    out = pl.BlockSpec((1, rows, block), lambda j: (clip, 0, j))
    whole = pl.BlockSpec((1, rows, width), lambda j: (clip, 0, 0))
    return pl.pallas_call(
        functools.partial(glu_kernel, size, len(pieces)),
        grid=(hidden // block,),
        in_specs=[
            pl.BlockSpec(memory_space=pltpu.SMEM),
            columns,
            columns,
            pl.BlockSpec((block, width), lambda j: (j, 0)),
            whole,
        ]
        + whole_specs(pieces)
        + [pl.BlockSpec(memory_space=pl.ANY)] * len(earlier),
        out_specs=[out, out, out, whole],
        out_shape=[shape_of((count, rows, hidden), bf16)] * 3
        + [shape_of((count, rows, width), bf16)],
        input_output_aliases={5 + len(pieces) + i: i for i in range(len(earlier))},
        compiler_params=params(),
        cost_estimate=pl.CostEstimate(
            flops=6 * rows * width * hidden,
            bytes_accessed=6 * rows * width + 6 * width * hidden + 6 * rows * hidden,
            transcendentals=rows * hidden,
        ),
        name="glu",
    )(order, w_gate, w_up, w_down, grads, *pieces, *earlier)


def glu_back_kernel(size, dg_ref, du_ref, gate_ref, up_ref, *refs):
    blocks = block_refs(refs, size)
    rows = dg_ref.shape[1] // size
    for k in range(size):
        part = slice(k * rows, (k + 1) * rows)
        back = dot(dg_ref[0, part], gate_ref[...], 1, 1) + dot(du_ref[0, part], up_ref[...], 1, 1)
        at = 0
        for ref in blocks[k]:
            ref[...] = back[at : at + ref.shape[0]].astype(bf16)
            at += ref.shape[0]


def glu_back(clip, grad_gate, grad_upper, w_gate, w_up):
    size = lax.axis_size("mp")
    _, frames, hidden = grad_gate.shape
    rows = frames // size
    width = w_gate.shape[0]
    block = 256
    sizes = [rows] * 3 + [rows // 2] * 2 if size == 4 else [rows] * size
    whole = pl.BlockSpec((1, frames, hidden), lambda j: (clip, 0, 0))
    part = pl.BlockSpec((block, hidden), lambda j: (j, 0))
    return pl.pallas_call(
        functools.partial(glu_back_kernel, size),
        grid=(width // block,),
        in_specs=[whole, whole, part, part],
        out_specs=[pl.BlockSpec((n, block), lambda j: (0, j)) for n in sizes],
        out_shape=[shape_of((n, width), bf16) for n in sizes],
        compiler_params=params(),
        cost_estimate=pl.CostEstimate(
            flops=4 * frames * width * hidden,
            bytes_accessed=4 * frames * hidden + 4 * width * hidden + 2 * frames * width,
            transcendentals=0,
        ),
        name="glu_back",
    )(grad_gate, grad_upper, w_gate, w_up)


def whole_grad_kernel(chips, given, core_ref, x_ref, y_ref, *refs):
    o_ref, turned_ref = refs[-2:]
    depth = o_ref.shape[3]

    @pl.when(pl.program_id(1) == 0)
    def _():
        turned_ref[...] = x_ref[0].T

    for z in range(chips):
        at = pl.multiple_of((2 * z + core_ref[0]) * depth, depth)
        result = dot(turned_ref[pl.ds(at, depth)], y_ref[0], 1, 1)
        if given:
            result = result + refs[0][0, z, 0].astype(f32)
        o_ref[0, z, 0] = result.astype(bf16)


def whole_grad(core, groups, lefts, rights, earlier):
    size = lax.axis_size("mp")
    n, frames, width = lefts.shape
    local = rights.shape[1] // size
    chips = groups // 2
    depth = width // groups
    out = pl.BlockSpec((1, chips, 1, depth, local), lambda w, m: (m, 0, w, 0, 0))
    return pl.pallas_call(
        functools.partial(whole_grad_kernel, chips, len(earlier)),
        grid=(n, size),
        in_specs=[
            pl.BlockSpec(memory_space=pltpu.SMEM),
            pl.BlockSpec((1, frames, width), lambda w, m: (w, 0, 0)),
            pl.BlockSpec((1, local, frames), lambda w, m: (w, m, 0)),
        ]
        + [out] * len(earlier),
        out_specs=out,
        out_shape=shape_of((size, chips, n, depth, local), bf16),
        scratch_shapes=[pltpu.VMEM((width, frames), bf16)],
        compiler_params=params(),
        cost_estimate=pl.CostEstimate(
            flops=n * frames * width * local * size,
            bytes_accessed=2 * n * (frames * width + 2 * width * local * size),
            transcendentals=0,
        ),
        name="whole_grad",
    )(core, lefts, rights, *earlier)


def turning(rows):
    size = lax.axis_size("mp")
    me = lax.axis_index("mp")
    starts = jnp.stack([(me ^ k) * rows for k in range(size)])
    places = (starts[:, None] + jnp.arange(rows)[None, :] + 1).reshape(-1).astype(f32)
    rates = jnp.exp(jnp.arange(HALF).astype(f32) * (-2.0 * math.log(10000.0) / HEAD_DIM))
    angles = rates[:, None] * places[None, :]
    return (jnp.cos(angles), jnp.sin(angles))


def row_blocks(values, count):
    return jnp.split(values, count, axis=0)


def sum_over_clips(values, axis):
    return lax.psum_scatter(values.astype(bf16), "dp", scatter_dimension=axis, tiled=True)


def shards(
    frames_in,
    prompt,
    lengths,
    tsteps,
    table,
    gain_one,
    shift_one,
    gain_two,
    shift_two,
    gain_three,
    shift_three,
    w_query,
    w_key,
    w_value,
    w_out,
    c_query,
    c_key,
    c_value,
    c_out,
    w_gate,
    w_up,
    w_down,
    cotangent,
):
    size = lax.axis_size("mp")
    groups = lax.axis_size("dp")
    count, rows, width = frames_in.shape
    clips = range(count)
    local = w_query.shape[1]
    here = lax.axis_index("mp")
    there = lax.axis_index("dp")
    core = there & 1
    chain = Chain()
    hold, mark, arrive = chain.hold, chain.mark, chain.arrive

    def joined(parts, axis):
        return jnp.concatenate(parts, axis=axis)

    resid, ones, low = [], [], []
    for b in clips:
        resid.append(hold(frames_in[b]).astype(f32))
        ones.append(norm_forward(resid[b], gain_one, shift_one))
        low.append(ones[b][0].astype(bf16))
        mark(low[b])
        if b == 0:
            spread_one = [Spread(low[0])]

    depth = width // groups
    query_part = lax.dynamic_slice_in_dim(hold(c_query), there * depth, depth, 0)
    out_part = lax.dynamic_slice_in_dim(hold(c_out), there * depth, depth, 1).T
    side = jnp.stack([query_part, out_part])
    side = [side] + [swap(side, "mp", k) for k in range(1, size)]
    w_turned = joined([hold(w_query).T, w_key.T, w_value.T], 0)
    cosine, sine = turning(rows)
    mark(w_turned)
    memory = joined([hold(c_key), c_value], 1)
    memory = jnp.stack([dot(memory, prompt[b], 0, 1).astype(bf16) for b in clips])
    mark(memory)
    for b in clips:
        spread_one[b].first = arrive(spread_one[b].first)
        spread_one[b].second_step()
        if b + 1 < count:
            spread_one.append(Spread(hold(low[b + 1])))
        if b == 0:
            side = arrive(side)
            query_wide = joined([part[0] for part in side], 1)
            out_wide = joined([part[1] for part in side], 1)
            mark(query_wide, out_wide)
            c_query_all = lax.all_gather(query_wide, "dp", axis=0, tiled=True)
            out_wide = after(out_wide, c_query_all)
            c_out_all = lax.all_gather(out_wide, "dp", axis=0, tiled=True)
            picked = jnp.take(hold(table), tsteps, axis=0)
            prefix_normed, prefix_normal, prefix_scale = norm_forward(picked, gain_one, shift_one)
            prefix_low = prefix_normed.astype(bf16)
            front = dot(w_turned[local:], prefix_low, 1, 1).astype(bf16)
            mark(front)
            spread_one[0].last = arrive(spread_one[0].last)
            half = lax.dynamic_slice_in_dim(hold(w_out), core * (local // 2), local // 2, 0)
            spread_out = Spread(half)
    front_keys = [front[:local, b : b + 1] for b in clips]
    front_values = [front[local:, b : b + 1] for b in clips]

    turned, mixed_part, logsum, mixed = [], [], [], []
    frames_one = ()
    for b in clips:
        if b:
            spread_one[b].last = arrive(spread_one[b].last)
        pieces = hold(spread_one[b].pieces())
        out, frames_one = project(b, count, pieces, w_turned, cosine, sine, list(frames_one))
        frames_one = (frames_one,)
        turned.append(out)
        mark(out)
        if b == 0:
            spread_out.first = arrive(spread_out.first)
            spread_out.second_step()
        out, sums = self_forward(hold(turned[b]), front_keys[b], front_values[b])
        mixed_part.append(out)
        logsum.append(sums)
        mark(out)
        mixed.append(trade(jnp.split(out, size, axis=1)))
        if b == 0:
            memory = hold(memory)
            memory = [memory] + [swap(memory, "mp", k) for k in range(1, size)]
            spread_out.last = arrive(spread_out.last)
            got = spread_out.pieces()[1:]
            got = joined(got, 0).reshape(size - 1, local // 2, width)
            other = swap(got, "dp", 1)
    frames_one = frames_one[0]
    down_in = lax.all_gather(hold(cotangent), "mp", axis=1, tiled=True)
    other = arrive(other)
    rest = joined([jnp.where(core == 0, got, other), jnp.where(core == 0, other, got)], 1)
    out_all = joined([w_out, rest.reshape(-1, width)], 0)
    memory = jnp.stack(memory, axis=1)
    cross_keys = [memory[b, :, :local].reshape(size * local, -1) for b in clips]
    cross_values = [memory[b, :, local:].reshape(size * local, -1) for b in clips]
    mark(out_all)

    first, twos, normed_two, cross_query, cross_sums, cross_mixed = [], [], [], [], [], []
    second, threes, low = [], [], []
    for b in clips:
        mixed[b] = joined(hold(mixed[b]), 0)
        first.append(resid[b] + dot(mixed[b], out_all, 0, 0))
        twos.append(norm_forward(first[b], gain_two, shift_two))
        normed_two.append(twos[b][0].astype(bf16))
        cross_query.append((dot(c_query_all, normed_two[b], 0, 1) * FACTOR).astype(bf16))
        out, sums = cross_forward(
            b, size, lengths, cross_query[b], cross_keys[b], cross_values[b]
        )
        cross_mixed.append(out)
        cross_sums.append(sums)
        mark(out)
    spread_three = []
    for b in clips:
        second.append(first[b] + dot(hold(cross_mixed[b]), c_out_all, 0, 1))
        threes.append(norm_forward(second[b], gain_three, shift_three))
        low.append(threes[b][0].astype(bf16))
        mark(low[b])
        if b == 0:
            spread_three.append(Spread(low[b]))

    order = jnp.stack([here ^ k for k in range(size)]).astype(jnp.int32)
    back_pieces, back_three = [], []
    parts = ()
    for b in clips:
        if b + 1 < count:
            spread_three[b].first = arrive(spread_three[b].first)
            spread_three[b].second_step()
            spread_three.append(Spread(hold(low[b + 1])))
            spread_three[b].last = arrive(spread_three[b].last)
            spread_three[b + 1].first = arrive(spread_three[b + 1].first)
            spread_three[b + 1].second_step()
        pieces = hold(spread_three[b].pieces())
        parts = glu(b, order, pieces, down_in, w_gate, w_up, w_down, list(parts))
        mark(parts[1])
        if b:
            came = arrive(came)
            back_three.append(settle_last(back_pieces[b - 1], came))
        grad_gate, grad_upper = hold((parts[1], parts[2]))
        back_pieces.append(glu_back(b, grad_gate, grad_upper, w_gate, w_up))
        mark(back_pieces[b][0])
        came = settle_first(back_pieces[b])
        if b + 1 < count:
            spread_three[b + 1].last = arrive(spread_three[b + 1].last)

    def flat(values):
        return values.reshape(-1, values.shape[-1])

    hidden, grad_gate, grad_upper, frames_three = parts
    raw_w_down = dot(flat(hold(down_in)), flat(hidden), 0, 0).astype(bf16)
    grad_w_down = sum_over_clips(raw_w_down, 0)
    mark(raw_w_down)
    back_three.append(settle_last(back_pieces[-1], arrive(came)))

    grad_two, grad_one, cross_in, self_in = [], [], [], []
    grad_cross_query, grad_memory, grad_mixed, back_two = [], [], [], []
    for b in clips:
        back_three[b] = total(hold(back_three[b]))
        cot = cotangent[b].astype(f32)
        grad_two.append(cot + norm_backward(back_three[b], threes[b][1], threes[b][2], gain_three))
        cross_in.append(grad_two[b].astype(bf16))
        grads = dot(c_out_all, cross_in[b], 0, 1).astype(bf16)
        grad_queries, grad_keys, grad_values = cross_backward(
            b,
            size,
            lengths,
            cross_query[b],
            cross_keys[b],
            cross_values[b],
            grads,
            cross_mixed[b],
            cross_sums[b],
        )
        grad_cross_query.append(grad_queries)
        grad_memory.append(
            joined([grad_keys.reshape(size, local, -1), grad_values.reshape(size, local, -1)], 1)
        )
        back_two.append(dot(grad_queries, c_query_all, 0, 1))
        grad_one.append(
            grad_two[b] + norm_backward(back_two[b], twos[b][1], twos[b][2], gain_two)
        )
        self_in.append(grad_one[b].astype(bf16))
        grads = dot(out_all, self_in[b], 1, 1).astype(bf16)
        mark(grads)
        grad_mixed.append(trade(row_blocks(grads, size)))
        if b == 0:
            raw_w_gate = dot(flat(hold(frames_three)), flat(grad_gate), 0, 0).astype(bf16)
            grad_w_gate = sum_over_clips(raw_w_gate, 0)
            mark(raw_w_gate)

    branch = dot(flat(hold(hidden)), w_down, 1, 0).astype(bf16)
    mark(branch)
    branch = lax.psum_scatter(
        branch.reshape(count, size * rows, width), "mp", scatter_dimension=1, tiled=True
    )
    grad_memory = jnp.stack(grad_memory)
    grad_memory = trade([grad_memory[:, k] for k in range(size)])

    w_self = w_turned.T
    grad_self, grad_front, back_one = [], [], []
    for b in clips:
        grads, grad_front_key, grad_front_value = self_backward(
            turned[b],
            joined(hold(grad_mixed[b]), 1),
            mixed_part[b],
            logsum[b],
            front_keys[b],
            front_values[b],
            cosine,
            sine,
        )
        grad_self.append(grads.reshape(3 * local, -1))
        grad_front.append(joined([grad_front_key, grad_front_value], 0))
        mark(grads)
        if b:
            came = arrive(came)
            back_one.append(settle_last(pieces, came))
        pieces = cut(dot(hold(grad_self[b]), w_turned, 0, 0).astype(bf16))
        mark(*pieces)
        came = settle_first(pieces)
        if b == 0:
            raw_w_up = dot(flat(hold(frames_three)), flat(grad_upper), 0, 0).astype(bf16)
            grad_w_up = sum_over_clips(raw_w_up, 0)
            mark(raw_w_up)

    grad_front = joined(grad_front, 1)
    turned_grads = joined(hold(grad_self), 1)
    raw_w_self = dot(flat(frames_one), turned_grads, 0, 1)
    filled = joined([jnp.zeros((local, count), bf16), grad_front], 0)
    raw_w_self = raw_w_self + dot(prefix_low, filled, 0, 1)
    low_w_self = raw_w_self.astype(bf16).reshape(groups, -1, 3 * local)
    mark(low_w_self)
    mine, other = core_half(low_w_self)
    back_one.append(settle_last(pieces, arrive(came)))

    lefts = jnp.stack([joined(hold(part), 0) for part in (normed_two, cross_in, self_in)])
    rights = jnp.stack([joined(part, 1) for part in (grad_cross_query, cross_mixed, mixed)])
    other_raws = whole_grad(jnp.stack([1 - core]), groups, lefts, rights, [])
    mark(other_raws)
    other_raws = swap(other_raws, "dp", 1)
    low_w_self = plus(mine, arrive(other))
    mark(low_w_self)
    grad_w_self = chips_sum(low_w_self)

    grad_memory = total(arrive(grad_memory)).astype(bf16)
    grad_memory = joined([grad_memory[b] for b in clips], 1)
    grad_c_memory = dot(prompt.reshape(-1, prompt.shape[-1]), grad_memory, 0, 1).astype(bf16)
    mark(grad_c_memory)
    grad_c_memory = sum_over_clips(grad_c_memory, 0)

    raws = whole_grad(jnp.stack([core]), groups, lefts, rights, [arrive(other_raws)])
    mark(raws)
    pieces = [raws[k].reshape(-1, local) for k in range(size)]
    pieces = cut(joined(pieces, 0))
    came = settle_first(pieces)

    small = []
    wide_w_self = w_self.astype(f32)
    sums = jnp.sum(turned_grads.astype(f32), axis=1)
    front_sums = jnp.sum(grad_front.astype(f32), axis=1)
    sums = joined([sums[:local], sums[local:] + front_sums], 0)
    shift_term = jnp.sum(wide_w_self * sums[None, :], axis=1)
    gain_term = jnp.sum(wide_w_self * raw_w_self, axis=1)
    small.append((gain_term - shift_one * shift_term) / gain_one)
    small.append(shift_term)
    for back, kept in ((back_two, twos), (back_three, threes)):
        small.append(sum(jnp.sum(back[b] * kept[b][1], axis=0) for b in clips))
        small.append(sum(jnp.sum(back[b], axis=0) for b in clips))

    steps = jnp.where(here == 0, tsteps, 0).astype(f32)
    steps = lax.dynamic_update_slice(jnp.zeros((width,), f32), steps, (there * count,))
    small.append(steps)

    back_prefix = dot(grad_front, w_turned[local:], 0, 0)
    grad_picked = norm_backward(back_prefix, prefix_normal, prefix_scale, gain_one)
    spots = jnp.arange(groups)[:, None, None] == there
    spots = jnp.where(spots, grad_picked[None], 0.0).reshape(groups * count, width)
    small = joined([jnp.stack(small), spots], 0)
    mark(small)
    raws = total(settle_last(pieces, arrive(came)))
    raws = raws.astype(bf16).reshape(groups // 2, -1, local)
    mark(raws)
    raws = chips_sum(raws).reshape(3, -1, local)
    small = all_sum(small)
    all_steps = small[6, : groups * count]
    matches = jnp.arange(table.shape[0])[:, None].astype(f32) == all_steps[None, :]
    grad_table = jnp.dot(matches.astype(f32), small[7:], precision=lax.Precision.HIGHEST)

    back_one = [total(terms) for terms in back_one]
    grad_frames = [
        grad_one[b] + norm_backward(back_one[b], ones[b][1], ones[b][2], gain_one) for b in clips
    ]
    output = [second[b] + branch[b].astype(f32) for b in clips]

    def wide(value):
        return value.astype(f32)

    return (
        jnp.stack(output),
        jnp.stack(grad_frames),
        grad_table,
        small[0],
        small[1],
        small[2],
        small[3],
        small[4],
        small[5],
        grad_w_self[:, :local],
        grad_w_self[:, local : 2 * local],
        grad_w_self[:, 2 * local :],
        raws[2].T,
        raws[0],
        wide(grad_c_memory[:, :local]),
        wide(grad_c_memory[:, local:]),
        raws[1].T,
        wide(grad_w_gate),
        wide(grad_w_up),
        wide(grad_w_down.T),
    )


def solution(mesh):
    placed = (
        P("dp", "mp", None),
        P("dp", None, None),
        P("dp"),
        P("dp"),
        P(),
        P(),
        P(),
        P(),
        P(),
        P(),
        P(),
        P(None, "mp"),
        P(None, "mp"),
        P(None, "mp"),
        P("mp", None),
        P(None, "mp"),
        P(None, "mp"),
        P(None, "mp"),
        P("mp", None),
        P(None, "mp"),
        P(None, "mp"),
        P("mp", None),
        P("dp", "mp", None),
    )
    return jax.shard_map(
        shards,
        mesh=mesh,
        in_specs=placed,
        out_specs=(
            P("dp", "mp", None),
            P("dp", "mp", None),
            P(),
            P(),
            P(),
            P(),
            P(),
            P(),
            P(),
            P("dp", "mp"),
            P("dp", "mp"),
            P("dp", "mp"),
            P("mp", "dp"),
            P("dp", "mp"),
            P("dp", "mp"),
            P("dp", "mp"),
            P("mp", "dp"),
            P("dp", "mp"),
            P("dp", "mp"),
            P("mp", "dp"),
        ),
        check_vma=False,
    )
```

```python
import functools
import math

import jax
import jax.numpy as jnp
from jax import lax
from jax.experimental import pallas as pl
from jax.experimental.pallas import tpu as pltpu
from jax.sharding import PartitionSpec as P

HEAD_DIM = 64
HALF = HEAD_DIM // 2
FACTOR = 1.0 / math.sqrt(HEAD_DIM)

norm_eps = 1e-05

f32 = jnp.float32
bf16 = jnp.bfloat16


def dot(left, right, left_axis, right_axis):
    return lax.dot_general(
        left, right, (((left_axis,), (right_axis,)), ((), ())), preferred_element_type=f32
    )


def norm_forward(values, gain, shift):
    center = values - jnp.mean(values, axis=-1, keepdims=True)
    scale = lax.rsqrt(jnp.mean(center * center, axis=-1, keepdims=True) + norm_eps)
    normal = center * scale
    return (normal * gain + shift, normal, scale)


def norm_backward(grad, normal, scale, gain):
    inner = grad * gain
    return scale * (
        inner
        - jnp.mean(inner, axis=-1, keepdims=True)
        - normal * jnp.mean(inner * normal, axis=-1, keepdims=True)
    )


def bits_of(size):
    return [1 << place for place in range(size.bit_length() - 1)]


def swap(values, axis, k):
    return lax.ppermute(values, axis, [(i, i ^ k) for i in range(lax.axis_size(axis))])


def after(values, *others):
    return lax.optimization_barrier((values,) + others)[0]


class Spread:
    def __init__(self, values):
        self.values = values
        if lax.axis_size("mp") == 4:
            self.first = (swap(values, "mp", 1), swap(values, "mp", 2))
        else:
            self.first = tuple(swap(values, "mp", k) for k in range(1, lax.axis_size("mp")))
        self.last = ()

    def second_step(self):
        if lax.axis_size("mp") == 4:
            half = self.values.shape[0] // 2
            one, two = self.first
            self.last = (swap(one[:half], "mp", 2), swap(two[half:], "mp", 1))

    def pieces(self):
        return [self.values, *self.first, *self.last]


def trade(blocks):
    return [blocks[0]] + [swap(blocks[k], "mp", k) for k in range(1, len(blocks))]


def cut(values):
    size = lax.axis_size("mp")
    blocks = jnp.split(values, size, axis=0)
    return blocks[:3] + jnp.split(blocks[3], 2, axis=0) if size == 4 else blocks


def settle_first(pieces):
    if lax.axis_size("mp") != 4:
        return ()
    return (swap(pieces[3], "mp", 2), swap(pieces[4], "mp", 1))


def settle_last(pieces, came):
    if lax.axis_size("mp") != 4:
        return trade(pieces)
    high, low = came
    half = high.shape[0]
    one = jnp.concatenate([plus(pieces[1][:half], high), pieces[1][half:]], axis=0)
    two = jnp.concatenate([pieces[2][:half], plus(pieces[2][half:], low)], axis=0)
    return [pieces[0], swap(one, "mp", 1), swap(two, "mp", 2)]


class Chain:
    def __init__(self):
        self.last = ()

    def hold(self, values):
        return after(values, *self.last) if self.last else values

    def mark(self, *values):
        self.last = values

    def arrive(self, values):
        values = self.hold(values)
        self.mark(values)
        return values


def plus(left, right):
    return (left.astype(f32) + right.astype(f32)).astype(bf16)


def total(terms):
    result = terms[0].astype(f32)
    for term in terms[1:]:
        result = result + term.astype(f32)
    return result


def all_sum(values):
    for axis in ("mp", "dp"):
        for bit in bits_of(lax.axis_size(axis)):
            values = values + swap(values, axis, bit)
    return values


def core_half(blocks):
    core = lax.axis_index("dp") & 1
    pairs = blocks.reshape((blocks.shape[0] // 2, 2) + blocks.shape[1:])
    mine = lax.dynamic_index_in_dim(pairs, core, 1, False)
    other = lax.dynamic_index_in_dim(pairs, 1 - core, 1, False)
    return (mine, swap(other, "dp", 1))


def chips_sum(blocks):
    here = lax.axis_index("dp") >> 1
    mine = [
        lax.dynamic_index_in_dim(blocks, here ^ k, 0, False) for k in range(blocks.shape[0])
    ]
    return total([mine[0]] + [swap(mine[k], "dp", 2 * k) for k in range(1, len(mine))])


def self_forward_kernel(block, q_ref, k_ref, v_ref, pk_ref, pv_ref, o_ref, l_ref):
    keys = k_ref[...]
    values = v_ref[...]
    front_key = pk_ref[...].astype(f32)
    front_value = pv_ref[...].astype(f32)
    for start in range(0, q_ref.shape[1], block):
        part = slice(start, start + block)
        queries = q_ref[:, part]
        scores = dot(keys, queries, 0, 0)
        front = jnp.sum(queries.astype(f32) * front_key, axis=0, keepdims=True)
        top = jnp.maximum(jnp.max(scores, axis=0, keepdims=True), front)
        weights = jnp.exp(scores - top)
        front_weight = jnp.exp(front - top)
        total = jnp.sum(weights, axis=0, keepdims=True) + front_weight
        mixed = dot(values, weights.astype(bf16), 1, 0)
        mixed = mixed + front_value * front_weight.astype(bf16).astype(f32)
        o_ref[:, part] = (mixed * (1.0 / total)).astype(bf16)
        l_ref[0, :, part] = top + jnp.log(total)


def self_backward_kernel(
    block,
    q_ref,
    k_ref,
    v_ref,
    g_ref,
    o_ref,
    l_ref,
    pk_ref,
    pv_ref,
    cos_ref,
    sin_ref,
    d_ref,
    dpk_ref,
    dpv_ref,
):
    frames = q_ref.shape[1]
    keys = k_ref[...]
    values = v_ref[...]
    front_key = pk_ref[...].astype(f32)
    front_value = pv_ref[...].astype(f32)
    grad_keys = jnp.zeros((HEAD_DIM, frames), f32)
    grad_values = jnp.zeros((HEAD_DIM, frames), f32)
    grad_front_key = jnp.zeros((HEAD_DIM, 1), f32)
    grad_front_value = jnp.zeros((HEAD_DIM, 1), f32)
    for start in range(0, frames, block):
        part = slice(start, start + block)
        queries = q_ref[:, part]
        grads = g_ref[:, part]
        wide_queries = queries.astype(f32)
        wide_grads = grads.astype(f32)
        logsum = l_ref[0, :, part]
        mixsum = jnp.sum(o_ref[:, part].astype(f32) * wide_grads, axis=0, keepdims=True)
        probs = jnp.exp(dot(keys, queries, 0, 0) - logsum)
        grad_probs = dot(values, grads, 0, 0)
        grad_scores = (probs * (grad_probs - mixsum)).astype(bf16)
        grad_values = grad_values + dot(grads, probs.astype(bf16), 1, 1)
        grad_keys = grad_keys + dot(queries, grad_scores, 1, 1)
        grad_queries = dot(keys, grad_scores, 1, 0)
        front = jnp.exp(jnp.sum(wide_queries * front_key, axis=0, keepdims=True) - logsum)
        grad_front = jnp.sum(wide_grads * front_value, axis=0, keepdims=True)
        grad_front = (front * (grad_front - mixsum)).astype(bf16).astype(f32)
        front = front.astype(bf16).astype(f32)
        grad_front_key += jnp.sum(wide_queries * grad_front, axis=1, keepdims=True)
        grad_front_value += jnp.sum(wide_grads * front, axis=1, keepdims=True)
        grad_queries = (grad_queries + front_key * grad_front) * FACTOR
        cosine = cos_ref[:, part]
        sine = sin_ref[:, part]
        upper, lower = grad_queries[:HALF], grad_queries[HALF:]
        d_ref[0, :HALF, part] = (upper * cosine + lower * sine).astype(bf16)
        d_ref[0, HALF:, part] = (lower * cosine - upper * sine).astype(bf16)
    cosine = cos_ref[...]
    sine = sin_ref[...]
    upper, lower = grad_keys[:HALF], grad_keys[HALF:]
    d_ref[1, :HALF, :] = (upper * cosine + lower * sine).astype(bf16)
    d_ref[1, HALF:, :] = (lower * cosine - upper * sine).astype(bf16)
    d_ref[2] = grad_values.astype(bf16)
    dpk_ref[...] = grad_front_key.astype(bf16)
    dpv_ref[...] = grad_front_value.astype(bf16)


def cross_forward_kernel(clip, heads, n_ref, q_ref, k_ref, v_ref, o_ref, l_ref):
    live = lax.broadcasted_iota(jnp.int32, (k_ref.shape[1], 1), 0) < n_ref[clip]
    for head in range(heads):
        part = slice(head * HEAD_DIM, (head + 1) * HEAD_DIM)
        scores = jnp.where(live, dot(k_ref[part], q_ref[part], 0, 0), -1e30)
        top = jnp.max(scores, axis=0, keepdims=True)
        weights = jnp.exp(scores - top)
        total = jnp.sum(weights, axis=0, keepdims=True)
        mixed = dot(v_ref[part], weights.astype(bf16), 1, 0)
        o_ref[part] = (mixed * (1.0 / total)).astype(bf16)
        l_ref[head] = top + jnp.log(total)


def cross_backward_kernel(
    clip, heads, n_ref, q_ref, k_ref, v_ref, g_ref, o_ref, l_ref, dq_ref, dk_ref, dv_ref
):
    live = lax.broadcasted_iota(jnp.int32, (k_ref.shape[1], 1), 0) < n_ref[clip]
    for head in range(heads):
        part = slice(head * HEAD_DIM, (head + 1) * HEAD_DIM)
        queries = q_ref[part]
        keys = k_ref[part]
        grads = g_ref[part]
        mixsum = jnp.sum(o_ref[part].astype(f32) * grads.astype(f32), axis=0, keepdims=True)
        scores = jnp.where(live, dot(keys, queries, 0, 0), -1e30)
        probs = jnp.exp(scores - l_ref[head])
        grad_scores = (probs * (dot(v_ref[part], grads, 0, 0) - mixsum)).astype(bf16)
        dq_ref[part] = (dot(keys, grad_scores, 1, 0) * FACTOR).astype(bf16)
        dk_ref[part] = dot(queries, grad_scores, 1, 1).astype(bf16)
        dv_ref[part] = dot(grads, probs.astype(bf16), 1, 1).astype(bf16)


def shape_of(shape, kind):
    return jax.ShapeDtypeStruct(shape, kind)


def params():
    return pltpu.CompilerParams(vmem_limit_bytes=48 * 2**20)


def self_cost(heads, frames, products):
    return pl.CostEstimate(
        flops=products * 2 * heads * frames * frames * HEAD_DIM * 4,
        bytes_accessed=products * 2 * heads * frames * HEAD_DIM * 2,
        transcendentals=heads * frames * frames,
    )


def self_forward(turned, front_keys, front_values):
    heads = front_keys.shape[0] // HEAD_DIM
    frames = turned.shape[1]

    def at(third):
        return pl.BlockSpec((HEAD_DIM, frames), lambda h: (third * heads + h, 0))

    column = pl.BlockSpec((HEAD_DIM, 1), lambda h: (h, 0))
    return pl.pallas_call(
        functools.partial(self_forward_kernel, frames),
        grid=(heads,),
        in_specs=[at(0), at(1), at(2), column, column],
        out_specs=[at(0), pl.BlockSpec((1, 1, frames), lambda h: (h, 0, 0))],
        out_shape=[
            shape_of((heads * HEAD_DIM, frames), bf16),
            shape_of((heads, 1, frames), f32),
        ],
        compiler_params=params(),
        cost_estimate=self_cost(heads, frames, 2),
        name="self_forward",
    )(turned, turned, turned, front_keys, front_values)


def self_backward(turned, grads, mixed, logsum, front_keys, front_values, cosine, sine):
    heads = front_keys.shape[0] // HEAD_DIM
    frames = turned.shape[1]

    def at(third):
        return pl.BlockSpec((HEAD_DIM, frames), lambda h: (third * heads + h, 0))

    column = pl.BlockSpec((HEAD_DIM, 1), lambda h: (h, 0))
    angles = pl.BlockSpec((HALF, frames), lambda h: (0, 0))
    return pl.pallas_call(
        functools.partial(self_backward_kernel, min(256, frames)),
        grid=(heads,),
        in_specs=[
            at(0),
            at(1),
            at(2),
            at(0),
            at(0),
            pl.BlockSpec((1, 1, frames), lambda h: (h, 0, 0)),
            column,
            column,
            angles,
            angles,
        ],
        out_specs=[
            pl.BlockSpec((3, HEAD_DIM, frames), lambda h: (0, h, 0)),
            column,
            column,
        ],
        out_shape=[
            shape_of((3, heads * HEAD_DIM, frames), bf16),
            shape_of((heads * HEAD_DIM, 1), bf16),
            shape_of((heads * HEAD_DIM, 1), bf16),
        ],
        compiler_params=params(),
        cost_estimate=self_cost(heads, frames, 5),
        name="self_backward",
    )(turned, turned, turned, grads, mixed, logsum, front_keys, front_values, cosine, sine)


def cross_specs(groups, heads, frames, slots):
    at_frames = pl.BlockSpec((heads * HEAD_DIM, frames), lambda h: (h, 0))
    at_slots = pl.BlockSpec((heads * HEAD_DIM, slots), lambda h: (h, 0))
    at_sums = pl.BlockSpec((heads, 1, frames), lambda h: (h, 0, 0))
    return (at_frames, at_slots, at_sums)


def cross_cost(rows, frames, slots, products):
    return pl.CostEstimate(
        flops=products * 2 * rows * frames * slots * 4,
        bytes_accessed=products * 2 * rows * frames,
        transcendentals=rows // HEAD_DIM * frames * slots,
    )


def cross_forward(clip, groups, lengths, queries, keys, values):
    rows, frames = queries.shape
    heads = rows // HEAD_DIM // groups
    slots = keys.shape[1]
    at_frames, at_slots, at_sums = cross_specs(groups, heads, frames, slots)
    return pl.pallas_call(
        functools.partial(cross_forward_kernel, clip, heads),
        grid=(groups,),
        in_specs=[pl.BlockSpec(memory_space=pltpu.SMEM), at_frames, at_slots, at_slots],
        out_specs=[at_frames, at_sums],
        out_shape=[
            shape_of((rows, frames), bf16),
            shape_of((rows // HEAD_DIM, 1, frames), f32),
        ],
        compiler_params=params(),
        cost_estimate=cross_cost(rows, frames, slots, 2),
        name="cross_forward",
    )(lengths, queries, keys, values)


def cross_backward(clip, groups, lengths, queries, keys, values, grads, mixed, logsum):
    rows, frames = queries.shape
    heads = rows // HEAD_DIM // groups
    slots = keys.shape[1]
    at_frames, at_slots, at_sums = cross_specs(groups, heads, frames, slots)
    return pl.pallas_call(
        functools.partial(cross_backward_kernel, clip, heads),
        grid=(groups,),
        in_specs=[
            pl.BlockSpec(memory_space=pltpu.SMEM),
            at_frames,
            at_slots,
            at_slots,
            at_frames,
            at_frames,
            at_sums,
        ],
        out_specs=[at_frames, at_slots, at_slots],
        out_shape=[
            shape_of((rows, frames), bf16),
            shape_of((rows, slots), bf16),
            shape_of((rows, slots), bf16),
        ],
        compiler_params=params(),
        cost_estimate=cross_cost(rows, frames, slots, 5),
        name="cross_backward",
    )(lengths, queries, keys, values, grads, mixed, logsum)


def block_refs(refs, size):
    return [refs[0:1], refs[1:2], refs[2:3], refs[3:5]] if size == 4 else [[r] for r in refs]


def block_value(refs):
    parts = [ref[...] for ref in refs]
    return parts[0] if len(parts) == 1 else jnp.concatenate(parts, axis=0)


def whole_specs(pieces):
    return [pl.BlockSpec(piece.shape, lambda j: (0, 0)) for piece in pieces]


def project_kernel(size, heads, w_ref, cos_ref, sin_ref, *refs):
    d_ref, x_ref = refs[-2:]
    blocks = block_refs(refs[: 5 if size == 4 else size], size)
    for k in range(size):

        @pl.when(pl.program_id(0) == k)
        def _(k=k):
            frames = block_value(blocks[k])
            x_ref[0] = frames
            raw = dot(w_ref[...], frames, 1, 1)
            cosine = cos_ref[...]
            sine = sin_ref[...]
            for head in range(2 * heads):
                at = head * HEAD_DIM
                upper = raw[at : at + HALF]
                lower = raw[at + HALF : at + HEAD_DIM]
                first = upper * cosine - lower * sine
                second = lower * cosine + upper * sine
                if head < heads:
                    first, second = first * FACTOR, second * FACTOR
                d_ref[at : at + HALF] = first.astype(bf16)
                d_ref[at + HALF : at + HEAD_DIM] = second.astype(bf16)
            at = 2 * heads * HEAD_DIM
            d_ref[at:] = raw[at:].astype(bf16)


def project(clip, count, pieces, w_turned, cosine, sine, earlier):
    size = lax.axis_size("mp")
    depth, width = w_turned.shape
    rows = pieces[0].shape[0]
    angles = pl.BlockSpec((HALF, rows), lambda k: (0, k))
    return pl.pallas_call(
        functools.partial(project_kernel, size, depth // 3 // HEAD_DIM),
        grid=(size,),
        in_specs=[pl.BlockSpec((depth, width), lambda k: (0, 0)), angles, angles]
        + whole_specs(pieces)
        + [pl.BlockSpec(memory_space=pl.ANY)] * len(earlier),
        out_specs=[
            pl.BlockSpec((depth, rows), lambda k: (0, k)),
            pl.BlockSpec((1, rows, width), lambda k: (clip, k, 0)),
        ],
        out_shape=[
            shape_of((depth, size * rows), bf16),
            shape_of((count, size * rows, width), bf16),
        ],
        input_output_aliases={3 + len(pieces): 1} if earlier else {},
        compiler_params=params(),
        cost_estimate=pl.CostEstimate(
            flops=2 * depth * width * size * rows,
            bytes_accessed=4 * size * rows * width + 2 * depth * (width + size * rows),
            transcendentals=0,
        ),
        name="project",
    )(w_turned, cosine, sine, *pieces, *earlier)


def glu_kernel(size, given, n_ref, gate_ref, up_ref, down_ref, *refs):
    h_ref, dg_ref, du_ref, x_ref, c_ref = refs[-5:]
    blocks = block_refs(refs[:given], size)
    grads = block_refs(refs[given : 2 * given], size)
    rows = h_ref.shape[1] // size

    @pl.when(pl.program_id(0) == 0)
    def _():
        for k in range(size):
            there = pl.ds(pl.multiple_of(n_ref[k] * rows, rows), rows)
            x_ref[0, k * rows : (k + 1) * rows] = block_value(blocks[k])
            c_ref[0, there] = block_value(grads[k])

    for k in range(size):
        frames = block_value(blocks[k])
        part = slice(k * rows, (k + 1) * rows)
        there = pl.ds(pl.multiple_of(n_ref[k] * rows, rows), rows)
        gate = dot(frames, gate_ref[...], 1, 0)
        upper = dot(frames, up_ref[...], 1, 0)
        grad_hidden = dot(block_value(grads[k]), down_ref[...], 1, 1)
        sigma = 1.0 / (1.0 + jnp.exp(-gate))
        silu = gate * sigma
        h_ref[0, there] = (silu * upper).astype(bf16)
        dg_ref[0, part] = (grad_hidden * upper * (sigma + silu * (1.0 - sigma))).astype(bf16)
        du_ref[0, part] = (grad_hidden * silu).astype(bf16)


def glu(clip, count, order, pieces, grads, w_gate, w_up, w_down, earlier):
    size = lax.axis_size("mp")
    width, hidden = w_gate.shape
    rows = size * pieces[0].shape[0]
    block = 256
    columns = pl.BlockSpec((width, block), lambda j: (0, j))
    out = pl.BlockSpec((1, rows, block), lambda j: (clip, 0, j))
    whole = pl.BlockSpec((1, rows, width), lambda j: (clip, 0, 0))
    return pl.pallas_call(
        functools.partial(glu_kernel, size, len(pieces)),
        grid=(hidden // block,),
        in_specs=[
            pl.BlockSpec(memory_space=pltpu.SMEM),
            columns,
            columns,
            pl.BlockSpec((block, width), lambda j: (j, 0)),
        ]
        + whole_specs(pieces)
        + whole_specs(grads)
        + [pl.BlockSpec(memory_space=pl.ANY)] * len(earlier),
        out_specs=[out, out, out, whole, whole],
        out_shape=[shape_of((count, rows, hidden), bf16)] * 3
        + [shape_of((count, rows, width), bf16)] * 2,
        input_output_aliases={4 + 2 * len(pieces) + i: i for i in range(len(earlier))},
        compiler_params=params(),
        cost_estimate=pl.CostEstimate(
            flops=6 * rows * width * hidden,
            bytes_accessed=8 * rows * width + 6 * width * hidden + 6 * rows * hidden,
            transcendentals=rows * hidden,
        ),
        name="glu",
    )(order, w_gate, w_up, w_down, *pieces, *grads, *earlier)


def glu_back_kernel(size, dg_ref, du_ref, gate_ref, up_ref, *refs):
    blocks = block_refs(refs, size)
    rows = dg_ref.shape[1] // size
    for k in range(size):
        part = slice(k * rows, (k + 1) * rows)
        back = dot(dg_ref[0, part], gate_ref[...], 1, 1) + dot(du_ref[0, part], up_ref[...], 1, 1)
        at = 0
        for ref in blocks[k]:
            ref[...] = back[at : at + ref.shape[0]].astype(bf16)
            at += ref.shape[0]


def glu_back(clip, grad_gate, grad_upper, w_gate, w_up):
    size = lax.axis_size("mp")
    _, frames, hidden = grad_gate.shape
    rows = frames // size
    width = w_gate.shape[0]
    block = 256
    sizes = [rows] * 3 + [rows // 2] * 2 if size == 4 else [rows] * size
    whole = pl.BlockSpec((1, frames, hidden), lambda j: (clip, 0, 0))
    part = pl.BlockSpec((block, hidden), lambda j: (j, 0))
    return pl.pallas_call(
        functools.partial(glu_back_kernel, size),
        grid=(width // block,),
        in_specs=[whole, whole, part, part],
        out_specs=[pl.BlockSpec((n, block), lambda j: (0, j)) for n in sizes],
        out_shape=[shape_of((n, width), bf16) for n in sizes],
        compiler_params=params(),
        cost_estimate=pl.CostEstimate(
            flops=4 * frames * width * hidden,
            bytes_accessed=4 * frames * hidden + 4 * width * hidden + 2 * frames * width,
            transcendentals=0,
        ),
        name="glu_back",
    )(grad_gate, grad_upper, w_gate, w_up)


def whole_grad_kernel(chips, given, core_ref, x_ref, y_ref, *refs):
    o_ref, turned_ref = refs[-2:]
    depth = o_ref.shape[3]

    @pl.when(pl.program_id(1) == 0)
    def _():
        turned_ref[...] = x_ref[0].T

    for z in range(chips):
        at = pl.multiple_of((2 * z + core_ref[0]) * depth, depth)
        result = dot(turned_ref[pl.ds(at, depth)], y_ref[0], 1, 1)
        if given:
            result = result + refs[0][0, z, 0].astype(f32)
        o_ref[0, z, 0] = result.astype(bf16)


def whole_grad(core, groups, lefts, rights, earlier):
    size = lax.axis_size("mp")
    n, frames, width = lefts.shape
    local = rights.shape[1] // size
    chips = groups // 2
    depth = width // groups
    out = pl.BlockSpec((1, chips, 1, depth, local), lambda w, m: (m, 0, w, 0, 0))
    return pl.pallas_call(
        functools.partial(whole_grad_kernel, chips, len(earlier)),
        grid=(n, size),
        in_specs=[
            pl.BlockSpec(memory_space=pltpu.SMEM),
            pl.BlockSpec((1, frames, width), lambda w, m: (w, 0, 0)),
            pl.BlockSpec((1, local, frames), lambda w, m: (w, m, 0)),
        ]
        + [out] * len(earlier),
        out_specs=out,
        out_shape=shape_of((size, chips, n, depth, local), bf16),
        scratch_shapes=[pltpu.VMEM((width, frames), bf16)],
        compiler_params=params(),
        cost_estimate=pl.CostEstimate(
            flops=n * frames * width * local * size,
            bytes_accessed=2 * n * (frames * width + 2 * width * local * size),
            transcendentals=0,
        ),
        name="whole_grad",
    )(core, lefts, rights, *earlier)


def turning(rows):
    size = lax.axis_size("mp")
    me = lax.axis_index("mp")
    starts = jnp.stack([(me ^ k) * rows for k in range(size)])
    places = (starts[:, None] + jnp.arange(rows)[None, :] + 1).reshape(-1).astype(f32)
    rates = jnp.exp(jnp.arange(HALF).astype(f32) * (-2.0 * math.log(10000.0) / HEAD_DIM))
    angles = rates[:, None] * places[None, :]
    return (jnp.cos(angles), jnp.sin(angles))


def row_blocks(values, count):
    return jnp.split(values, count, axis=0)


def sum_over_clips(values, axis):
    return lax.psum_scatter(values.astype(bf16), "dp", scatter_dimension=axis, tiled=True)


def shards(
    frames_in,
    prompt,
    lengths,
    tsteps,
    table,
    gain_one,
    shift_one,
    gain_two,
    shift_two,
    gain_three,
    shift_three,
    w_query,
    w_key,
    w_value,
    w_out,
    c_query,
    c_key,
    c_value,
    c_out,
    w_gate,
    w_up,
    w_down,
    cotangent,
):
    size = lax.axis_size("mp")
    groups = lax.axis_size("dp")
    count, rows, width = frames_in.shape
    clips = range(count)
    local = w_query.shape[1]
    here = lax.axis_index("mp")
    there = lax.axis_index("dp")
    core = there & 1
    chain = Chain()
    hold, mark, arrive = chain.hold, chain.mark, chain.arrive

    def joined(parts, axis):
        return jnp.concatenate(parts, axis=axis)

    resid, ones, low = [], [], []
    for b in clips:
        resid.append(hold(frames_in[b]).astype(f32))
        ones.append(norm_forward(resid[b], gain_one, shift_one))
        low.append(ones[b][0].astype(bf16))
        mark(low[b])
        if b == 0:
            spread_one = [Spread(low[0])]

    depth = width // groups
    side = lax.dynamic_slice_in_dim(hold(c_query), there * depth, depth, 0)
    side = [side] + [swap(side, "mp", k) for k in range(1, size)]
    w_turned = joined([hold(w_query).T, w_key.T, w_value.T], 0)
    cosine, sine = turning(rows)
    mark(w_turned)
    memory = joined([hold(c_key), c_value], 1)
    memory = jnp.stack([dot(memory, prompt[b], 0, 1).astype(bf16) for b in clips])
    mark(memory)
    spread_one[0].first = arrive(spread_one[0].first)
    spread_one[0].second_step()
    for b in clips[1:]:
        spread_one.append(Spread(hold(low[b])))
    side = joined(arrive(side), 1)
    mark(side)
    c_query_all = lax.all_gather(side, "dp", axis=0, tiled=True)
    side = lax.dynamic_slice_in_dim(hold(c_out), there * depth, depth, 1).T
    side = [side] + [swap(side, "mp", k) for k in range(1, size)]
    picked = jnp.take(hold(table), tsteps, axis=0)
    prefix_normed, prefix_normal, prefix_scale = norm_forward(picked, gain_one, shift_one)
    prefix_low = prefix_normed.astype(bf16)
    front = dot(w_turned[local:], prefix_low, 1, 1).astype(bf16)
    mark(front)
    front_keys = [front[:local, b : b + 1] for b in clips]
    front_values = [front[local:, b : b + 1] for b in clips]
    spread_one[0].last = arrive(spread_one[0].last)
    half = lax.dynamic_slice_in_dim(hold(w_out), core * (local // 2), local // 2, 0)
    spread_out = Spread(half)

    turned, mixed_part, logsum, mixed = [], [], [], []
    frames_one = ()
    for b in clips:
        if b:
            spread_one[b].last = arrive(spread_one[b].last)
        pieces = hold(spread_one[b].pieces())
        out, frames_one = project(b, count, pieces, w_turned, cosine, sine, list(frames_one))
        frames_one = (frames_one,)
        turned.append(out)
        mark(out)
        if b == 0:
            for later in spread_one[1:]:
                later.first = arrive(later.first)
                later.second_step()
            side = joined(arrive(side), 1)
            mark(side)
            c_out_all = lax.all_gather(side, "dp", axis=0, tiled=True)
        else:
            spread_out.last = arrive(spread_out.last)
            got = spread_out.pieces()[1:]
            got = joined(got, 0).reshape(size - 1, local // 2, width)
            mark(got)
            other = swap(got, "dp", 1)
            spread_down = [Spread(hold(cotangent[0]))]
        out, sums = self_forward(hold(turned[b]), front_keys[b], front_values[b])
        mixed_part.append(out)
        logsum.append(sums)
        mark(out)
        mixed.append(trade(jnp.split(out, size, axis=1)))
        if b == 0:
            memory = hold(memory)
            memory = [memory] + [swap(memory, "mp", k) for k in range(1, size)]
            spread_out.first = arrive(spread_out.first)
            spread_out.second_step()
    frames_one = frames_one[0]
    other = arrive(other)
    rest = joined([jnp.where(core == 0, got, other), jnp.where(core == 0, other, got)], 1)
    out_all = joined([w_out, rest.reshape(-1, width)], 0)
    mark(out_all)
    memory = jnp.stack(arrive(memory), axis=1)
    cross_keys = [memory[b, :, :local].reshape(size * local, -1) for b in clips]
    cross_values = [memory[b, :, local:].reshape(size * local, -1) for b in clips]
    mark(memory)

    first, twos, normed_two, cross_query, cross_sums, cross_mixed = [], [], [], [], [], []
    second, threes, low = [], [], []
    for b in clips:
        mixed[b] = joined(hold(mixed[b]), 0)
        first.append(resid[b] + dot(mixed[b], out_all, 0, 0))
        twos.append(norm_forward(first[b], gain_two, shift_two))
        normed_two.append(twos[b][0].astype(bf16))
        mark(normed_two[b])
    for b in clips:
        cross_query.append((dot(c_query_all, hold(normed_two[b]), 0, 1) * FACTOR).astype(bf16))
        out, sums = cross_forward(
            b, size, lengths, cross_query[b], cross_keys[b], cross_values[b]
        )
        cross_mixed.append(out)
        cross_sums.append(sums)
        mark(out)
        if b == 0:
            spread_down[0].first = arrive(spread_down[0].first)
            spread_down[0].second_step()
    spread_three = []
    for b in clips:
        second.append(first[b] + dot(hold(cross_mixed[b]), c_out_all, 0, 1))
        threes.append(norm_forward(second[b], gain_three, shift_three))
        low.append(threes[b][0].astype(bf16))
        mark(low[b])
        if b == 0:
            spread_three.append(Spread(low[b]))

    order = jnp.stack([here ^ k for k in range(size)]).astype(jnp.int32)
    back_pieces, back_three = [], []
    parts = ()
    for b in clips:
        if b == 0:
            spread_down[0].last = arrive(spread_down[0].last)
            spread_three[0].first = arrive(spread_three[0].first)
            spread_three[0].second_step()
            spread_three.extend(Spread(hold(later)) for later in low[1:])
            spread_down.extend(Spread(hold(later)) for later in cotangent[1:])
        spread_three[b].last = arrive(spread_three[b].last)
        pieces = hold(spread_three[b].pieces())
        parts = glu(
            b, count, order, pieces, spread_down[b].pieces(), w_gate, w_up, w_down, list(parts)
        )
        mark(parts[1])
        if b == 0:
            for later in spread_three[1:] + spread_down[1:]:
                later.first = arrive(later.first)
                later.second_step()
        else:
            back_three.append(settle_last(back_pieces[b - 1], arrive(came)))
        grad_gate, grad_upper = hold((parts[1], parts[2]))
        back_pieces.append(glu_back(b, grad_gate, grad_upper, w_gate, w_up))
        mark(back_pieces[b][0])
        came = settle_first(back_pieces[b])
        if b == 0:
            for later in spread_three[1:] + spread_down[1:]:
                later.last = arrive(later.last)

    def flat(values):
        return values.reshape(-1, values.shape[-1])

    hidden, grad_gate, grad_upper, frames_three, down_in = parts
    raw_w_down = dot(flat(hold(down_in)), flat(hidden), 0, 0).astype(bf16)
    grad_w_down = sum_over_clips(raw_w_down, 0)
    mark(raw_w_down)
    back_three.append(settle_last(back_pieces[-1], arrive(came)))

    grad_two, grad_one, cross_in, self_in = [], [], [], []
    grad_cross_query, grad_memory, grad_mixed, back_two = [], [], [], []
    for b in clips:
        back_three[b] = total(hold(back_three[b]))
        cot = cotangent[b].astype(f32)
        grad_two.append(cot + norm_backward(back_three[b], threes[b][1], threes[b][2], gain_three))
        cross_in.append(grad_two[b].astype(bf16))
        grads = dot(c_out_all, cross_in[b], 0, 1).astype(bf16)
        grad_queries, grad_keys, grad_values = cross_backward(
            b,
            size,
            lengths,
            cross_query[b],
            cross_keys[b],
            cross_values[b],
            grads,
            cross_mixed[b],
            cross_sums[b],
        )
        grad_cross_query.append(grad_queries)
        grad_memory.append(
            joined([grad_keys.reshape(size, local, -1), grad_values.reshape(size, local, -1)], 1)
        )
        back_two.append(dot(grad_queries, c_query_all, 0, 1))
        grad_one.append(
            grad_two[b] + norm_backward(back_two[b], twos[b][1], twos[b][2], gain_two)
        )
        self_in.append(grad_one[b].astype(bf16))
        grads = dot(out_all, self_in[b], 1, 1).astype(bf16)
        mark(grads)
        grad_mixed.append(trade(row_blocks(grads, size)))
        if b == 0:
            raw_w_gate = dot(flat(hold(frames_three)), flat(grad_gate), 0, 0).astype(bf16)
            grad_w_gate = sum_over_clips(raw_w_gate, 0)
            mark(raw_w_gate)

    grad_memory = jnp.stack(hold(grad_memory))
    mark(grad_memory)
    grad_memory = trade([grad_memory[:, k] for k in range(size)])
    lefts = jnp.stack([joined(hold(part), 0) for part in (normed_two, cross_in, self_in)])
    rights = jnp.stack([joined(part, 1) for part in (grad_cross_query, cross_mixed, mixed)])
    other_raws = whole_grad(jnp.stack([1 - core]), groups, lefts, rights, [])
    mark(other_raws)
    other_raws = swap(other_raws, "dp", 1)

    w_self = w_turned.T
    grad_self, grad_front, back_one = [], [], []
    for b in clips:
        grads, grad_front_key, grad_front_value = self_backward(
            turned[b],
            joined(hold(grad_mixed[b]), 1),
            mixed_part[b],
            logsum[b],
            front_keys[b],
            front_values[b],
            cosine,
            sine,
        )
        grad_self.append(grads.reshape(3 * local, -1))
        grad_front.append(joined([grad_front_key, grad_front_value], 0))
        mark(grads)
        if b:
            raws_terms = settle_last(raws_pieces, arrive(raws_came))
        pieces = cut(dot(hold(grad_self[b]), w_turned, 0, 0).astype(bf16))
        mark(*pieces)
        came = settle_first(pieces)
        if b == 0:
            grad_w_down = arrive(grad_w_down)
            raw_w_up = dot(flat(hold(frames_three)), flat(grad_upper), 0, 0).astype(bf16)
            grad_w_up = sum_over_clips(raw_w_up, 0)
            mark(raw_w_up)
            back_one.append(settle_last(pieces, arrive(came)))
            raws = whole_grad(jnp.stack([core]), groups, lefts, rights, [arrive(other_raws)])
            mark(raws)
            raws_pieces = cut(raws.reshape(-1, local))
            raws_came = settle_first(raws_pieces)
            branch = dot(flat(hold(hidden)), w_down, 1, 0).astype(bf16)
            mark(branch)
            branch = branch.reshape(count, size * rows, width)
            branch = lax.psum_scatter(branch, "mp", scatter_dimension=1, tiled=True)

    grad_front = joined(grad_front, 1)
    turned_grads = joined(hold(grad_self), 1)
    raw_w_self = dot(flat(frames_one), turned_grads, 0, 1)
    filled = joined([jnp.zeros((local, count), bf16), grad_front], 0)
    raw_w_self = raw_w_self + dot(prefix_low, filled, 0, 1)
    mark(raw_w_self)
    grad_memory = total(hold(grad_memory)).astype(bf16)
    grad_memory = joined([grad_memory[b] for b in clips], 1)
    tokens = prompt.reshape(-1, prompt.shape[-1])
    low_w_self = joined(
        [
            raw_w_self.astype(bf16).reshape(groups, -1, 3 * local),
            joined(
                [
                    dot(tokens, part, 0, 1).astype(bf16).reshape(groups, -1, local)
                    for part in jnp.split(grad_memory, 2, axis=0)
                ],
                1,
            ),
        ],
        2,
    )
    mark(low_w_self)
    mine, other = core_half(low_w_self)
    back_one.append(settle_last(pieces, arrive(came)))
    grad_w_gate = arrive(grad_w_gate)
    raws = total(hold(raws_terms)).astype(bf16).reshape(groups // 2, -1, local)
    mark(raws)
    raws = chips_sum(raws).reshape(3, -1, local)
    low_w_self = plus(mine, arrive(other))
    mark(low_w_self)
    grad_w_self = chips_sum(low_w_self)

    small = []
    wide_w_self = w_self.astype(f32)
    sums = jnp.sum(turned_grads.astype(f32), axis=1)
    front_sums = jnp.sum(grad_front.astype(f32), axis=1)
    sums = joined([sums[:local], sums[local:] + front_sums], 0)
    shift_term = jnp.sum(wide_w_self * sums[None, :], axis=1)
    gain_term = jnp.sum(wide_w_self * raw_w_self, axis=1)
    small.append((gain_term - shift_one * shift_term) / gain_one)
    small.append(shift_term)
    for back, kept in ((back_two, twos), (back_three, threes)):
        small.append(sum(jnp.sum(back[b] * kept[b][1], axis=0) for b in clips))
        small.append(sum(jnp.sum(back[b], axis=0) for b in clips))

    steps = jnp.where(here == 0, tsteps, 0).astype(f32)
    steps = lax.dynamic_update_slice(jnp.zeros((width,), f32), steps, (there * count,))
    small.append(steps)

    back_prefix = dot(grad_front, w_turned[local:], 0, 0)
    grad_picked = norm_backward(back_prefix, prefix_normal, prefix_scale, gain_one)
    spots = jnp.arange(groups)[:, None, None] == there
    spots = jnp.where(spots, grad_picked[None], 0.0).reshape(groups * count, width)
    small = all_sum(joined([jnp.stack(small), spots], 0))
    all_steps = small[6, : groups * count]
    matches = jnp.arange(table.shape[0])[:, None].astype(f32) == all_steps[None, :]
    grad_table = jnp.dot(matches.astype(f32), small[7:], precision=lax.Precision.HIGHEST)

    back_one = [total(terms) for terms in back_one]
    grad_frames = [
        grad_one[b] + norm_backward(back_one[b], ones[b][1], ones[b][2], gain_one) for b in clips
    ]
    mark(grad_table, *grad_frames)
    grad_w_up = arrive(grad_w_up)
    branch = arrive(branch)
    output = [second[b] + branch[b].astype(f32) for b in clips]

    depth_c = prompt.shape[-1] // groups

    def wide(value):
        return value.astype(f32)

    return (
        jnp.stack(output),
        jnp.stack(grad_frames),
        grad_table,
        small[0],
        small[1],
        small[2],
        small[3],
        small[4],
        small[5],
        grad_w_self[:, :local],
        grad_w_self[:, local : 2 * local],
        grad_w_self[:, 2 * local : 3 * local],
        raws[2].T,
        raws[0],
        grad_w_self[: depth_c, 3 * local :],
        grad_w_self[depth_c:, 3 * local :],
        raws[1].T,
        wide(grad_w_gate),
        wide(grad_w_up),
        wide(grad_w_down.T),
    )


def solution(mesh):
    placed = (
        P("dp", "mp", None),
        P("dp", None, None),
        P("dp"),
        P("dp"),
        P(),
        P(),
        P(),
        P(),
        P(),
        P(),
        P(),
        P(None, "mp"),
        P(None, "mp"),
        P(None, "mp"),
        P("mp", None),
        P(None, "mp"),
        P(None, "mp"),
        P(None, "mp"),
        P("mp", None),
        P(None, "mp"),
        P(None, "mp"),
        P("mp", None),
        P("dp", "mp", None),
    )
    return jax.shard_map(
        shards,
        mesh=mesh,
        in_specs=placed,
        out_specs=(
            P("dp", "mp", None),
            P("dp", "mp", None),
            P(),
            P(),
            P(),
            P(),
            P(),
            P(),
            P(),
            P("dp", "mp"),
            P("dp", "mp"),
            P("dp", "mp"),
            P("mp", "dp"),
            P("dp", "mp"),
            P("dp", "mp"),
            P("dp", "mp"),
            P("mp", "dp"),
            P("dp", "mp"),
            P("dp", "mp"),
            P("mp", "dp"),
        ),
        check_vma=False,
    )
```

```python
import functools
import math

import jax
import jax.numpy as jnp
from jax import lax
from jax.experimental import pallas as pl
from jax.experimental.pallas import tpu as pltpu
from jax.sharding import PartitionSpec as P

HEAD_DIM = 64
HALF = HEAD_DIM // 2
FACTOR = 1.0 / math.sqrt(HEAD_DIM)

norm_eps = 1e-05

f32 = jnp.float32
bf16 = jnp.bfloat16


def dot(left, right, left_axis, right_axis):
    return lax.dot_general(
        left, right, (((left_axis,), (right_axis,)), ((), ())), preferred_element_type=f32
    )


def norm_forward(values, gain, shift):
    center = values - jnp.mean(values, axis=-1, keepdims=True)
    scale = lax.rsqrt(jnp.mean(center * center, axis=-1, keepdims=True) + norm_eps)
    normal = center * scale
    return (normal * gain + shift, normal, scale)


def norm_backward(grad, normal, scale, gain):
    inner = grad * gain
    return scale * (
        inner
        - jnp.mean(inner, axis=-1, keepdims=True)
        - normal * jnp.mean(inner * normal, axis=-1, keepdims=True)
    )


def bits_of(size):
    return [1 << place for place in range(size.bit_length() - 1)]


def swap(values, axis, k):
    return lax.ppermute(values, axis, [(i, i ^ k) for i in range(lax.axis_size(axis))])


def after(values, *others):
    return lax.optimization_barrier((values,) + others)[0]


class Spread:
    def __init__(self, values):
        self.values = values
        self.last = ()
        size = lax.axis_size("mp")
        partners = (1, 2) if size == 4 else range(1, size)
        self.first = tuple(swap(values, "mp", k) for k in partners)

    def second_step(self):
        if lax.axis_size("mp") == 4:
            one, two = self.first
            half = one.shape[0] // 2
            self.last = (swap(one[:half], "mp", 2), swap(two[half:], "mp", 1))

    def pieces(self):
        return [self.values, *self.first, *self.last]


def place(blocks, axis):
    here = lax.axis_index("mp")
    step = blocks[0].shape[axis]
    shape = list(blocks[0].shape)
    shape[axis] = step * len(blocks)
    result = jnp.zeros(shape, blocks[0].dtype)
    for k, block in enumerate(blocks):
        result = lax.dynamic_update_slice_in_dim(result, block, (here ^ k) * step, axis)
    return result


def gathered(values):
    return exchange(jnp.broadcast_to(values[None], (lax.axis_size("mp"),) + values.shape))


def exchange(blocks):
    return lax.all_to_all(blocks, "mp", 0, 0)


class Settle:
    def __init__(self, blocks):
        here = lax.axis_index("mp")
        size = blocks.shape[0]
        self.mine = [lax.dynamic_index_in_dim(blocks, here ^ k, 0, False) for k in range(size)]
        self.came = ()

    def first_step(self):
        if len(self.mine) == 4:
            half = self.mine[3].shape[0] // 2
            self.came = (swap(self.mine[3][:half], "mp", 2), swap(self.mine[3][half:], "mp", 1))

    def add(self):
        if len(self.mine) == 4:
            _, one, two, _ = self.mine
            high, low = self.came
            half = high.shape[0]
            one = jnp.concatenate([plus(one[:half], high), one[half:]], axis=0)
            two = jnp.concatenate([two[:half], plus(two[half:], low)], axis=0)
            self.mine = [self.mine[0], one, two]

    def second_step(self):
        return [self.mine[0]] + [swap(self.mine[k], "mp", k) for k in range(1, len(self.mine))]


def plus(left, right):
    return (left.astype(f32) + right.astype(f32)).astype(bf16)


def total(terms):
    result = terms[0].astype(f32)
    for k in range(1, len(terms)):
        result = result + terms[k].astype(f32)
    return result


def all_sum(values):
    for axis in ("dp", "mp"):
        for bit in bits_of(lax.axis_size(axis)):
            values = values + swap(values, axis, bit)
    return values


def core_half(blocks):
    core = lax.axis_index("dp") & 1
    pairs = blocks.reshape((blocks.shape[0] // 2, 2) + blocks.shape[1:])
    mine = lax.dynamic_index_in_dim(pairs, core, 1, False)
    other = lax.dynamic_index_in_dim(pairs, 1 - core, 1, False)
    return (mine, swap(other, "dp", 1))


class Chain:
    def __init__(self):
        self.last = ()

    def hold(self, values):
        return after(values, *self.last) if self.last else values

    def mark(self, *values):
        self.last = values

    def arrive(self, values):
        values = self.hold(values)
        self.mark(values)
        return values


def plus(left, right):
    return (left.astype(f32) + right.astype(f32)).astype(bf16)


def total(terms):
    result = terms[0].astype(f32)
    for term in terms[1:]:
        result = result + term.astype(f32)
    return result


def all_sum(values):
    for axis in ("dp", "mp"):
        for bit in bits_of(lax.axis_size(axis)):
            values = values + swap(values, axis, bit)
    return values


def core_half(blocks):
    core = lax.axis_index("dp") & 1
    pairs = blocks.reshape((blocks.shape[0] // 2, 2) + blocks.shape[1:])
    mine = lax.dynamic_index_in_dim(pairs, core, 1, False)
    other = lax.dynamic_index_in_dim(pairs, 1 - core, 1, False)
    return (mine, swap(other, "dp", 1))


def chips_sum(blocks):
    here = lax.axis_index("dp") >> 1
    mine = [
        lax.dynamic_index_in_dim(blocks, here ^ k, 0, False) for k in range(blocks.shape[0])
    ]
    return total([mine[0]] + [swap(mine[k], "dp", 2 * k) for k in range(1, len(mine))])


def self_forward_kernel(q_ref, k_ref, v_ref, pk_ref, pv_ref, o_ref, l_ref):
    parts = head_parts(q_ref.shape[0])
    scores = [dot(k_ref[part], q_ref[part], 0, 0) for part in parts]
    for head, part in enumerate(parts):
        front = q_ref[part].astype(f32) * pk_ref[part].astype(f32)
        front = jnp.sum(front, axis=0, keepdims=True)
        top = jnp.maximum(jnp.max(scores[head], axis=0, keepdims=True), front)
        weights = jnp.exp(scores[head] - top)
        front_weight = jnp.exp(front - top)
        total = jnp.sum(weights, axis=0, keepdims=True) + front_weight
        mixed = dot(v_ref[part], weights.astype(bf16), 1, 0)
        mixed = mixed + pv_ref[part].astype(f32) * front_weight.astype(bf16).astype(f32)
        mixed = (mixed * (1.0 / total)).astype(bf16)
        frames = o_ref.shape[2]
        for k in range(o_ref.shape[0]):
            o_ref[k, part] = mixed[:, k * frames : (k + 1) * frames]
        l_ref[head] = top + jnp.log(total)


def self_backward_kernel(
    block,
    q_ref,
    k_ref,
    v_ref,
    g_ref,
    o_ref,
    l_ref,
    pk_ref,
    pv_ref,
    cos_ref,
    sin_ref,
    d_ref,
    dpk_ref,
    dpv_ref,
):
    frames = q_ref.shape[1]
    keys = k_ref[...]
    values = v_ref[...]
    front_key = pk_ref[...].astype(f32)
    front_value = pv_ref[...].astype(f32)
    grad_keys = jnp.zeros((HEAD_DIM, frames), f32)
    grad_values = jnp.zeros((HEAD_DIM, frames), f32)
    grad_front_key = jnp.zeros((HEAD_DIM, 1), f32)
    grad_front_value = jnp.zeros((HEAD_DIM, 1), f32)
    whole_grads = jnp.concatenate([g_ref[k] for k in range(g_ref.shape[0])], axis=1)
    whole_mixed = jnp.concatenate([o_ref[k] for k in range(o_ref.shape[0])], axis=1)
    for start in range(0, frames, block):
        part = slice(start, start + block)
        queries = q_ref[:, part]
        grads = whole_grads[:, part]
        wide_queries = queries.astype(f32)
        wide_grads = grads.astype(f32)
        logsum = l_ref[0, :, part]
        mixsum = jnp.sum(whole_mixed[:, part].astype(f32) * wide_grads, axis=0, keepdims=True)
        probs = jnp.exp(dot(keys, queries, 0, 0) - logsum)
        grad_probs = dot(values, grads, 0, 0)
        grad_scores = (probs * (grad_probs - mixsum)).astype(bf16)
        grad_values = grad_values + dot(grads, probs.astype(bf16), 1, 1)
        grad_keys = grad_keys + dot(queries, grad_scores, 1, 1)
        grad_queries = dot(keys, grad_scores, 1, 0)
        front = jnp.exp(jnp.sum(wide_queries * front_key, axis=0, keepdims=True) - logsum)
        grad_front = jnp.sum(wide_grads * front_value, axis=0, keepdims=True)
        grad_front = (front * (grad_front - mixsum)).astype(bf16).astype(f32)
        front = front.astype(bf16).astype(f32)
        grad_front_key += jnp.sum(wide_queries * grad_front, axis=1, keepdims=True)
        grad_front_value += jnp.sum(wide_grads * front, axis=1, keepdims=True)
        grad_queries = (grad_queries + front_key * grad_front) * FACTOR
        cosine = cos_ref[:, part]
        sine = sin_ref[:, part]
        upper, lower = grad_queries[:HALF], grad_queries[HALF:]
        d_ref[0, :HALF, part] = (upper * cosine + lower * sine).astype(bf16)
        d_ref[0, HALF:, part] = (lower * cosine - upper * sine).astype(bf16)
    cosine = cos_ref[...]
    sine = sin_ref[...]
    upper, lower = grad_keys[:HALF], grad_keys[HALF:]
    d_ref[1, :HALF, :] = (upper * cosine + lower * sine).astype(bf16)
    d_ref[1, HALF:, :] = (lower * cosine - upper * sine).astype(bf16)
    d_ref[2] = grad_values.astype(bf16)
    dpk_ref[...] = grad_front_key.astype(bf16)
    dpv_ref[...] = grad_front_value.astype(bf16)


def head_parts(rows):
    return [slice(at, at + HEAD_DIM) for at in range(0, rows, HEAD_DIM)]


def fetch(core, out_halves, out, wholes, targets, sems):
    mine, other = out_halves
    size, half, _ = mine.shape
    copies = []
    for k in range(size):
        for source, part in ((mine, core), (other, 1 - core)):
            at = pl.multiple_of((2 * k + part) * half, 16)
            target = out.at[pl.ds(at, half)]
            copies.append(pltpu.make_async_copy(source.at[k], target, sems.at[len(copies)]))
    first = len(copies)
    for source, target in zip(wholes, targets):
        copies.append(pltpu.make_async_copy(source, target, sems.at[len(copies)]))

    def start_out():
        for copy in copies[:first]:
            copy.start()

    def start_whole(k):
        copies[first + k].start()

    def get_out():
        for copy in copies[:first]:
            copy.wait()
        return out[...]

    def get_whole(k):
        copies[first + k].wait()
        return targets[k]

    return start_out, start_whole, get_out, get_whole


def local_forward_kernel(
    clip, n_ref, core_ref, order_ref, mixed_ref, x_ref, norm_ref, mem_ref, wo_mine, wo_other, cq_hbm, co_hbm, *refs
):
    first_ref, second_ref, two_ref, q_ref, o_ref, l_ref, three_ref, wo, cq, co, sems = refs
    start_out, start_whole, get_out, get_whole = fetch(
        core_ref[0], (wo_mine, wo_other), wo, (cq_hbm, co_hbm), (cq, co), sems
    )
    start_out()
    start_whole(0)
    start_whole(1)
    groups, depth, slots = mem_ref.shape
    local = depth // 2
    live = lax.broadcasted_iota(jnp.int32, (slots, 1), 0) < n_ref[clip]
    first = x_ref[...].astype(f32) + dot(mixed_ref[...], get_out(), 0, 0)
    first_ref[...] = first
    two = norm_forward(first, norm_ref[0:1], norm_ref[1:2])[0].astype(bf16)
    two_ref[...] = two
    weight = get_whole(0)
    for k in range(groups):
        q_ref[k * local : (k + 1) * local] = (dot(two, weight[k], 1, 0) * FACTOR).astype(bf16).T
    for group in range(groups):
        parts = head_parts(local)
        there = order_ref[group]
        at = group * local
        queries = [q_ref[at + p.start : at + p.stop] for p in parts]
        scores = [dot(mem_ref[there, p], q, 0, 0) for p, q in zip(parts, queries)]
        scores = [jnp.where(live, s, -1e30) for s in scores]
        tops = [jnp.max(s, axis=0, keepdims=True) for s in scores]
        weights = [jnp.exp(s - top) for s, top in zip(scores, tops)]
        totals = [jnp.sum(w, axis=0, keepdims=True) for w in weights]
        for head, p in enumerate(parts):
            values = mem_ref[there, local + p.start : local + p.stop]
            mixed = dot(values, weights[head].astype(bf16), 1, 0)
            o_ref[at + p.start : at + p.stop] = (mixed * (1.0 / totals[head])).astype(bf16)
            l_ref[group * len(parts) + head] = tops[head] + jnp.log(totals[head])
    weight = get_whole(1)
    second = first
    for k in range(groups):
        second = second + dot(o_ref[k * local : (k + 1) * local], weight[k], 0, 1)
    second_ref[...] = second
    three_ref[...] = norm_forward(second, norm_ref[2:3], norm_ref[3:4])[0].astype(bf16)


def local_specs(clip, count, rows, width, memory):
    groups, depth, slots = memory.shape
    heads = groups * depth // 2 // HEAD_DIM
    wide = pl.BlockSpec((rows, width), lambda i: (0, 0))
    turned = pl.BlockSpec((width, rows), lambda i: (0, 0))
    sums = pl.BlockSpec((heads, 1, rows), lambda i: (0, 0, 0))
    norms = pl.BlockSpec((4, width), lambda i: (0, 0))
    mem = pl.BlockSpec((groups, depth, slots // count), lambda i: (0, 0, clip))
    return (wide, turned, sums, norms, mem, heads)


def local_forward(clip, count, lengths, core, order, mixed, frames, norms, memory, weights):
    rows, width = frames.shape
    wide, turned, sums, norm_spec, mem, heads = local_specs(clip, count, rows, width, memory)
    return pl.pallas_call(
        functools.partial(local_forward_kernel, clip),
        grid=(1,),
        in_specs=[pl.BlockSpec(memory_space=pltpu.SMEM)] * 3
        + [turned, wide, norm_spec, mem]
        + [pl.BlockSpec(memory_space=pl.ANY)] * 4,
        out_specs=[wide, wide, wide, turned, turned, sums, wide],
        out_shape=[
            shape_of((rows, width), f32),
            shape_of((rows, width), f32),
            shape_of((rows, width), bf16),
            shape_of((width, rows), bf16),
            shape_of((width, rows), bf16),
            shape_of((heads, 1, rows), f32),
            shape_of((rows, width), bf16),
        ],
        scratch_shapes=[pltpu.VMEM((width, width), bf16)]
        + [pltpu.VMEM(weights[2].shape, bf16)] * 2
        + [pltpu.SemaphoreType.DMA((2 * memory.shape[0] + 2,))],
        compiler_params=params(),
        cost_estimate=cost(11.3),
        name="local_forward",
    )(lengths, core, order, mixed, frames, norms, memory, *weights)


def local_backward_kernel(
    clip,
    n_ref,
    core_ref,
    order_ref,
    b_ref,
    cot_ref,
    first_ref,
    second_ref,
    q_ref,
    o_ref,
    l_ref,
    norm_ref,
    mem_ref,
    wo_mine,
    wo_other,
    cq_hbm,
    co_hbm,
    *refs,
):
    cross_ref, self_ref, one_ref, dq_ref, d_ref, g_ref, term_ref, grads_ref, wo, cq, co, sems = refs
    start_out, start_whole, get_out, get_whole = fetch(
        core_ref[0], (wo_mine, wo_other), wo, (cq_hbm, co_hbm), (cq, co), sems
    )
    start_whole(1)
    start_whole(0)
    start_out()
    groups, depth, slots = mem_ref.shape
    local = depth // 2
    heads = local // HEAD_DIM
    live = lax.broadcasted_iota(jnp.int32, (slots, 1), 0) < n_ref[clip]

    back = total([b_ref[k] for k in range(b_ref.shape[0])])
    _, normal, scale = norm_forward(second_ref[...], norm_ref[2:3], norm_ref[3:4])
    term_ref[2:3] = jnp.sum(back * normal, axis=0, keepdims=True)
    term_ref[3:4] = jnp.sum(back, axis=0, keepdims=True)
    grad_two = cot_ref[...].astype(f32) + norm_backward(back, normal, scale, norm_ref[2:3])
    cross_in = grad_two.astype(bf16)
    cross_ref[...] = cross_in
    weight = get_whole(1)
    for k in range(groups):
        grads_ref[k * local : (k + 1) * local] = dot(cross_in, weight[k], 1, 0).astype(bf16).T
    for group in range(groups):
        for head, part in enumerate(head_parts(local)):
            there = slice(group * local + part.start, group * local + part.stop)
            queries = q_ref[there]
            keys = mem_ref[order_ref[group], part]
            grads = grads_ref[there]
            mixsum = jnp.sum(o_ref[there].astype(f32) * grads.astype(f32), axis=0, keepdims=True)
            scores = jnp.where(live, dot(keys, queries, 0, 0), -1e30)
            probs = jnp.exp(scores - l_ref[group * heads + head])
            values = slice(local + part.start, local + part.stop)
            grad_probs = dot(mem_ref[order_ref[group], values], grads, 0, 0)
            grad_scores = (probs * (grad_probs - mixsum)).astype(bf16)
            dq_ref[there] = (dot(keys, grad_scores, 1, 0) * FACTOR).astype(bf16)
            d_ref[group, part] = dot(queries, grad_scores, 1, 1).astype(bf16)
            d_ref[group, values] = dot(grads, probs.astype(bf16), 1, 1).astype(bf16)
    weight = get_whole(0)
    back = jnp.zeros(grad_two.shape, f32)
    for k in range(groups):
        back = back + dot(dq_ref[k * local : (k + 1) * local], weight[k], 0, 1)
    _, normal, scale = norm_forward(first_ref[...], norm_ref[0:1], norm_ref[1:2])
    term_ref[0:1] = jnp.sum(back * normal, axis=0, keepdims=True)
    term_ref[1:2] = jnp.sum(back, axis=0, keepdims=True)
    grad_one = grad_two + norm_backward(back, normal, scale, norm_ref[0:1])
    one_ref[...] = grad_one
    self_in = grad_one.astype(bf16)
    self_ref[...] = self_in
    g_ref[...] = dot(get_out(), self_in, 1, 1).astype(bf16)


def local_backward(
    clip, count, lengths, core, order, back, cotangent, first, second, cross, norms, memory, weights
):
    rows, width = cotangent.shape
    wide, turned, sums, norm_spec, mem, heads = local_specs(clip, count, rows, width, memory)
    groups, depth, slots = memory.shape
    slots = slots // count
    return pl.pallas_call(
        functools.partial(local_backward_kernel, clip),
        grid=(1,),
        in_specs=[
            pl.BlockSpec(memory_space=pltpu.SMEM),
            pl.BlockSpec(memory_space=pltpu.SMEM),
            pl.BlockSpec(memory_space=pltpu.SMEM),
            pl.BlockSpec(back.shape, lambda i: (0, 0, 0)),
            wide,
            wide,
            wide,
            turned,
            turned,
            sums,
            norm_spec,
            mem,
        ]
        + [pl.BlockSpec(memory_space=pl.ANY)] * 4,
        out_specs=[
            wide,
            wide,
            wide,
            turned,
            pl.BlockSpec((groups, depth, slots), lambda i: (0, 0, 0)),
            turned,
            norm_spec,
        ],
        out_shape=[
            shape_of((rows, width), bf16),
            shape_of((rows, width), bf16),
            shape_of((rows, width), f32),
            shape_of((width, rows), bf16),
            shape_of((groups, depth, slots), bf16),
            shape_of((width, rows), bf16),
            shape_of((4, width), f32),
        ],
        scratch_shapes=[pltpu.VMEM((width, rows), bf16)]
        + [pltpu.VMEM((width, width), bf16)]
        + [pltpu.VMEM(weights[2].shape, bf16)] * 2
        + [pltpu.SemaphoreType.DMA((2 * groups + 2,))],
        compiler_params=params(),
        cost_estimate=cost(5),
        name="local_backward",
    )(lengths, core, order, back, cotangent, first, second, *cross, norms, memory, *weights)


def cost(micros):
    micros = 0.4 * micros
    return pl.CostEstimate(
        flops=int(micros * 1.15e9), bytes_accessed=int(micros * 3.6e6), transcendentals=0
    )


def shape_of(shape, kind):
    return jax.ShapeDtypeStruct(shape, kind)


def params():
    return pltpu.CompilerParams(vmem_limit_bytes=48 * 2**20)


def self_forward(turned, front_keys, front_values):
    size = lax.axis_size("mp")
    heads = front_keys.shape[0] // HEAD_DIM
    frames = turned.shape[1]
    step = 3 if heads % 3 == 0 else 1
    rows = step * HEAD_DIM
    steps = heads // step

    def at(third):
        return pl.BlockSpec((rows, frames), lambda h: (third * steps + h, 0))

    column = pl.BlockSpec((rows, 1), lambda h: (h, 0))
    return pl.pallas_call(
        self_forward_kernel,
        grid=(steps,),
        in_specs=[at(0), at(1), at(2), column, column],
        out_specs=[
            pl.BlockSpec((size, rows, frames // size), lambda h: (0, h, 0)),
            pl.BlockSpec((step, 1, frames), lambda h: (h, 0, 0)),
        ],
        out_shape=[
            shape_of((size, heads * HEAD_DIM, frames // size), bf16),
            shape_of((heads, 1, frames), f32),
        ],
        compiler_params=params(),
        cost_estimate=cost(8.7),
        name="self_forward",
    )(turned, turned, turned, front_keys, front_values)


def self_backward(turned, grads, mixed, logsum, front_keys, front_values, cosine, sine):
    heads = front_keys.shape[0] // HEAD_DIM
    frames = turned.shape[1]

    def at(third):
        return pl.BlockSpec((HEAD_DIM, frames), lambda h: (third * heads + h, 0))

    column = pl.BlockSpec((HEAD_DIM, 1), lambda h: (h, 0))
    size = lax.axis_size("mp")
    blocks = pl.BlockSpec((size, HEAD_DIM, frames // size), lambda h: (0, h, 0))
    angles = pl.BlockSpec((HALF, frames), lambda h: (0, 0))
    return pl.pallas_call(
        functools.partial(self_backward_kernel, min(256, frames)),
        grid=(heads,),
        in_specs=[
            at(0),
            at(1),
            at(2),
            blocks,
            blocks,
            pl.BlockSpec((1, 1, frames), lambda h: (h, 0, 0)),
            column,
            column,
            angles,
            angles,
        ],
        out_specs=[
            pl.BlockSpec((3, HEAD_DIM, frames), lambda h: (0, h, 0)),
            column,
            column,
        ],
        out_shape=[
            shape_of((3, heads * HEAD_DIM, frames), bf16),
            shape_of((heads * HEAD_DIM, 1), bf16),
            shape_of((heads * HEAD_DIM, 1), bf16),
        ],
        compiler_params=params(),
        cost_estimate=cost(18),
        name="self_backward",
    )(turned, turned, turned, grads, mixed, logsum, front_keys, front_values, cosine, sine)


def block_refs(refs, size):
    if len(refs) == size:
        return [[ref] for ref in refs]
    return [refs[0:1], refs[1:2], refs[2:3], refs[3:5]]


def block_value(refs):
    parts = [ref[...] for ref in refs]
    return parts[0] if len(parts) == 1 else jnp.concatenate(parts, axis=0)


def whole_specs(arrays):
    return [pl.BlockSpec(array.shape, lambda j, *_: (0, 0)) for array in arrays]


def project_kernel(
    size, given, heads, n_ref, p_ref, norm_ref, wq_ref, wk_ref, wv_ref, cos_ref, sin_ref, *refs
):
    d_ref, x_ref, front_ref, w_ref = refs[-4:]
    blocks = block_refs(refs[:given], size)
    local = heads * HEAD_DIM

    @pl.when(pl.program_id(0) == 0)
    def _():
        for third, ref in enumerate((wq_ref, wk_ref, wv_ref)):
            w_ref[third * local : (third + 1) * local] = ref[...].T
        prefix = norm_forward(p_ref[...], norm_ref[0:1], norm_ref[1:2])[0].astype(bf16)
        front_ref[...] = dot(w_ref[local:], prefix, 1, 1).astype(bf16)

    for k in range(size):

        @pl.when(pl.program_id(0) == k)
        def _(k=k):
            frames = block_value(blocks[k])
            x_ref[0] = frames
            raw = dot(w_ref[...], frames, 1, 1)
            cosine = cos_ref[...]
            sine = sin_ref[...]
            for head in range(2 * heads):
                at = head * HEAD_DIM
                upper = raw[at : at + HALF]
                lower = raw[at + HALF : at + HEAD_DIM]
                first = upper * cosine - lower * sine
                second = lower * cosine + upper * sine
                if head < heads:
                    first, second = first * FACTOR, second * FACTOR
                d_ref[at : at + HALF] = first.astype(bf16)
                d_ref[at + HALF : at + HEAD_DIM] = second.astype(bf16)
            d_ref[2 * local :] = raw[2 * local :].astype(bf16)


def project(clip, count, order, picked, norms, pieces, weights, cosine, sine, earlier):
    size = lax.axis_size("mp")
    width, local = weights[0].shape
    depth = 3 * local
    rows = pieces[0].shape[0]
    angles = pl.BlockSpec((HALF, rows), lambda k, n: (0, n[k]))
    return pl.pallas_call(
        functools.partial(project_kernel, size, len(pieces), local // HEAD_DIM),
        grid_spec=pltpu.PrefetchScalarGridSpec(
            num_scalar_prefetch=1,
            grid=(size,),
            in_specs=whole_specs([picked, norms] + weights)
            + [angles, angles]
            + whole_specs(pieces)
            + [pl.BlockSpec(memory_space=pl.ANY)] * len(earlier),
            out_specs=[
                pl.BlockSpec((depth, rows), lambda k, n: (0, n[k])),
                pl.BlockSpec((1, rows, width), lambda k, n: (clip, n[k], 0)),
                pl.BlockSpec((2 * local, picked.shape[0]), lambda k, n: (0, 0)),
            ],
            scratch_shapes=[pltpu.VMEM((depth, width), bf16)],
        ),
        out_shape=[
            shape_of((depth, size * rows), bf16),
            shape_of((count, size * rows, width), bf16),
            shape_of((2 * local, picked.shape[0]), bf16),
        ],
        input_output_aliases={8 + len(pieces): 1} if earlier else {},
        compiler_params=params(),
        cost_estimate=cost(8),
        name="project",
    )(order, picked, norms, *weights, cosine, sine, *pieces, *earlier)


def glu_kernel(size, given, n_ref, gate_ref, up_ref, down_ref, *refs):
    h_ref, dg_ref, du_ref, x_ref, c_ref = refs[-5:]
    blocks = block_refs(refs[:given], size)
    grads = block_refs(refs[given : 2 * given], size)
    rows = h_ref.shape[1] // size

    @pl.when(pl.program_id(0) == 0)
    def _():
        for k in range(size):
            there = pl.ds(pl.multiple_of(n_ref[k] * rows, rows), rows)
            x_ref[0, there] = block_value(blocks[k])
            c_ref[0, there] = block_value(grads[k])

    for k in range(size):
        frames = block_value(blocks[k])
        there = pl.ds(pl.multiple_of(n_ref[k] * rows, rows), rows)
        gate = dot(frames, gate_ref[...], 1, 0)
        upper = dot(frames, up_ref[...], 1, 0)
        grad_hidden = dot(block_value(grads[k]), down_ref[...], 1, 1)
        sigma = 1.0 / (1.0 + jnp.exp(-gate))
        silu = gate * sigma
        h_ref[0, there] = (silu * upper).astype(bf16)
        dg_ref[0, there] = (grad_hidden * upper * (sigma + silu * (1.0 - sigma))).astype(bf16)
        du_ref[0, there] = (grad_hidden * silu).astype(bf16)


def glu(clip, count, order, pieces, grads, w_gate, w_up, w_down, earlier):
    size = lax.axis_size("mp")
    width, hidden = w_gate.shape
    rows = size * pieces[0].shape[0]
    block = 256
    columns = pl.BlockSpec((width, block), lambda j: (0, j))
    out = pl.BlockSpec((1, rows, block), lambda j: (clip, 0, j))
    whole = pl.BlockSpec((1, rows, width), lambda j: (clip, 0, 0))
    return pl.pallas_call(
        functools.partial(glu_kernel, size, len(pieces)),
        grid=(hidden // block,),
        in_specs=[
            pl.BlockSpec(memory_space=pltpu.SMEM),
            columns,
            columns,
            pl.BlockSpec((block, width), lambda j: (j, 0)),
        ]
        + whole_specs(pieces)
        + whole_specs(grads)
        + [pl.BlockSpec(memory_space=pl.ANY)] * len(earlier),
        out_specs=[out, out, out, whole, whole],
        out_shape=[shape_of((count, rows, hidden), bf16)] * 3
        + [shape_of((count, rows, width), bf16)] * 2,
        input_output_aliases={4 + 2 * len(pieces) + i: i for i in range(len(earlier))},
        compiler_params=params(),
        cost_estimate=cost(22),
        name="glu",
    )(order, w_gate, w_up, w_down, *pieces, *grads, *earlier)


def glu_back_kernel(dg_ref, du_ref, gate_ref, up_ref, o_ref):
    size, rows, _ = o_ref.shape
    for k in range(size):
        part = slice(k * rows, (k + 1) * rows)
        back = dot(dg_ref[0, part], gate_ref[...], 1, 1) + dot(du_ref[0, part], up_ref[...], 1, 1)
        o_ref[k] = back.astype(bf16)


def glu_back(clip, grad_gate, grad_upper, w_gate, w_up):
    size = lax.axis_size("mp")
    _, frames, hidden = grad_gate.shape
    rows = frames // size
    width = w_gate.shape[0]
    block = 256
    whole = pl.BlockSpec((1, frames, hidden), lambda j: (clip, 0, 0))
    part = pl.BlockSpec((block, hidden), lambda j: (j, 0))
    return pl.pallas_call(
        glu_back_kernel,
        grid=(width // block,),
        in_specs=[whole, whole, part, part],
        out_specs=pl.BlockSpec((size, rows, block), lambda j: (0, 0, j)),
        out_shape=shape_of((size, rows, width), bf16),
        compiler_params=params(),
        cost_estimate=cost(14.5),
        name="glu_back",
    )(grad_gate, grad_upper, w_gate, w_up)


def whole_grad_kernel(chips, n, count, given, core_ref, *refs):
    o_ref = refs[-2] if not given else refs[-1]
    turned_ref = refs[-1] if not given else refs[0]
    y_refs = refs[1:] if given else refs[n * count :]
    depth = o_ref.shape[3]

    if not given:

        @pl.when(pl.program_id(0) == 0)
        def _():
            for w in range(n):
                parts = [ref[...] for ref in refs[w * count : (w + 1) * count]]
                turned_ref[w] = jnp.concatenate(parts, axis=0).T

    for w in range(n):
        right = jnp.concatenate([ref[...] for ref in y_refs[w * count : (w + 1) * count]], axis=1)
        for z in range(chips):
            at = pl.multiple_of((2 * z + core_ref[0]) * depth, depth)
            result = dot(turned_ref[w, pl.ds(at, depth)], right, 1, 1)
            if given:
                result = result + refs[1 + n * count][0, z, w].astype(f32)
            o_ref[0, z, w] = result.astype(bf16)


def whole_grad(core, groups, lefts, rights, earlier):
    size = lax.axis_size("mp")
    n = len(rights)
    count = len(rights[0])
    rows = rights[0][0].shape[1]
    local = rights[0][0].shape[0] // size
    width = lefts.shape[1] if earlier else lefts[0][0].shape[1]
    chips = groups // 2
    depth = width // groups
    out = pl.BlockSpec((1, chips, n, depth, local), lambda m: (m, 0, 0, 0, 0))
    turned = pl.BlockSpec((n, width, count * rows), lambda m: (0, 0, 0))
    right = pl.BlockSpec((local, rows), lambda m: (m, 0))
    left = pl.BlockSpec((rows, width), lambda m: (0, 0))
    out_shape = shape_of((size, chips, n, depth, local), bf16)
    turned_shape = shape_of((n, width, count * rows), bf16)
    rights = [array for pair in rights for array in pair]
    lefts = [lefts] if earlier else [array for pair in lefts for array in pair]
    return pl.pallas_call(
        functools.partial(whole_grad_kernel, chips, n, count, len(earlier)),
        grid=(size,),
        in_specs=[pl.BlockSpec(memory_space=pltpu.SMEM)]
        + [turned if earlier else left] * len(lefts)
        + [right] * len(rights)
        + [out] * len(earlier),
        out_specs=out if earlier else [out, turned],
        out_shape=out_shape if earlier else [out_shape, turned_shape],
        compiler_params=params(),
        cost_estimate=cost(12),
        name="whole_grad",
    )(core, *lefts, *rights, *earlier)


def branch_kernel(x_ref, w_ref, o_ref):
    o_ref[0, 0] = dot(x_ref[0], w_ref[...], 1, 0).astype(bf16)


def branch_blocks(hidden, w_down):
    size = lax.axis_size("mp")
    count, frames, depth = hidden.shape
    width = w_down.shape[1]
    rows = frames // size
    return pl.pallas_call(
        branch_kernel,
        grid=(count, size),
        in_specs=[
            pl.BlockSpec((1, rows, depth), lambda b, k: (b, k, 0)),
            pl.BlockSpec((depth, width), lambda b, k: (0, 0)),
        ],
        out_specs=pl.BlockSpec((1, 1, rows, width), lambda b, k: (k, b, 0, 0)),
        out_shape=shape_of((size, count, rows, width), bf16),
        compiler_params=params(),
        cost_estimate=cost(13.2),
        name="branch",
    )(hidden, w_down)


def weight_grad_kernel(x_ref, g_ref, o_ref):
    o_ref[...] = dot(x_ref[...], g_ref[...], 0, 0).astype(bf16)


def weight_grad(frames, grads):
    frames = frames.reshape(-1, frames.shape[-1])
    grads = grads.reshape(-1, grads.shape[-1])
    rows, width = frames.shape
    hidden = grads.shape[1]
    block = 256
    return pl.pallas_call(
        weight_grad_kernel,
        grid=(width // block,),
        in_specs=[
            pl.BlockSpec((rows, block), lambda i: (0, i)),
            pl.BlockSpec((rows, hidden), lambda i: (0, 0)),
        ],
        out_specs=pl.BlockSpec((block, hidden), lambda i: (i, 0)),
        out_shape=shape_of((width, hidden), bf16),
        compiler_params=params(),
        cost_estimate=cost(10),
        name="weight_grad",
    )(frames, grads)


def self_weight_grad_kernel(count, x_ref, p_ref, f_ref, *refs):
    d_refs = refs[:count]
    w_refs = refs[count : count + 3]
    o_ref, gain_ref, shift_ref, sum_ref = refs[count + 3 :]
    local = w_refs[0].shape[1]

    @pl.when(pl.program_id(0) == 0)
    def _():
        ones = jnp.ones((8, x_ref.shape[1]), bf16)
        for third in range(3):
            part = slice(third * local, (third + 1) * local)
            sums = jnp.zeros((8, local), f32)
            for b in range(count):
                sums = sums + dot(ones, d_refs[b][third], 1, 1) + f_ref[b : b + 1, part]
            sum_ref[:, part] = sums

    gain = jnp.zeros(gain_ref.shape, f32)
    shift = jnp.zeros(shift_ref.shape, f32)
    result = jnp.zeros((x_ref.shape[2], 3 * local), f32)
    for b in range(count):
        grads = d_refs[b][...].reshape(3 * local, -1)
        result = result + dot(x_ref[b], grads, 0, 1) + p_ref[:, b : b + 1] * f_ref[b : b + 1]
    o_ref[...] = result.astype(bf16)
    for third in range(3):
        part = slice(third * local, (third + 1) * local)
        weight = w_refs[third][...].astype(f32)
        gain = gain + jnp.sum(weight * result[:, part], axis=1, keepdims=True)
        shift = shift + jnp.sum(weight * sum_ref[0:1, part], axis=1, keepdims=True)
    gain_ref[...] = gain
    shift_ref[...] = shift


def self_weight_grad(frames, prefix, grads, front, weights):
    count, rows, width = frames.shape
    local = grads[0].shape[1]
    depth = 3 * local
    block = 256
    weight = pl.BlockSpec((block, local), lambda i: (i, 0))
    column = pl.BlockSpec((block, 1), lambda i: (i, 0))
    return pl.pallas_call(
        functools.partial(self_weight_grad_kernel, count),
        grid=(width // block,),
        in_specs=[
            pl.BlockSpec((count, rows, block), lambda i: (0, 0, i)),
            pl.BlockSpec((block, count), lambda i: (i, 0)),
            pl.BlockSpec((count, depth), lambda i: (0, 0)),
        ]
        + [pl.BlockSpec((3, local, rows), lambda i: (0, 0, 0))] * count
        + [weight] * 3,
        out_specs=[pl.BlockSpec((block, depth), lambda i: (i, 0)), column, column],
        out_shape=[shape_of((width, depth), bf16)] + [shape_of((width, 1), f32)] * 2,
        scratch_shapes=[pltpu.VMEM((8, depth), f32)],
        compiler_params=params(),
        cost_estimate=cost(12),
        name="self_weight_grad",
    )(frames, prefix.T.astype(f32), front.astype(f32), *grads, *weights)


def self_back_kernel(d_ref, wq_ref, wk_ref, wv_ref, o_ref):
    local = wq_ref.shape[1]
    back = jnp.zeros(o_ref.shape[1:], f32)
    for third, ref in enumerate((wq_ref, wk_ref, wv_ref)):
        back = back + dot(d_ref[third], ref[...], 0, 1)
    o_ref[0] = back.astype(bf16)


def self_back(grads, weights):
    size = lax.axis_size("mp")
    _, local, frames = grads.shape
    width = weights[0].shape[0]
    rows = frames // size
    return pl.pallas_call(
        self_back_kernel,
        grid=(size,),
        in_specs=[pl.BlockSpec((3, local, rows), lambda k: (0, 0, k))] + whole_specs(weights),
        out_specs=pl.BlockSpec((1, rows, width), lambda k: (k, 0, 0)),
        out_shape=shape_of((size, rows, width), bf16),
        compiler_params=params(),
        cost_estimate=cost(7),
        name="self_back",
    )(grads, *weights)


def turning(frames):
    places = (jnp.arange(frames) + 1).astype(f32)
    rates = jnp.exp(jnp.arange(HALF).astype(f32) * (-2.0 * math.log(10000.0) / HEAD_DIM))
    angles = rates[:, None] * places[None, :]
    return (jnp.cos(angles), jnp.sin(angles))


def sum_over_clips(values, axis):
    return lax.psum_scatter(values.astype(bf16), "dp", scatter_dimension=axis, tiled=True)


def shards(
    frames_in,
    prompt,
    lengths,
    tsteps,
    table,
    gain_one,
    shift_one,
    gain_two,
    shift_two,
    gain_three,
    shift_three,
    w_query,
    w_key,
    w_value,
    w_out,
    c_query,
    c_key,
    c_value,
    c_out,
    w_gate,
    w_up,
    w_down,
    cotangent,
):
    size = lax.axis_size("mp")
    groups = lax.axis_size("dp")
    count, rows, width = frames_in.shape
    clips = range(count)
    local = w_query.shape[1]
    here = lax.axis_index("mp")
    there = lax.axis_index("dp")
    core = there & 1
    chain = Chain()
    hold, mark, arrive = chain.hold, chain.mark, chain.arrive

    def joined(parts, axis):
        return jnp.concatenate(parts, axis=axis)

    order = jnp.stack([here ^ k for k in range(size)]).astype(jnp.int32)
    this_core = jnp.stack([core]).astype(jnp.int32)
    depth = width // groups
    side = jnp.stack(
        [
            lax.dynamic_slice_in_dim(c_query, there * depth, depth, 0),
            lax.dynamic_slice_in_dim(c_out, there * depth, depth, 1).T,
        ]
    )
    side = lax.all_gather(side, "mp", axis=0)
    ones, low = [], []
    for b in clips:
        ones.append(norm_forward(hold(frames_in[b]).astype(f32), gain_one, shift_one))
        low.append(ones[b][0].astype(bf16))
        mark(low[b])
        if b == 0:
            spread_one = [Spread(low[0])]
            spread_one[0].first = arrive(spread_one[0].first)
            spread_one[0].second_step()
        else:
            spread_one.append(Spread(low[b]))
    tokens = prompt.reshape(-1, prompt.shape[-1])
    memory = [dot(hold(part), tokens, 0, 1).astype(bf16) for part in (c_key, c_value)]
    mark(*memory)
    memory = joined(memory, 0)
    side = arrive(side)
    c_query_all = lax.all_gather(side[:, 0], "dp", axis=1, tiled=True)
    c_out_all = lax.all_gather(side[:, 1], "dp", axis=1, tiled=True)
    cosine, sine = turning(size * rows)
    picked = [lax.dynamic_slice_in_dim(hold(table), tsteps[b], 1, 0) for b in clips]
    mark(*picked)
    picked = joined(picked + [jnp.ones((8 - count, width), f32)], 0)
    norm_one = jnp.stack([gain_one, shift_one])
    half = lax.dynamic_slice_in_dim(hold(w_out), core * (local // 2), local // 2, 0)
    mark(half)
    spread_one[0].last = arrive(spread_one[0].last)

    turned, mixed_part, logsum, mixed = [], [], [], []
    frames_one = ()
    weights = [w_query, w_key, w_value]
    for b in clips:
        if b:
            spread_one[b].last = arrive(spread_one[b].last)
        pieces = hold(spread_one[b].pieces())
        out, frames_one, front = project(
            b, count, order, picked, norm_one, pieces, weights, cosine, sine, list(frames_one)
        )
        frames_one = (frames_one,)
        turned.append(out)
        mark(out)
        if b == 0:
            front_keys = [front[:local, c : c + 1] for c in clips]
            front_values = [front[local:, c : c + 1] for c in clips]
            for later in spread_one[1:]:
                later.first = arrive(later.first)
                later.second_step()
            halves = gathered(hold(half))
        else:
            memory = hold(memory)
            memory = [memory] + [swap(memory, "mp", k) for k in range(1, size)]
            halves = arrive(halves)
            other = swap(halves, "dp", 1)
            mixed[0] = exchange(hold(mixed[0]))
        out, sums = self_forward(hold(turned[b]), front_keys[b], front_values[b])
        mixed_part.append(out)
        logsum.append(sums)
        mixed.append(out)
        mark(out)
    frames_one = frames_one[0]
    mixed[0] = arrive(mixed[0])
    for b in clips[1:]:
        mixed[b] = exchange(hold(mixed[b]))
    memory = jnp.stack(arrive(memory))
    mark(memory)
    spread_down = [Spread(hold(cotangent[0]))]
    other = arrive(other)
    local_weights = (halves, other, c_query_all, c_out_all)

    norms = jnp.stack([gain_two, shift_two, gain_three, shift_three])
    first, normed_two, cross, second, low, spread_three = [], [], [], [], [], []
    for b in clips:
        mixed[b] = hold(mixed[b]).reshape(size * local, rows)
        parts = local_forward(
            b, count, lengths, this_core, order, mixed[b], frames_in[b], norms, memory, local_weights
        )
        first.append(parts[0])
        second.append(parts[1])
        normed_two.append(parts[2])
        cross.append(parts[3:6])
        low.append(parts[6])
        mark(low[b])
        if b == 0:
            spread_three.append(Spread(low[b]))
            spread_down[0].first = arrive(spread_down[0].first)
            spread_down[0].second_step()

    back_three = []
    parts = ()
    spread_down[0].last = arrive(spread_down[0].last)
    spread_three[0].first = arrive(spread_three[0].first)
    spread_three[0].second_step()
    spread_three.extend(Spread(hold(later)) for later in low[1:])
    spread_three[0].last = arrive(spread_three[0].last)
    spread_down.extend(Spread(hold(later)) for later in cotangent[1:])
    for b in clips:
        pieces = hold(spread_three[b].pieces())
        parts = glu(
            b, count, order, pieces, spread_down[b].pieces(), w_gate, w_up, w_down, list(parts)
        )
        mark(parts[1])
        if b == 0:
            for later in spread_three[1:] + spread_down[1:]:
                later.first = arrive(later.first)
                later.second_step()
        grad_gate, grad_upper = hold((parts[1], parts[2]))
        back = glu_back(b, grad_gate, grad_upper, w_gate, w_up)
        mark(back)
        if b == 0:
            for later in spread_three[1:] + spread_down[1:]:
                later.last = arrive(later.last)
        else:
            back_three[b - 1] = arrive(back_three[b - 1])
        back_three.append(exchange(hold(back)))

    hidden, grad_gate, grad_upper, frames_three, down_in = parts
    raw_w_down = weight_grad(hold(down_in), hidden)
    grad_w_down = sum_over_clips(raw_w_down, 0)
    mark(raw_w_down)
    branch = branch_blocks(hold(hidden), w_down)
    mark(branch)
    branch = lax.psum_scatter(branch, "mp", scatter_dimension=0, tiled=True)[0]
    raw_w_gate = weight_grad(hold(frames_three), grad_gate)
    grad_w_gate = sum_over_clips(raw_w_gate, 0)
    mark(raw_w_gate)

    grad_one, cross_in, self_in = [], [], []
    grad_cross_query, grad_memory, grad_mixed, norm_terms = [], [], [], []
    for b in clips:
        if b:
            back_three[b] = arrive(back_three[b])
            grad_mixed[b - 1] = exchange(hold(grad_mixed[b - 1]))
        parts = local_backward(
            b,
            count,
            lengths,
            this_core,
            order,
            hold(back_three[b]),
            cotangent[b],
            first[b],
            second[b],
            cross[b],
            norms,
            memory,
            local_weights,
        )
        cross_in.append(parts[0])
        self_in.append(parts[1])
        grad_one.append(parts[2])
        grad_cross_query.append(parts[3])
        grad_memory.append(parts[4])
        norm_terms.append(parts[6])
        mark(parts[5])
        grad_mixed.append(parts[5].reshape(size, local, rows))
    for b in clips[:-1]:
        grad_mixed[b] = arrive(grad_mixed[b])
    grad_mixed[-1] = exchange(hold(grad_mixed[-1]))

    grad_memory = Settle(joined(hold(grad_memory), 2))
    mark(*grad_memory.mine)
    grad_memory = grad_memory.second_step()
    rights = (grad_cross_query, [part[1] for part in cross], mixed)
    other_raws, lefts = whole_grad(
        1 - this_core, groups, (normed_two, hold(cross_in), self_in), rights, []
    )
    mark(other_raws)
    other_raws = swap(other_raws, "dp", 1)
    raw_w_up = weight_grad(hold(frames_three), grad_upper)
    grad_w_up = sum_over_clips(raw_w_up, 0)
    mark(raw_w_up)
    raws = whole_grad(this_core, groups, lefts, rights, [arrive(other_raws)])
    mark(raws)
    raws = Settle(hold(raws).reshape(size, -1, local))
    mark(*raws.mine)
    raws.first_step()

    grad_self, grad_front, back_one = [], [], []
    for b in clips:
        grads, grad_front_key, grad_front_value = self_backward(
            turned[b],
            hold(grad_mixed[b]),
            mixed_part[b],
            logsum[b],
            front_keys[b],
            front_values[b],
            cosine,
            sine,
        )
        grad_self.append(grads)
        grad_front.append(joined([grad_front_key, grad_front_value], 0))
        mark(grads)
        if b + 1 < count:
            grad_mixed[b + 1] = arrive(grad_mixed[b + 1])
            raws.came = arrive(raws.came)
            raws.add()
            mark(*raws.mine)
            raws = raws.second_step()
            back = self_back(hold(grad_self[b]), weights)
            mark(back)
            back_one.append(exchange(hold(back)))
            grad_memory = total(arrive(grad_memory)).astype(bf16)
            low_memory = [
                dot(tokens, part, 0, 1).astype(bf16) for part in jnp.split(grad_memory, 2, axis=0)
            ]
            mark(*low_memory)
            low_memory = [part.reshape(groups, -1, local) for part in low_memory]
            mine, other = core_half(joined(low_memory, 1))

    raws = total(arrive(raws)).astype(bf16).reshape(groups // 2, 3, -1, local)
    memory_half = plus(mine, arrive(other))
    mark(raws, memory_half)
    raws = joined([raws, memory_half[:, None]], 1)
    cores = [list(range(c, groups, 2)) for c in range(2)]
    raws = lax.psum_scatter(raws, "dp", scatter_dimension=0, axis_index_groups=cores, tiled=True)[0]
    prefix_normed, prefix_normal, prefix_scale = norm_forward(
        picked[:count], gain_one, shift_one
    )
    prefix_low = prefix_normed.astype(bf16)
    grad_front = joined(grad_front, 1)
    wide_front = joined([jnp.zeros((count, local), bf16), grad_front.T], 1)
    low_w_self, gain_term, shift_term = self_weight_grad(
        frames_one, prefix_low, hold(grad_self), wide_front, weights
    )
    grad_w_self = sum_over_clips(low_w_self, 0)
    mark(low_w_self)
    back = self_back(hold(grad_self[-1]), weights)
    mark(back)
    back_one = arrive(back_one)
    back_one.append(exchange(hold(back)))

    def wide(value):
        return value.astype(f32)

    small = []
    gain_term, shift_term = gain_term[:, 0], shift_term[:, 0]
    small.append((gain_term - shift_one * shift_term) / gain_one)
    small.append(shift_term)
    norm_terms = sum(norm_terms[1:], norm_terms[0])
    steps = jnp.where(here == 0, tsteps, 0).astype(f32)
    steps = lax.dynamic_update_slice(jnp.zeros((width,), f32), steps, (there * count,))

    back_prefix = dot(grad_front[:local], w_key, 0, 1) + dot(grad_front[local:], w_value, 0, 1)
    grad_picked = norm_backward(back_prefix, prefix_normal, prefix_scale, gain_one)
    spots = jnp.arange(groups)[:, None, None] == there
    spots = jnp.where(spots, grad_picked[None], 0.0).reshape(groups * count, width)
    small = hold(joined([jnp.stack(small), norm_terms, steps[None], spots], 0))
    small = all_sum(small)
    all_steps = small[6, : groups * count]
    matches = jnp.arange(table.shape[0])[:, None].astype(f32) == all_steps[None, :]
    grad_table = jnp.dot(matches.astype(f32), small[7:], precision=lax.Precision.HIGHEST)

    mark(small)
    back_one[-1] = arrive(back_one[-1])
    back_one = [total(terms) for terms in back_one]
    grad_frames = [
        grad_one[b] + norm_backward(back_one[b], ones[b][1], ones[b][2], gain_one) for b in clips
    ]
    mark(grad_table, *grad_frames)
    grad_w_down = wide(arrive(grad_w_down).T)
    branch = arrive(branch)
    output = [second[b] + branch[b].astype(f32) for b in clips]
    grad_w_gate = wide(arrive(grad_w_gate))
    grad_w_up = arrive(grad_w_up)
    raws = arrive(raws).astype(f32)
    grad_w_self = arrive(grad_w_self)

    depth_c = prompt.shape[-1] // groups

    return (
        jnp.stack(output),
        jnp.stack(grad_frames),
        grad_table,
        small[0],
        small[1],
        small[2],
        small[3],
        small[4],
        small[5],
        wide(grad_w_self[:, :local]),
        wide(grad_w_self[:, local : 2 * local]),
        wide(grad_w_self[:, 2 * local :]),
        raws[2].T,
        raws[0],
        raws[3, :depth_c],
        raws[3, depth_c:],
        raws[1].T,
        grad_w_gate,
        wide(grad_w_up),
        grad_w_down,
    )


def solution(mesh):
    placed = (
        P("dp", "mp", None),
        P("dp", None, None),
        P("dp"),
        P("dp"),
        P(),
        P(),
        P(),
        P(),
        P(),
        P(),
        P(),
        P(None, "mp"),
        P(None, "mp"),
        P(None, "mp"),
        P("mp", None),
        P(None, "mp"),
        P(None, "mp"),
        P(None, "mp"),
        P("mp", None),
        P(None, "mp"),
        P(None, "mp"),
        P("mp", None),
        P("dp", "mp", None),
    )
    return jax.shard_map(
        shards,
        mesh=mesh,
        in_specs=placed,
        out_specs=(
            P("dp", "mp", None),
            P("dp", "mp", None),
            P(),
            P(),
            P(),
            P(),
            P(),
            P(),
            P(),
            P("dp", "mp"),
            P("dp", "mp"),
            P("dp", "mp"),
            P("mp", "dp"),
            P("dp", "mp"),
            P("dp", "mp"),
            P("dp", "mp"),
            P("mp", "dp"),
            P("dp", "mp"),
            P("dp", "mp"),
            P("mp", "dp"),
        ),
        check_vma=False,
    )
```

```python
import functools
import math

import jax
import jax.numpy as jnp
from jax import lax
from jax.experimental import pallas as pl
from jax.experimental.pallas import tpu as pltpu
from jax.sharding import PartitionSpec as P

HEAD_DIM = 64
HALF = HEAD_DIM // 2
FACTOR = 1.0 / math.sqrt(HEAD_DIM)

norm_eps = 1e-05

f32 = jnp.float32
bf16 = jnp.bfloat16


def dot(left, right, left_axis, right_axis):
    return lax.dot_general(
        left, right, (((left_axis,), (right_axis,)), ((), ())), preferred_element_type=f32
    )


def norm_forward(values, gain, shift):
    center = values - jnp.mean(values, axis=-1, keepdims=True)
    scale = lax.rsqrt(jnp.mean(center * center, axis=-1, keepdims=True) + norm_eps)
    normal = center * scale
    return (normal * gain + shift, normal, scale)


def norm_backward(grad, normal, scale, gain):
    inner = grad * gain
    return scale * (
        inner
        - jnp.mean(inner, axis=-1, keepdims=True)
        - normal * jnp.mean(inner * normal, axis=-1, keepdims=True)
    )


def bits_of(size):
    return [1 << place for place in range(size.bit_length() - 1)]


def swap(values, axis, k):
    return lax.ppermute(values, axis, [(i, i ^ k) for i in range(lax.axis_size(axis))])


def after(values, *others):
    return lax.optimization_barrier((values,) + others)[0]


class Spread:
    def __init__(self, values):
        self.values = values
        self.last = ()
        size = lax.axis_size("mp")
        partners = (1, 2) if size == 4 else range(1, size)
        self.first = tuple(swap(values, "mp", k) for k in partners)

    def second_step(self):
        if lax.axis_size("mp") == 4:
            one, two = self.first
            half = one.shape[0] // 2
            self.last = (swap(one[:half], "mp", 2), swap(two[half:], "mp", 1))

    def pieces(self):
        return [self.values, *self.first, *self.last]


def place(blocks, axis):
    here = lax.axis_index("mp")
    step = blocks[0].shape[axis]
    shape = list(blocks[0].shape)
    shape[axis] = step * len(blocks)
    result = jnp.zeros(shape, blocks[0].dtype)
    for k, block in enumerate(blocks):
        result = lax.dynamic_update_slice_in_dim(result, block, (here ^ k) * step, axis)
    return result


def gathered(values):
    return exchange(jnp.broadcast_to(values[None], (lax.axis_size("mp"),) + values.shape))


def exchange(blocks):
    return lax.all_to_all(blocks, "mp", 0, 0)


class Settle:
    def __init__(self, blocks):
        here = lax.axis_index("mp")
        size = blocks.shape[0]
        self.mine = [lax.dynamic_index_in_dim(blocks, here ^ k, 0, False) for k in range(size)]
        self.came = ()

    def first_step(self):
        if len(self.mine) == 4:
            half = self.mine[3].shape[0] // 2
            self.came = (swap(self.mine[3][:half], "mp", 2), swap(self.mine[3][half:], "mp", 1))

    def add(self):
        if len(self.mine) == 4:
            _, one, two, _ = self.mine
            high, low = self.came
            half = high.shape[0]
            one = jnp.concatenate([plus(one[:half], high), one[half:]], axis=0)
            two = jnp.concatenate([two[:half], plus(two[half:], low)], axis=0)
            self.mine = [self.mine[0], one, two]

    def second_step(self):
        return [self.mine[0]] + [swap(self.mine[k], "mp", k) for k in range(1, len(self.mine))]


def plus(left, right):
    return (left.astype(f32) + right.astype(f32)).astype(bf16)


def total(terms):
    result = terms[0].astype(f32)
    for k in range(1, len(terms)):
        result = result + terms[k].astype(f32)
    return result


def all_sum(values):
    for axis in ("dp", "mp"):
        for bit in bits_of(lax.axis_size(axis)):
            values = values + swap(values, axis, bit)
    return values


def core_half(blocks):
    core = lax.axis_index("dp") & 1
    pairs = blocks.reshape((blocks.shape[0] // 2, 2) + blocks.shape[1:])
    mine = lax.dynamic_index_in_dim(pairs, core, 1, False)
    other = lax.dynamic_index_in_dim(pairs, 1 - core, 1, False)
    return (mine, swap(other, "dp", 1))


class Chain:
    def __init__(self):
        self.last = ()

    def hold(self, values):
        return after(values, *self.last) if self.last else values

    def mark(self, *values):
        self.last = values

    def arrive(self, values):
        values = self.hold(values)
        self.mark(values)
        return values


def plus(left, right):
    return (left.astype(f32) + right.astype(f32)).astype(bf16)


def total(terms):
    result = terms[0].astype(f32)
    for term in terms[1:]:
        result = result + term.astype(f32)
    return result


def all_sum(values):
    for axis in ("dp", "mp"):
        for bit in bits_of(lax.axis_size(axis)):
            values = values + swap(values, axis, bit)
    return values


def core_half(blocks):
    core = lax.axis_index("dp") & 1
    pairs = blocks.reshape((blocks.shape[0] // 2, 2) + blocks.shape[1:])
    mine = lax.dynamic_index_in_dim(pairs, core, 1, False)
    other = lax.dynamic_index_in_dim(pairs, 1 - core, 1, False)
    return (mine, swap(other, "dp", 1))


def chips_sum(blocks):
    here = lax.axis_index("dp") >> 1
    mine = [
        lax.dynamic_index_in_dim(blocks, here ^ k, 0, False) for k in range(blocks.shape[0])
    ]
    return total([mine[0]] + [swap(mine[k], "dp", 2 * k) for k in range(1, len(mine))])


def self_forward_kernel(q_ref, k_ref, v_ref, pk_ref, pv_ref, o_ref, l_ref):
    parts = head_parts(q_ref.shape[0])
    scores = [dot(k_ref[part], q_ref[part], 0, 0) for part in parts]
    for head, part in enumerate(parts):
        front = q_ref[part].astype(f32) * pk_ref[part].astype(f32)
        front = jnp.sum(front, axis=0, keepdims=True)
        top = jnp.maximum(jnp.max(scores[head], axis=0, keepdims=True), front)
        weights = jnp.exp(scores[head] - top)
        front_weight = jnp.exp(front - top)
        total = jnp.sum(weights, axis=0, keepdims=True) + front_weight
        mixed = dot(v_ref[part], weights.astype(bf16), 1, 0)
        mixed = mixed + pv_ref[part].astype(f32) * front_weight.astype(bf16).astype(f32)
        mixed = (mixed * (1.0 / total)).astype(bf16)
        frames = o_ref.shape[2]
        for k in range(o_ref.shape[0]):
            o_ref[k, part] = mixed[:, k * frames : (k + 1) * frames]
        l_ref[head] = top + jnp.log(total)


def self_backward_kernel(
    block,
    q_ref,
    k_ref,
    v_ref,
    g_ref,
    o_ref,
    l_ref,
    pk_ref,
    pv_ref,
    cos_ref,
    sin_ref,
    d_ref,
    dpk_ref,
    dpv_ref,
):
    frames = q_ref.shape[1]
    keys = k_ref[...]
    values = v_ref[...]
    front_key = pk_ref[...].astype(f32)
    front_value = pv_ref[...].astype(f32)
    grad_keys = jnp.zeros((HEAD_DIM, frames), f32)
    grad_values = jnp.zeros((HEAD_DIM, frames), f32)
    grad_front_key = jnp.zeros((HEAD_DIM, 1), f32)
    grad_front_value = jnp.zeros((HEAD_DIM, 1), f32)
    whole_grads = jnp.concatenate([g_ref[k] for k in range(g_ref.shape[0])], axis=1)
    whole_mixed = jnp.concatenate([o_ref[k] for k in range(o_ref.shape[0])], axis=1)
    for start in range(0, frames, block):
        part = slice(start, start + block)
        queries = q_ref[:, part]
        grads = whole_grads[:, part]
        wide_queries = queries.astype(f32)
        wide_grads = grads.astype(f32)
        logsum = l_ref[0, :, part]
        mixsum = jnp.sum(whole_mixed[:, part].astype(f32) * wide_grads, axis=0, keepdims=True)
        probs = jnp.exp(dot(keys, queries, 0, 0) - logsum)
        grad_probs = dot(values, grads, 0, 0)
        grad_scores = (probs * (grad_probs - mixsum)).astype(bf16)
        grad_values = grad_values + dot(grads, probs.astype(bf16), 1, 1)
        grad_keys = grad_keys + dot(queries, grad_scores, 1, 1)
        grad_queries = dot(keys, grad_scores, 1, 0)
        front = jnp.exp(jnp.sum(wide_queries * front_key, axis=0, keepdims=True) - logsum)
        grad_front = jnp.sum(wide_grads * front_value, axis=0, keepdims=True)
        grad_front = (front * (grad_front - mixsum)).astype(bf16).astype(f32)
        front = front.astype(bf16).astype(f32)
        grad_front_key += jnp.sum(wide_queries * grad_front, axis=1, keepdims=True)
        grad_front_value += jnp.sum(wide_grads * front, axis=1, keepdims=True)
        grad_queries = (grad_queries + front_key * grad_front) * FACTOR
        cosine = cos_ref[:, part]
        sine = sin_ref[:, part]
        upper, lower = grad_queries[:HALF], grad_queries[HALF:]
        d_ref[0, :HALF, part] = (upper * cosine + lower * sine).astype(bf16)
        d_ref[0, HALF:, part] = (lower * cosine - upper * sine).astype(bf16)
    cosine = cos_ref[...]
    sine = sin_ref[...]
    upper, lower = grad_keys[:HALF], grad_keys[HALF:]
    d_ref[1, :HALF, :] = (upper * cosine + lower * sine).astype(bf16)
    d_ref[1, HALF:, :] = (lower * cosine - upper * sine).astype(bf16)
    d_ref[2] = grad_values.astype(bf16)
    dpk_ref[...] = grad_front_key.astype(bf16)
    dpv_ref[...] = grad_front_value.astype(bf16)


def head_parts(rows):
    return [slice(at, at + HEAD_DIM) for at in range(0, rows, HEAD_DIM)]


def fetch(core, out_halves, out, wholes, targets, sems):
    mine, other = out_halves
    size, half, _ = mine.shape
    copies = []
    for k in range(size):
        for source, part in ((mine, core), (other, 1 - core)):
            at = pl.multiple_of((2 * k + part) * half, 16)
            target = out.at[pl.ds(at, half)]
            copies.append(pltpu.make_async_copy(source.at[k], target, sems.at[len(copies)]))
    first = len(copies)
    for source, target in zip(wholes, targets):
        copies.append(pltpu.make_async_copy(source, target, sems.at[len(copies)]))

    def start_out():
        for copy in copies[:first]:
            copy.start()

    def start_whole(k):
        copies[first + k].start()

    def get_out():
        for copy in copies[:first]:
            copy.wait()
        return out[...]

    def get_whole(k):
        copies[first + k].wait()
        return targets[k]

    return start_out, start_whole, get_out, get_whole


def local_forward_kernel(
    clip, n_ref, core_ref, order_ref, mixed_ref, x_ref, norm_ref, mem_ref, wo_mine, wo_other, cq_hbm, co_hbm, *refs
):
    first_ref, second_ref, two_ref, q_ref, o_ref, l_ref, three_ref, wo, cq, co, sems = refs
    start_out, start_whole, get_out, get_whole = fetch(
        core_ref[0], (wo_mine, wo_other), wo, (cq_hbm, co_hbm), (cq, co), sems
    )
    start_out()
    start_whole(0)
    start_whole(1)
    groups, depth, slots = mem_ref.shape
    local = depth // 2
    live = lax.broadcasted_iota(jnp.int32, (slots, 1), 0) < n_ref[clip]
    first = x_ref[...].astype(f32) + dot(mixed_ref[...], get_out(), 0, 0)
    first_ref[...] = first
    two = norm_forward(first, norm_ref[0:1], norm_ref[1:2])[0].astype(bf16)
    two_ref[...] = two
    weight = get_whole(0)
    for k in range(groups):
        q_ref[k * local : (k + 1) * local] = (dot(two, weight[k], 1, 0) * FACTOR).astype(bf16).T
    for group in range(groups):
        parts = head_parts(local)
        there = order_ref[group]
        at = group * local
        queries = [q_ref[at + p.start : at + p.stop] for p in parts]
        scores = [dot(mem_ref[there, p], q, 0, 0) for p, q in zip(parts, queries)]
        scores = [jnp.where(live, s, -1e30) for s in scores]
        tops = [jnp.max(s, axis=0, keepdims=True) for s in scores]
        weights = [jnp.exp(s - top) for s, top in zip(scores, tops)]
        totals = [jnp.sum(w, axis=0, keepdims=True) for w in weights]
        for head, p in enumerate(parts):
            values = mem_ref[there, local + p.start : local + p.stop]
            mixed = dot(values, weights[head].astype(bf16), 1, 0)
            o_ref[at + p.start : at + p.stop] = (mixed * (1.0 / totals[head])).astype(bf16)
            l_ref[group * len(parts) + head] = tops[head] + jnp.log(totals[head])
    weight = get_whole(1)
    second = first
    for k in range(groups):
        second = second + dot(o_ref[k * local : (k + 1) * local], weight[k], 0, 1)
    second_ref[...] = second
    three_ref[...] = norm_forward(second, norm_ref[2:3], norm_ref[3:4])[0].astype(bf16)


def local_specs(clip, count, rows, width, memory):
    groups, depth, slots = memory.shape
    heads = groups * depth // 2 // HEAD_DIM
    wide = pl.BlockSpec((rows, width), lambda i: (0, 0))
    turned = pl.BlockSpec((width, rows), lambda i: (0, 0))
    sums = pl.BlockSpec((heads, 1, rows), lambda i: (0, 0, 0))
    norms = pl.BlockSpec((4, width), lambda i: (0, 0))
    mem = pl.BlockSpec((groups, depth, slots // count), lambda i: (0, 0, clip))
    return (wide, turned, sums, norms, mem, heads)


def local_forward(clip, count, lengths, core, order, mixed, frames, norms, memory, weights):
    rows, width = frames.shape
    wide, turned, sums, norm_spec, mem, heads = local_specs(clip, count, rows, width, memory)
    return pl.pallas_call(
        functools.partial(local_forward_kernel, clip),
        grid=(1,),
        in_specs=[pl.BlockSpec(memory_space=pltpu.SMEM)] * 3
        + [turned, wide, norm_spec, mem]
        + [pl.BlockSpec(memory_space=pl.ANY)] * 4,
        out_specs=[wide, wide, wide, turned, turned, sums, wide],
        out_shape=[
            shape_of((rows, width), f32),
            shape_of((rows, width), f32),
            shape_of((rows, width), bf16),
            shape_of((width, rows), bf16),
            shape_of((width, rows), bf16),
            shape_of((heads, 1, rows), f32),
            shape_of((rows, width), bf16),
        ],
        scratch_shapes=[pltpu.VMEM((width, width), bf16)]
        + [pltpu.VMEM(weights[2].shape, bf16)] * 2
        + [pltpu.SemaphoreType.DMA((2 * memory.shape[0] + 2,))],
        compiler_params=params(),
        cost_estimate=cost(11.3),
        name="local_forward",
    )(lengths, core, order, mixed, frames, norms, memory, *weights)


def local_backward_kernel(
    clip,
    n_ref,
    core_ref,
    order_ref,
    b_ref,
    cot_ref,
    first_ref,
    second_ref,
    q_ref,
    o_ref,
    l_ref,
    norm_ref,
    mem_ref,
    wo_mine,
    wo_other,
    cq_hbm,
    co_hbm,
    *refs,
):
    cross_ref, self_ref, one_ref, dq_ref, d_ref, g_ref, term_ref, grads_ref, wo, cq, co, sems = refs
    start_out, start_whole, get_out, get_whole = fetch(
        core_ref[0], (wo_mine, wo_other), wo, (cq_hbm, co_hbm), (cq, co), sems
    )
    start_whole(1)
    start_whole(0)
    start_out()
    groups, depth, slots = mem_ref.shape
    local = depth // 2
    heads = local // HEAD_DIM
    live = lax.broadcasted_iota(jnp.int32, (slots, 1), 0) < n_ref[clip]

    back = total([b_ref[k] for k in range(b_ref.shape[0])])
    _, normal, scale = norm_forward(second_ref[...], norm_ref[2:3], norm_ref[3:4])
    term_ref[2:3] = jnp.sum(back * normal, axis=0, keepdims=True)
    term_ref[3:4] = jnp.sum(back, axis=0, keepdims=True)
    grad_two = cot_ref[...].astype(f32) + norm_backward(back, normal, scale, norm_ref[2:3])
    cross_in = grad_two.astype(bf16)
    cross_ref[...] = cross_in
    weight = get_whole(1)
    for k in range(groups):
        grads_ref[k * local : (k + 1) * local] = dot(cross_in, weight[k], 1, 0).astype(bf16).T
    for group in range(groups):
        for head, part in enumerate(head_parts(local)):
            there = slice(group * local + part.start, group * local + part.stop)
            queries = q_ref[there]
            keys = mem_ref[order_ref[group], part]
            grads = grads_ref[there]
            mixsum = jnp.sum(o_ref[there].astype(f32) * grads.astype(f32), axis=0, keepdims=True)
            scores = jnp.where(live, dot(keys, queries, 0, 0), -1e30)
            probs = jnp.exp(scores - l_ref[group * heads + head])
            values = slice(local + part.start, local + part.stop)
            grad_probs = dot(mem_ref[order_ref[group], values], grads, 0, 0)
            grad_scores = (probs * (grad_probs - mixsum)).astype(bf16)
            dq_ref[there] = (dot(keys, grad_scores, 1, 0) * FACTOR).astype(bf16)
            d_ref[group, part] = dot(queries, grad_scores, 1, 1).astype(bf16)
            d_ref[group, values] = dot(grads, probs.astype(bf16), 1, 1).astype(bf16)
    weight = get_whole(0)
    back = jnp.zeros(grad_two.shape, f32)
    for k in range(groups):
        back = back + dot(dq_ref[k * local : (k + 1) * local], weight[k], 0, 1)
    _, normal, scale = norm_forward(first_ref[...], norm_ref[0:1], norm_ref[1:2])
    term_ref[0:1] = jnp.sum(back * normal, axis=0, keepdims=True)
    term_ref[1:2] = jnp.sum(back, axis=0, keepdims=True)
    grad_one = grad_two + norm_backward(back, normal, scale, norm_ref[0:1])
    one_ref[...] = grad_one
    self_in = grad_one.astype(bf16)
    self_ref[...] = self_in
    g_ref[...] = dot(get_out(), self_in, 1, 1).astype(bf16)


def local_backward(
    clip, count, lengths, core, order, back, cotangent, first, second, cross, norms, memory, weights
):
    rows, width = cotangent.shape
    wide, turned, sums, norm_spec, mem, heads = local_specs(clip, count, rows, width, memory)
    groups, depth, slots = memory.shape
    slots = slots // count
    return pl.pallas_call(
        functools.partial(local_backward_kernel, clip),
        grid=(1,),
        in_specs=[
            pl.BlockSpec(memory_space=pltpu.SMEM),
            pl.BlockSpec(memory_space=pltpu.SMEM),
            pl.BlockSpec(memory_space=pltpu.SMEM),
            pl.BlockSpec(back.shape, lambda i: (0, 0, 0)),
            wide,
            wide,
            wide,
            turned,
            turned,
            sums,
            norm_spec,
            mem,
        ]
        + [pl.BlockSpec(memory_space=pl.ANY)] * 4,
        out_specs=[
            wide,
            wide,
            wide,
            turned,
            pl.BlockSpec((groups, depth, slots), lambda i: (0, 0, 0)),
            turned,
            norm_spec,
        ],
        out_shape=[
            shape_of((rows, width), bf16),
            shape_of((rows, width), bf16),
            shape_of((rows, width), f32),
            shape_of((width, rows), bf16),
            shape_of((groups, depth, slots), bf16),
            shape_of((width, rows), bf16),
            shape_of((4, width), f32),
        ],
        scratch_shapes=[pltpu.VMEM((width, rows), bf16)]
        + [pltpu.VMEM((width, width), bf16)]
        + [pltpu.VMEM(weights[2].shape, bf16)] * 2
        + [pltpu.SemaphoreType.DMA((2 * groups + 2,))],
        compiler_params=params(),
        cost_estimate=cost(40),
        name="local_backward",
    )(lengths, core, order, back, cotangent, first, second, *cross, norms, memory, *weights)


def cost(micros):
    micros = 0.4 * micros
    return pl.CostEstimate(
        flops=int(micros * 1.15e9), bytes_accessed=int(micros * 3.6e6), transcendentals=0
    )


def shape_of(shape, kind):
    return jax.ShapeDtypeStruct(shape, kind)


def params():
    return pltpu.CompilerParams(vmem_limit_bytes=48 * 2**20)


def self_forward(turned, front_keys, front_values):
    size = lax.axis_size("mp")
    heads = front_keys.shape[0] // HEAD_DIM
    frames = turned.shape[1]
    step = 3 if heads % 3 == 0 else 1
    rows = step * HEAD_DIM
    steps = heads // step

    def at(third):
        return pl.BlockSpec((rows, frames), lambda h: (third * steps + h, 0))

    column = pl.BlockSpec((rows, 1), lambda h: (h, 0))
    return pl.pallas_call(
        self_forward_kernel,
        grid=(steps,),
        in_specs=[at(0), at(1), at(2), column, column],
        out_specs=[
            pl.BlockSpec((size, rows, frames // size), lambda h: (0, h, 0)),
            pl.BlockSpec((step, 1, frames), lambda h: (h, 0, 0)),
        ],
        out_shape=[
            shape_of((size, heads * HEAD_DIM, frames // size), bf16),
            shape_of((heads, 1, frames), f32),
        ],
        compiler_params=params(),
        cost_estimate=cost(8.7),
        name="self_forward",
    )(turned, turned, turned, front_keys, front_values)


def self_backward(turned, grads, mixed, logsum, front_keys, front_values, cosine, sine):
    heads = front_keys.shape[0] // HEAD_DIM
    frames = turned.shape[1]

    def at(third):
        return pl.BlockSpec((HEAD_DIM, frames), lambda h: (third * heads + h, 0))

    column = pl.BlockSpec((HEAD_DIM, 1), lambda h: (h, 0))
    size = lax.axis_size("mp")
    blocks = pl.BlockSpec((size, HEAD_DIM, frames // size), lambda h: (0, h, 0))
    angles = pl.BlockSpec((HALF, frames), lambda h: (0, 0))
    return pl.pallas_call(
        functools.partial(self_backward_kernel, min(256, frames)),
        grid=(heads,),
        in_specs=[
            at(0),
            at(1),
            at(2),
            blocks,
            blocks,
            pl.BlockSpec((1, 1, frames), lambda h: (h, 0, 0)),
            column,
            column,
            angles,
            angles,
        ],
        out_specs=[
            pl.BlockSpec((3, HEAD_DIM, frames), lambda h: (0, h, 0)),
            column,
            column,
        ],
        out_shape=[
            shape_of((3, heads * HEAD_DIM, frames), bf16),
            shape_of((heads * HEAD_DIM, 1), bf16),
            shape_of((heads * HEAD_DIM, 1), bf16),
        ],
        compiler_params=params(),
        cost_estimate=cost(45),
        name="self_backward",
    )(turned, turned, turned, grads, mixed, logsum, front_keys, front_values, cosine, sine)


def block_refs(refs, size):
    if len(refs) == size:
        return [[ref] for ref in refs]
    return [refs[0:1], refs[1:2], refs[2:3], refs[3:5]]


def block_value(refs):
    parts = [ref[...] for ref in refs]
    return parts[0] if len(parts) == 1 else jnp.concatenate(parts, axis=0)


def whole_specs(arrays):
    return [pl.BlockSpec(array.shape, lambda j, *_: (0, 0)) for array in arrays]


def project_kernel(
    size, given, heads, n_ref, p_ref, norm_ref, wq_ref, wk_ref, wv_ref, cos_ref, sin_ref, *refs
):
    d_ref, x_ref, front_ref, w_ref = refs[-4:]
    blocks = block_refs(refs[:given], size)
    local = heads * HEAD_DIM

    @pl.when(pl.program_id(0) == 0)
    def _():
        for third, ref in enumerate((wq_ref, wk_ref, wv_ref)):
            w_ref[third * local : (third + 1) * local] = ref[...].T
        prefix = norm_forward(p_ref[...], norm_ref[0:1], norm_ref[1:2])[0].astype(bf16)
        front_ref[...] = dot(w_ref[local:], prefix, 1, 1).astype(bf16)

    for k in range(size):

        @pl.when(pl.program_id(0) == k)
        def _(k=k):
            frames = block_value(blocks[k])
            x_ref[0] = frames
            raw = dot(w_ref[...], frames, 1, 1)
            cosine = cos_ref[...]
            sine = sin_ref[...]
            for head in range(2 * heads):
                at = head * HEAD_DIM
                upper = raw[at : at + HALF]
                lower = raw[at + HALF : at + HEAD_DIM]
                first = upper * cosine - lower * sine
                second = lower * cosine + upper * sine
                if head < heads:
                    first, second = first * FACTOR, second * FACTOR
                d_ref[at : at + HALF] = first.astype(bf16)
                d_ref[at + HALF : at + HEAD_DIM] = second.astype(bf16)
            d_ref[2 * local :] = raw[2 * local :].astype(bf16)


def project(clip, count, order, picked, norms, pieces, weights, cosine, sine, earlier):
    size = lax.axis_size("mp")
    width, local = weights[0].shape
    depth = 3 * local
    rows = pieces[0].shape[0]
    angles = pl.BlockSpec((HALF, rows), lambda k, n: (0, n[k]))
    return pl.pallas_call(
        functools.partial(project_kernel, size, len(pieces), local // HEAD_DIM),
        grid_spec=pltpu.PrefetchScalarGridSpec(
            num_scalar_prefetch=1,
            grid=(size,),
            in_specs=whole_specs([picked, norms] + weights)
            + [angles, angles]
            + whole_specs(pieces)
            + [pl.BlockSpec(memory_space=pl.ANY)] * len(earlier),
            out_specs=[
                pl.BlockSpec((depth, rows), lambda k, n: (0, n[k])),
                pl.BlockSpec((1, rows, width), lambda k, n: (clip, n[k], 0)),
                pl.BlockSpec((2 * local, picked.shape[0]), lambda k, n: (0, 0)),
            ],
            scratch_shapes=[pltpu.VMEM((depth, width), bf16)],
        ),
        out_shape=[
            shape_of((depth, size * rows), bf16),
            shape_of((count, size * rows, width), bf16),
            shape_of((2 * local, picked.shape[0]), bf16),
        ],
        input_output_aliases={8 + len(pieces): 1} if earlier else {},
        compiler_params=params(),
        cost_estimate=cost(8),
        name="project",
    )(order, picked, norms, *weights, cosine, sine, *pieces, *earlier)


def glu_kernel(size, given, n_ref, gate_ref, up_ref, down_ref, *refs):
    h_ref, dg_ref, du_ref, x_ref, c_ref = refs[-5:]
    blocks = block_refs(refs[:given], size)
    grads = block_refs(refs[given : 2 * given], size)
    rows = h_ref.shape[1] // size

    @pl.when(pl.program_id(0) == 0)
    def _():
        for k in range(size):
            there = pl.ds(pl.multiple_of(n_ref[k] * rows, rows), rows)
            x_ref[0, there] = block_value(blocks[k])
            c_ref[0, there] = block_value(grads[k])

    for k in range(size):
        frames = block_value(blocks[k])
        there = pl.ds(pl.multiple_of(n_ref[k] * rows, rows), rows)
        gate = dot(frames, gate_ref[...], 1, 0)
        upper = dot(frames, up_ref[...], 1, 0)
        grad_hidden = dot(block_value(grads[k]), down_ref[...], 1, 1)
        sigma = 1.0 / (1.0 + jnp.exp(-gate))
        silu = gate * sigma
        h_ref[0, there] = (silu * upper).astype(bf16)
        dg_ref[0, there] = (grad_hidden * upper * (sigma + silu * (1.0 - sigma))).astype(bf16)
        du_ref[0, there] = (grad_hidden * silu).astype(bf16)


def glu(clip, count, order, pieces, grads, w_gate, w_up, w_down, earlier):
    size = lax.axis_size("mp")
    width, hidden = w_gate.shape
    rows = size * pieces[0].shape[0]
    block = 256
    columns = pl.BlockSpec((width, block), lambda j: (0, j))
    out = pl.BlockSpec((1, rows, block), lambda j: (clip, 0, j))
    whole = pl.BlockSpec((1, rows, width), lambda j: (clip, 0, 0))
    return pl.pallas_call(
        functools.partial(glu_kernel, size, len(pieces)),
        grid=(hidden // block,),
        in_specs=[
            pl.BlockSpec(memory_space=pltpu.SMEM),
            columns,
            columns,
            pl.BlockSpec((block, width), lambda j: (j, 0)),
        ]
        + whole_specs(pieces)
        + whole_specs(grads)
        + [pl.BlockSpec(memory_space=pl.ANY)] * len(earlier),
        out_specs=[out, out, out, whole, whole],
        out_shape=[shape_of((count, rows, hidden), bf16)] * 3
        + [shape_of((count, rows, width), bf16)] * 2,
        input_output_aliases={4 + 2 * len(pieces) + i: i for i in range(len(earlier))},
        compiler_params=params(),
        cost_estimate=cost(22),
        name="glu",
    )(order, w_gate, w_up, w_down, *pieces, *grads, *earlier)


def glu_back_kernel(dg_ref, du_ref, gate_ref, up_ref, o_ref):
    size, rows, _ = o_ref.shape
    for k in range(size):
        part = slice(k * rows, (k + 1) * rows)
        back = dot(dg_ref[0, part], gate_ref[...], 1, 1) + dot(du_ref[0, part], up_ref[...], 1, 1)
        o_ref[k] = back.astype(bf16)


def glu_back(clip, grad_gate, grad_upper, w_gate, w_up):
    size = lax.axis_size("mp")
    _, frames, hidden = grad_gate.shape
    rows = frames // size
    width = w_gate.shape[0]
    block = 256
    whole = pl.BlockSpec((1, frames, hidden), lambda j: (clip, 0, 0))
    part = pl.BlockSpec((block, hidden), lambda j: (j, 0))
    return pl.pallas_call(
        glu_back_kernel,
        grid=(width // block,),
        in_specs=[whole, whole, part, part],
        out_specs=pl.BlockSpec((size, rows, block), lambda j: (0, 0, j)),
        out_shape=shape_of((size, rows, width), bf16),
        compiler_params=params(),
        cost_estimate=cost(14.5),
        name="glu_back",
    )(grad_gate, grad_upper, w_gate, w_up)


def whole_grad_kernel(chips, n, count, given, core_ref, *refs):
    o_ref = refs[-2] if not given else refs[-1]
    turned_ref = refs[-1] if not given else refs[0]
    y_refs = refs[1:] if given else refs[n * count :]
    depth = o_ref.shape[3]

    if not given:

        @pl.when(pl.program_id(0) == 0)
        def _():
            for w in range(n):
                parts = [ref[...] for ref in refs[w * count : (w + 1) * count]]
                turned_ref[w] = jnp.concatenate(parts, axis=0).T

    for w in range(n):
        right = jnp.concatenate([ref[...] for ref in y_refs[w * count : (w + 1) * count]], axis=1)
        for z in range(chips):
            at = pl.multiple_of((2 * z + core_ref[0]) * depth, depth)
            result = dot(turned_ref[w, pl.ds(at, depth)], right, 1, 1)
            if given:
                result = result + refs[1 + n * count][0, z, w].astype(f32)
            o_ref[0, z, w] = result.astype(bf16)


def whole_grad(core, groups, lefts, rights, earlier):
    size = lax.axis_size("mp")
    n = len(rights)
    count = len(rights[0])
    rows = rights[0][0].shape[1]
    local = rights[0][0].shape[0] // size
    width = lefts.shape[1] if earlier else lefts[0][0].shape[1]
    chips = groups // 2
    depth = width // groups
    out = pl.BlockSpec((1, chips, n, depth, local), lambda m: (m, 0, 0, 0, 0))
    turned = pl.BlockSpec((n, width, count * rows), lambda m: (0, 0, 0))
    right = pl.BlockSpec((local, rows), lambda m: (m, 0))
    left = pl.BlockSpec((rows, width), lambda m: (0, 0))
    out_shape = shape_of((size, chips, n, depth, local), bf16)
    turned_shape = shape_of((n, width, count * rows), bf16)
    rights = [array for pair in rights for array in pair]
    lefts = [lefts] if earlier else [array for pair in lefts for array in pair]
    return pl.pallas_call(
        functools.partial(whole_grad_kernel, chips, n, count, len(earlier)),
        grid=(size,),
        in_specs=[pl.BlockSpec(memory_space=pltpu.SMEM)]
        + [turned if earlier else left] * len(lefts)
        + [right] * len(rights)
        + [out] * len(earlier),
        out_specs=out if earlier else [out, turned],
        out_shape=out_shape if earlier else [out_shape, turned_shape],
        compiler_params=params(),
        cost_estimate=cost(30),
        name="whole_grad",
    )(core, *lefts, *rights, *earlier)


def branch_kernel(x_ref, w_ref, o_ref):
    o_ref[0, 0] = dot(x_ref[0], w_ref[...], 1, 0).astype(bf16)


def branch_blocks(hidden, w_down):
    size = lax.axis_size("mp")
    count, frames, depth = hidden.shape
    width = w_down.shape[1]
    rows = frames // size
    return pl.pallas_call(
        branch_kernel,
        grid=(count, size),
        in_specs=[
            pl.BlockSpec((1, rows, depth), lambda b, k: (b, k, 0)),
            pl.BlockSpec((depth, width), lambda b, k: (0, 0)),
        ],
        out_specs=pl.BlockSpec((1, 1, rows, width), lambda b, k: (k, b, 0, 0)),
        out_shape=shape_of((size, count, rows, width), bf16),
        compiler_params=params(),
        cost_estimate=cost(13.2),
        name="branch",
    )(hidden, w_down)


def weight_grad_kernel(x_ref, g_ref, o_ref):
    o_ref[...] = dot(x_ref[...], g_ref[...], 0, 0).astype(bf16)


def weight_grad(frames, grads):
    frames = frames.reshape(-1, frames.shape[-1])
    grads = grads.reshape(-1, grads.shape[-1])
    rows, width = frames.shape
    hidden = grads.shape[1]
    block = 256
    return pl.pallas_call(
        weight_grad_kernel,
        grid=(width // block,),
        in_specs=[
            pl.BlockSpec((rows, block), lambda i: (0, i)),
            pl.BlockSpec((rows, hidden), lambda i: (0, 0)),
        ],
        out_specs=pl.BlockSpec((block, hidden), lambda i: (i, 0)),
        out_shape=shape_of((width, hidden), bf16),
        compiler_params=params(),
        cost_estimate=cost(10),
        name="weight_grad",
    )(frames, grads)


def self_weight_grad_kernel(count, x_ref, p_ref, f_ref, *refs):
    d_refs = refs[:count]
    w_refs = refs[count : count + 3]
    o_ref, gain_ref, shift_ref, sum_ref = refs[count + 3 :]
    local = w_refs[0].shape[1]

    @pl.when(pl.program_id(0) == 0)
    def _():
        ones = jnp.ones((8, x_ref.shape[1]), bf16)
        for third in range(3):
            part = slice(third * local, (third + 1) * local)
            sums = jnp.zeros((8, local), f32)
            for b in range(count):
                sums = sums + dot(ones, d_refs[b][third], 1, 1) + f_ref[b : b + 1, part]
            sum_ref[:, part] = sums

    gain = jnp.zeros(gain_ref.shape, f32)
    shift = jnp.zeros(shift_ref.shape, f32)
    result = jnp.zeros((x_ref.shape[2], 3 * local), f32)
    for b in range(count):
        grads = d_refs[b][...].reshape(3 * local, -1)
        result = result + dot(x_ref[b], grads, 0, 1) + p_ref[:, b : b + 1] * f_ref[b : b + 1]
    o_ref[...] = result.astype(bf16)
    for third in range(3):
        part = slice(third * local, (third + 1) * local)
        weight = w_refs[third][...].astype(f32)
        gain = gain + jnp.sum(weight * result[:, part], axis=1, keepdims=True)
        shift = shift + jnp.sum(weight * sum_ref[0:1, part], axis=1, keepdims=True)
    gain_ref[...] = gain
    shift_ref[...] = shift


def self_weight_grad(frames, prefix, grads, front, weights):
    count, rows, width = frames.shape
    local = grads[0].shape[1]
    depth = 3 * local
    block = 256
    weight = pl.BlockSpec((block, local), lambda i: (i, 0))
    column = pl.BlockSpec((block, 1), lambda i: (i, 0))
    return pl.pallas_call(
        functools.partial(self_weight_grad_kernel, count),
        grid=(width // block,),
        in_specs=[
            pl.BlockSpec((count, rows, block), lambda i: (0, 0, i)),
            pl.BlockSpec((block, count), lambda i: (i, 0)),
            pl.BlockSpec((count, depth), lambda i: (0, 0)),
        ]
        + [pl.BlockSpec((3, local, rows), lambda i: (0, 0, 0))] * count
        + [weight] * 3,
        out_specs=[pl.BlockSpec((block, depth), lambda i: (i, 0)), column, column],
        out_shape=[shape_of((width, depth), bf16)] + [shape_of((width, 1), f32)] * 2,
        scratch_shapes=[pltpu.VMEM((8, depth), f32)],
        compiler_params=params(),
        cost_estimate=cost(12),
        name="self_weight_grad",
    )(frames, prefix.T.astype(f32), front.astype(f32), *grads, *weights)


def self_back_kernel(d_ref, wq_ref, wk_ref, wv_ref, o_ref):
    local = wq_ref.shape[1]
    back = jnp.zeros(o_ref.shape[1:], f32)
    for third, ref in enumerate((wq_ref, wk_ref, wv_ref)):
        back = back + dot(d_ref[third], ref[...], 0, 1)
    o_ref[0] = back.astype(bf16)


def self_back(grads, weights):
    size = lax.axis_size("mp")
    _, local, frames = grads.shape
    width = weights[0].shape[0]
    rows = frames // size
    return pl.pallas_call(
        self_back_kernel,
        grid=(size,),
        in_specs=[pl.BlockSpec((3, local, rows), lambda k: (0, 0, k))] + whole_specs(weights),
        out_specs=pl.BlockSpec((1, rows, width), lambda k: (k, 0, 0)),
        out_shape=shape_of((size, rows, width), bf16),
        compiler_params=params(),
        cost_estimate=cost(7),
        name="self_back",
    )(grads, *weights)


def turning(frames):
    places = (jnp.arange(frames) + 1).astype(f32)
    rates = jnp.exp(jnp.arange(HALF).astype(f32) * (-2.0 * math.log(10000.0) / HEAD_DIM))
    angles = rates[:, None] * places[None, :]
    return (jnp.cos(angles), jnp.sin(angles))


def sum_over_clips(values, axis):
    return lax.psum_scatter(values.astype(bf16), "dp", scatter_dimension=axis, tiled=True)


def shards(
    frames_in,
    prompt,
    lengths,
    tsteps,
    table,
    gain_one,
    shift_one,
    gain_two,
    shift_two,
    gain_three,
    shift_three,
    w_query,
    w_key,
    w_value,
    w_out,
    c_query,
    c_key,
    c_value,
    c_out,
    w_gate,
    w_up,
    w_down,
    cotangent,
):
    size = lax.axis_size("mp")
    groups = lax.axis_size("dp")
    count, rows, width = frames_in.shape
    clips = range(count)
    local = w_query.shape[1]
    here = lax.axis_index("mp")
    there = lax.axis_index("dp")
    core = there & 1
    chain = Chain()
    hold, mark, arrive = chain.hold, chain.mark, chain.arrive

    def joined(parts, axis):
        return jnp.concatenate(parts, axis=axis)

    order = jnp.stack([here ^ k for k in range(size)]).astype(jnp.int32)
    this_core = jnp.stack([core]).astype(jnp.int32)
    depth = width // groups
    side = jnp.stack(
        [
            lax.dynamic_slice_in_dim(c_query, there * depth, depth, 0),
            lax.dynamic_slice_in_dim(c_out, there * depth, depth, 1).T,
        ]
    )
    side = lax.all_gather(side, "mp", axis=0)
    ones, low = [], []
    for b in clips:
        ones.append(norm_forward(hold(frames_in[b]).astype(f32), gain_one, shift_one))
        low.append(ones[b][0].astype(bf16))
        mark(low[b])
        if b == 0:
            spread_one = [Spread(low[0])]
            spread_one[0].first = arrive(spread_one[0].first)
            spread_one[0].second_step()
        else:
            spread_one.append(Spread(low[b]))
    tokens = prompt.reshape(-1, prompt.shape[-1])
    memory = [dot(hold(part), tokens, 0, 1).astype(bf16) for part in (c_key, c_value)]
    mark(*memory)
    memory = joined(memory, 0)
    side = arrive(side)
    c_query_all = lax.all_gather(side[:, 0], "dp", axis=1, tiled=True)
    c_out_all = lax.all_gather(side[:, 1], "dp", axis=1, tiled=True)
    cosine, sine = turning(size * rows)
    picked = [lax.dynamic_slice_in_dim(hold(table), tsteps[b], 1, 0) for b in clips]
    mark(*picked)
    picked = joined(picked + [jnp.ones((8 - count, width), f32)], 0)
    norm_one = jnp.stack([gain_one, shift_one])
    half = lax.dynamic_slice_in_dim(hold(w_out), core * (local // 2), local // 2, 0)
    mark(half)
    spread_one[0].last = arrive(spread_one[0].last)
    for later in spread_one[1:]:
        later.first = arrive(later.first)
        later.second_step()
        later.last = arrive(later.last)
    halves = gathered(hold(half))

    turned, mixed_part, logsum, mixed = [], [], [], []
    frames_one = ()
    weights = [w_query, w_key, w_value]
    for b in clips:
        pieces = hold(spread_one[b].pieces())
        out, frames_one, front = project(
            b, count, order, picked, norm_one, pieces, weights, cosine, sine, list(frames_one)
        )
        frames_one = (frames_one,)
        turned.append(out)
        mark(out)
        if b == 0:
            front_keys = [front[:local, c : c + 1] for c in clips]
            front_values = [front[local:, c : c + 1] for c in clips]
        else:
            memory = hold(memory)
            memory = [memory] + [swap(memory, "mp", k) for k in range(1, size)]
            halves = arrive(halves)
            other = swap(halves, "dp", 1)
            mixed[0] = exchange(hold(mixed[0]))
        out, sums = self_forward(hold(turned[b]), front_keys[b], front_values[b])
        mixed_part.append(out)
        logsum.append(sums)
        mixed.append(out)
        mark(out)
    frames_one = frames_one[0]
    mixed[0] = arrive(mixed[0])
    for b in clips[1:]:
        mixed[b] = exchange(hold(mixed[b]))
    memory = jnp.stack(arrive(memory))
    mark(memory)
    spread_down = [Spread(hold(cotangent[0]))]
    other = arrive(other)
    local_weights = (halves, other, c_query_all, c_out_all)

    norms = jnp.stack([gain_two, shift_two, gain_three, shift_three])
    first, normed_two, cross, second, low, spread_three = [], [], [], [], [], []
    for b in clips:
        mixed[b] = hold(mixed[b]).reshape(size * local, rows)
        parts = local_forward(
            b, count, lengths, this_core, order, mixed[b], frames_in[b], norms, memory, local_weights
        )
        first.append(parts[0])
        second.append(parts[1])
        normed_two.append(parts[2])
        cross.append(parts[3:6])
        low.append(parts[6])
        mark(low[b])
        if b == 0:
            spread_three.append(Spread(low[b]))
            spread_down[0].first = arrive(spread_down[0].first)
            spread_down[0].second_step()

    back_three = []
    parts = ()
    spread_down[0].last = arrive(spread_down[0].last)
    spread_three[0].first = arrive(spread_three[0].first)
    spread_three[0].second_step()
    spread_three.extend(Spread(hold(later)) for later in low[1:])
    spread_three[0].last = arrive(spread_three[0].last)
    spread_down.extend(Spread(hold(later)) for later in cotangent[1:])
    for b in clips:
        pieces = hold(spread_three[b].pieces())
        parts = glu(
            b, count, order, pieces, spread_down[b].pieces(), w_gate, w_up, w_down, list(parts)
        )
        mark(parts[1])
        if b == 0:
            for later in spread_three[1:] + spread_down[1:]:
                later.first = arrive(later.first)
                later.second_step()
        grad_gate, grad_upper = hold((parts[1], parts[2]))
        back = glu_back(b, grad_gate, grad_upper, w_gate, w_up)
        mark(back)
        if b == 0:
            for later in spread_three[1:] + spread_down[1:]:
                later.last = arrive(later.last)
        else:
            back_three[b - 1] = arrive(back_three[b - 1])
        back_three.append(exchange(hold(back)))

    hidden, grad_gate, grad_upper, frames_three, down_in = parts
    raw_w_down = weight_grad(hold(down_in), hidden)
    grad_w_down = sum_over_clips(raw_w_down, 0)
    mark(raw_w_down)
    branch = branch_blocks(hold(hidden), w_down)
    mark(branch)
    branch = lax.psum_scatter(branch, "mp", scatter_dimension=0, tiled=True)[0]
    raw_w_gate = weight_grad(hold(frames_three), grad_gate)
    grad_w_gate = sum_over_clips(raw_w_gate, 0)
    mark(raw_w_gate)

    grad_one, cross_in, self_in = [], [], []
    grad_cross_query, grad_memory, grad_mixed, norm_terms = [], [], [], []
    for b in clips:
        if b:
            back_three[b] = arrive(back_three[b])
            grad_mixed[b - 1] = exchange(hold(grad_mixed[b - 1]))
        parts = local_backward(
            b,
            count,
            lengths,
            this_core,
            order,
            hold(back_three[b]),
            cotangent[b],
            first[b],
            second[b],
            cross[b],
            norms,
            memory,
            local_weights,
        )
        cross_in.append(parts[0])
        self_in.append(parts[1])
        grad_one.append(parts[2])
        grad_cross_query.append(parts[3])
        grad_memory.append(parts[4])
        norm_terms.append(parts[6])
        mark(parts[5])
        grad_mixed.append(parts[5].reshape(size, local, rows))
    for b in clips[:-1]:
        grad_mixed[b] = arrive(grad_mixed[b])
    grad_mixed[-1] = exchange(hold(grad_mixed[-1]))

    grad_memory = Settle(joined(hold(grad_memory), 2))
    mark(*grad_memory.mine)
    grad_memory = grad_memory.second_step()
    rights = (grad_cross_query, [part[1] for part in cross], mixed)
    other_raws, lefts = whole_grad(
        1 - this_core, groups, (normed_two, hold(cross_in), self_in), rights, []
    )
    mark(other_raws)
    other_raws = swap(other_raws, "dp", 1)
    raw_w_up = weight_grad(hold(frames_three), grad_upper)
    grad_w_up = sum_over_clips(raw_w_up, 0)
    mark(raw_w_up)
    raws = whole_grad(this_core, groups, lefts, rights, [arrive(other_raws)])
    mark(raws)
    raws = Settle(hold(raws).reshape(size, -1, local))
    mark(*raws.mine)
    raws.first_step()

    grad_self, grad_front, back_one = [], [], []
    for b in clips:
        grads, grad_front_key, grad_front_value = self_backward(
            turned[b],
            hold(grad_mixed[b]),
            mixed_part[b],
            logsum[b],
            front_keys[b],
            front_values[b],
            cosine,
            sine,
        )
        grad_self.append(grads)
        grad_front.append(joined([grad_front_key, grad_front_value], 0))
        mark(grads)
        if b + 1 < count:
            grad_mixed[b + 1] = arrive(grad_mixed[b + 1])
            raws.came = arrive(raws.came)
            raws.add()
            mark(*raws.mine)
            raws = raws.second_step()
            back = self_back(hold(grad_self[b]), weights)
            mark(back)
            back_one.append(exchange(hold(back)))
            grad_memory = total(arrive(grad_memory)).astype(bf16)
            low_memory = [
                dot(tokens, part, 0, 1).astype(bf16) for part in jnp.split(grad_memory, 2, axis=0)
            ]
            mark(*low_memory)
            low_memory = [part.reshape(groups, -1, local) for part in low_memory]
            mine, other = core_half(joined(low_memory, 1))

    raws = total(arrive(raws)).astype(bf16).reshape(groups // 2, 3, -1, local)
    memory_half = plus(mine, arrive(other))
    mark(raws, memory_half)
    raws = joined([raws, memory_half[:, None]], 1)
    cores = [list(range(c, groups, 2)) for c in range(2)]
    raws = lax.psum_scatter(raws, "dp", scatter_dimension=0, axis_index_groups=cores, tiled=True)[0]
    prefix_normed, prefix_normal, prefix_scale = norm_forward(
        picked[:count], gain_one, shift_one
    )
    prefix_low = prefix_normed.astype(bf16)
    grad_front = joined(grad_front, 1)
    wide_front = joined([jnp.zeros((count, local), bf16), grad_front.T], 1)
    low_w_self, gain_term, shift_term = self_weight_grad(
        frames_one, prefix_low, hold(grad_self), wide_front, weights
    )
    grad_w_self = sum_over_clips(low_w_self, 0)
    mark(low_w_self)
    back = self_back(hold(grad_self[-1]), weights)
    mark(back)
    back_one = arrive(back_one)
    back_one.append(exchange(hold(back)))

    def wide(value):
        return value.astype(f32)

    small = []
    gain_term, shift_term = gain_term[:, 0], shift_term[:, 0]
    small.append((gain_term - shift_one * shift_term) / gain_one)
    small.append(shift_term)
    norm_terms = sum(norm_terms[1:], norm_terms[0])
    steps = jnp.where(here == 0, tsteps, 0).astype(f32)
    steps = lax.dynamic_update_slice(jnp.zeros((width,), f32), steps, (there * count,))

    back_prefix = dot(grad_front[:local], w_key, 0, 1) + dot(grad_front[local:], w_value, 0, 1)
    grad_picked = norm_backward(back_prefix, prefix_normal, prefix_scale, gain_one)
    spots = jnp.arange(groups)[:, None, None] == there
    spots = jnp.where(spots, grad_picked[None], 0.0).reshape(groups * count, width)
    small = hold(joined([jnp.stack(small), norm_terms, steps[None], spots], 0))
    small = all_sum(small)
    all_steps = small[6, : groups * count]
    matches = jnp.arange(table.shape[0])[:, None].astype(f32) == all_steps[None, :]
    grad_table = jnp.dot(matches.astype(f32), small[7:], precision=lax.Precision.HIGHEST)

    mark(small)
    back_one[-1] = arrive(back_one[-1])
    back_one = [total(terms) for terms in back_one]
    grad_frames = [
        grad_one[b] + norm_backward(back_one[b], ones[b][1], ones[b][2], gain_one) for b in clips
    ]
    mark(grad_table, *grad_frames)
    grad_w_down = wide(arrive(grad_w_down).T)
    branch = arrive(branch)
    output = [second[b] + branch[b].astype(f32) for b in clips]
    grad_w_gate = wide(arrive(grad_w_gate))
    grad_w_up = arrive(grad_w_up)
    raws = arrive(raws).astype(f32)
    grad_w_self = arrive(grad_w_self)

    depth_c = prompt.shape[-1] // groups

    return (
        jnp.stack(output),
        jnp.stack(grad_frames),
        grad_table,
        small[0],
        small[1],
        small[2],
        small[3],
        small[4],
        small[5],
        wide(grad_w_self[:, :local]),
        wide(grad_w_self[:, local : 2 * local]),
        wide(grad_w_self[:, 2 * local :]),
        raws[2].T,
        raws[0],
        raws[3, :depth_c],
        raws[3, depth_c:],
        raws[1].T,
        grad_w_gate,
        wide(grad_w_up),
        grad_w_down,
    )


def solution(mesh):
    placed = (
        P("dp", "mp", None),
        P("dp", None, None),
        P("dp"),
        P("dp"),
        P(),
        P(),
        P(),
        P(),
        P(),
        P(),
        P(),
        P(None, "mp"),
        P(None, "mp"),
        P(None, "mp"),
        P("mp", None),
        P(None, "mp"),
        P(None, "mp"),
        P(None, "mp"),
        P("mp", None),
        P(None, "mp"),
        P(None, "mp"),
        P("mp", None),
        P("dp", "mp", None),
    )
    return jax.shard_map(
        shards,
        mesh=mesh,
        in_specs=placed,
        out_specs=(
            P("dp", "mp", None),
            P("dp", "mp", None),
            P(),
            P(),
            P(),
            P(),
            P(),
            P(),
            P(),
            P("dp", "mp"),
            P("dp", "mp"),
            P("dp", "mp"),
            P("mp", "dp"),
            P("dp", "mp"),
            P("dp", "mp"),
            P("dp", "mp"),
            P("mp", "dp"),
            P("dp", "mp"),
            P("dp", "mp"),
            P("mp", "dp"),
        ),
        check_vma=False,
    )
```

```python
import functools
import math

import jax
import jax.numpy as jnp
from jax import lax
from jax.experimental import pallas as pl
from jax.experimental.pallas import tpu as pltpu
from jax.sharding import PartitionSpec as P

HEAD_DIM = 64
HALF = HEAD_DIM // 2
FACTOR = 1.0 / math.sqrt(HEAD_DIM)

norm_eps = 1e-05

f32 = jnp.float32
bf16 = jnp.bfloat16


def dot(left, right, left_axis, right_axis):
    return lax.dot_general(
        left, right, (((left_axis,), (right_axis,)), ((), ())), preferred_element_type=f32
    )


def norm_forward(values, gain, shift):
    center = values - jnp.mean(values, axis=-1, keepdims=True)
    scale = lax.rsqrt(jnp.mean(center * center, axis=-1, keepdims=True) + norm_eps)
    normal = center * scale
    return (normal * gain + shift, normal, scale)


def norm_backward(grad, normal, scale, gain):
    inner = grad * gain
    return scale * (
        inner
        - jnp.mean(inner, axis=-1, keepdims=True)
        - normal * jnp.mean(inner * normal, axis=-1, keepdims=True)
    )


def bits_of(size):
    return [1 << place for place in range(size.bit_length() - 1)]


def swap(values, axis, k):
    return lax.ppermute(values, axis, [(i, i ^ k) for i in range(lax.axis_size(axis))])


def after(values, *others):
    return lax.optimization_barrier((values,) + others)[0]


class Spread:
    def __init__(self, values):
        self.values = values
        self.last = ()
        size = lax.axis_size("mp")
        partners = (1, 2) if size == 4 else range(1, size)
        self.first = tuple(swap(values, "mp", k) for k in partners)

    def second_step(self):
        if lax.axis_size("mp") == 4:
            one, two = self.first
            half = one.shape[0] // 2
            self.last = (swap(one[:half], "mp", 2), swap(two[half:], "mp", 1))

    def pieces(self):
        return [self.values, *self.first, *self.last]


def place(blocks, axis):
    here = lax.axis_index("mp")
    step = blocks[0].shape[axis]
    shape = list(blocks[0].shape)
    shape[axis] = step * len(blocks)
    result = jnp.zeros(shape, blocks[0].dtype)
    for k, block in enumerate(blocks):
        result = lax.dynamic_update_slice_in_dim(result, block, (here ^ k) * step, axis)
    return result


def gathered(values):
    return exchange(jnp.broadcast_to(values[None], (lax.axis_size("mp"),) + values.shape))


def exchange(blocks):
    return lax.all_to_all(blocks, "mp", 0, 0)


class Settle:
    def __init__(self, blocks):
        here = lax.axis_index("mp")
        size = blocks.shape[0]
        self.mine = [lax.dynamic_index_in_dim(blocks, here ^ k, 0, False) for k in range(size)]
        self.came = ()

    def first_step(self):
        if len(self.mine) == 4:
            half = self.mine[3].shape[0] // 2
            self.came = (swap(self.mine[3][:half], "mp", 2), swap(self.mine[3][half:], "mp", 1))

    def add(self):
        if len(self.mine) == 4:
            _, one, two, _ = self.mine
            high, low = self.came
            half = high.shape[0]
            one = jnp.concatenate([plus(one[:half], high), one[half:]], axis=0)
            two = jnp.concatenate([two[:half], plus(two[half:], low)], axis=0)
            self.mine = [self.mine[0], one, two]

    def second_step(self):
        return [self.mine[0]] + [swap(self.mine[k], "mp", k) for k in range(1, len(self.mine))]


def plus(left, right):
    return (left.astype(f32) + right.astype(f32)).astype(bf16)


def total(terms):
    result = terms[0].astype(f32)
    for k in range(1, len(terms)):
        result = result + terms[k].astype(f32)
    return result


def all_sum(values):
    for axis in ("dp", "mp"):
        for bit in bits_of(lax.axis_size(axis)):
            values = values + swap(values, axis, bit)
    return values


def core_half(blocks):
    core = lax.axis_index("dp") & 1
    pairs = blocks.reshape((blocks.shape[0] // 2, 2) + blocks.shape[1:])
    mine = lax.dynamic_index_in_dim(pairs, core, 1, False)
    other = lax.dynamic_index_in_dim(pairs, 1 - core, 1, False)
    return (mine, swap(other, "dp", 1))


class Chain:
    def __init__(self):
        self.last = ()

    def hold(self, values):
        return after(values, *self.last) if self.last else values

    def mark(self, *values):
        self.last = values

    def arrive(self, values):
        values = self.hold(values)
        self.mark(values)
        return values


def plus(left, right):
    return (left.astype(f32) + right.astype(f32)).astype(bf16)


def total(terms):
    result = terms[0].astype(f32)
    for term in terms[1:]:
        result = result + term.astype(f32)
    return result


def all_sum(values):
    for axis in ("dp", "mp"):
        for bit in bits_of(lax.axis_size(axis)):
            values = values + swap(values, axis, bit)
    return values


def core_half(blocks):
    core = lax.axis_index("dp") & 1
    pairs = blocks.reshape((blocks.shape[0] // 2, 2) + blocks.shape[1:])
    mine = lax.dynamic_index_in_dim(pairs, core, 1, False)
    other = lax.dynamic_index_in_dim(pairs, 1 - core, 1, False)
    return (mine, swap(other, "dp", 1))


def chips_sum(blocks):
    here = lax.axis_index("dp") >> 1
    mine = [
        lax.dynamic_index_in_dim(blocks, here ^ k, 0, False) for k in range(blocks.shape[0])
    ]
    return total([mine[0]] + [swap(mine[k], "dp", 2 * k) for k in range(1, len(mine))])


def self_forward_kernel(q_ref, k_ref, v_ref, pk_ref, pv_ref, o_ref, l_ref):
    parts = head_parts(q_ref.shape[0])
    scores = [dot(k_ref[part], q_ref[part], 0, 0) for part in parts]
    for head, part in enumerate(parts):
        front = q_ref[part].astype(f32) * pk_ref[part].astype(f32)
        front = jnp.sum(front, axis=0, keepdims=True)
        top = jnp.maximum(jnp.max(scores[head], axis=0, keepdims=True), front)
        weights = jnp.exp(scores[head] - top)
        front_weight = jnp.exp(front - top)
        total = jnp.sum(weights, axis=0, keepdims=True) + front_weight
        mixed = dot(v_ref[part], weights.astype(bf16), 1, 0)
        mixed = mixed + pv_ref[part].astype(f32) * front_weight.astype(bf16).astype(f32)
        mixed = (mixed * (1.0 / total)).astype(bf16)
        frames = o_ref.shape[2]
        for k in range(o_ref.shape[0]):
            o_ref[k, part] = mixed[:, k * frames : (k + 1) * frames]
        l_ref[head] = top + jnp.log(total)


def self_backward_kernel(
    block,
    q_ref,
    k_ref,
    v_ref,
    g_ref,
    o_ref,
    l_ref,
    pk_ref,
    pv_ref,
    cos_ref,
    sin_ref,
    d_ref,
    dpk_ref,
    dpv_ref,
):
    frames = q_ref.shape[1]
    keys = k_ref[...]
    values = v_ref[...]
    front_key = pk_ref[...].astype(f32)
    front_value = pv_ref[...].astype(f32)
    grad_keys = jnp.zeros((HEAD_DIM, frames), f32)
    grad_values = jnp.zeros((HEAD_DIM, frames), f32)
    grad_front_key = jnp.zeros((HEAD_DIM, 1), f32)
    grad_front_value = jnp.zeros((HEAD_DIM, 1), f32)
    whole_grads = jnp.concatenate([g_ref[k] for k in range(g_ref.shape[0])], axis=1)
    whole_mixed = jnp.concatenate([o_ref[k] for k in range(o_ref.shape[0])], axis=1)
    for start in range(0, frames, block):
        part = slice(start, start + block)
        queries = q_ref[:, part]
        grads = whole_grads[:, part]
        wide_queries = queries.astype(f32)
        wide_grads = grads.astype(f32)
        logsum = l_ref[0, :, part]
        mixsum = jnp.sum(whole_mixed[:, part].astype(f32) * wide_grads, axis=0, keepdims=True)
        probs = jnp.exp(dot(keys, queries, 0, 0) - logsum)
        grad_probs = dot(values, grads, 0, 0)
        grad_scores = (probs * (grad_probs - mixsum)).astype(bf16)
        grad_values = grad_values + dot(grads, probs.astype(bf16), 1, 1)
        grad_keys = grad_keys + dot(queries, grad_scores, 1, 1)
        grad_queries = dot(keys, grad_scores, 1, 0)
        front = jnp.exp(jnp.sum(wide_queries * front_key, axis=0, keepdims=True) - logsum)
        grad_front = jnp.sum(wide_grads * front_value, axis=0, keepdims=True)
        grad_front = (front * (grad_front - mixsum)).astype(bf16).astype(f32)
        front = front.astype(bf16).astype(f32)
        grad_front_key += jnp.sum(wide_queries * grad_front, axis=1, keepdims=True)
        grad_front_value += jnp.sum(wide_grads * front, axis=1, keepdims=True)
        grad_queries = (grad_queries + front_key * grad_front) * FACTOR
        cosine = cos_ref[:, part]
        sine = sin_ref[:, part]
        upper, lower = grad_queries[:HALF], grad_queries[HALF:]
        d_ref[0, :HALF, part] = (upper * cosine + lower * sine).astype(bf16)
        d_ref[0, HALF:, part] = (lower * cosine - upper * sine).astype(bf16)
    cosine = cos_ref[...]
    sine = sin_ref[...]
    upper, lower = grad_keys[:HALF], grad_keys[HALF:]
    d_ref[1, :HALF, :] = (upper * cosine + lower * sine).astype(bf16)
    d_ref[1, HALF:, :] = (lower * cosine - upper * sine).astype(bf16)
    d_ref[2] = grad_values.astype(bf16)
    dpk_ref[...] = grad_front_key.astype(bf16)
    dpv_ref[...] = grad_front_value.astype(bf16)


def head_parts(rows):
    return [slice(at, at + HEAD_DIM) for at in range(0, rows, HEAD_DIM)]


def fetch(core, out_halves, out, wholes, targets, sems):
    mine, other = out_halves
    size, half, _ = mine.shape
    copies = []
    for k in range(size):
        for source, part in ((mine, core), (other, 1 - core)):
            at = pl.multiple_of((2 * k + part) * half, 16)
            target = out.at[pl.ds(at, half)]
            copies.append(pltpu.make_async_copy(source.at[k], target, sems.at[len(copies)]))
    first = len(copies)
    for source, target in zip(wholes, targets):
        copies.append(pltpu.make_async_copy(source, target, sems.at[len(copies)]))

    def start_out():
        for copy in copies[:first]:
            copy.start()

    def start_whole(k):
        copies[first + k].start()

    def get_out():
        for copy in copies[:first]:
            copy.wait()
        return out[...]

    def get_whole(k):
        copies[first + k].wait()
        return targets[k]

    return start_out, start_whole, get_out, get_whole


def local_forward_kernel(
    clip, n_ref, core_ref, order_ref, mixed_ref, x_ref, norm_ref, mem_ref, wo_mine, wo_other, cq_hbm, co_hbm, *refs
):
    first_ref, second_ref, two_ref, q_ref, o_ref, l_ref, three_ref, wo, cq, co, sems = refs
    start_out, start_whole, get_out, get_whole = fetch(
        core_ref[0], (wo_mine, wo_other), wo, (cq_hbm, co_hbm), (cq, co), sems
    )
    start_out()
    start_whole(0)
    start_whole(1)
    groups, depth, slots = mem_ref.shape
    local = depth // 2
    live = lax.broadcasted_iota(jnp.int32, (slots, 1), 0) < n_ref[clip]
    first = x_ref[...].astype(f32) + dot(mixed_ref[...], get_out(), 0, 0)
    first_ref[...] = first
    two = norm_forward(first, norm_ref[0:1], norm_ref[1:2])[0].astype(bf16)
    two_ref[...] = two
    weight = get_whole(0)
    for k in range(groups):
        q_ref[k * local : (k + 1) * local] = (dot(two, weight[k], 1, 0) * FACTOR).astype(bf16).T
    for group in range(groups):
        parts = head_parts(local)
        there = order_ref[group]
        at = group * local
        queries = [q_ref[at + p.start : at + p.stop] for p in parts]
        scores = [dot(mem_ref[there, p], q, 0, 0) for p, q in zip(parts, queries)]
        scores = [jnp.where(live, s, -1e30) for s in scores]
        tops = [jnp.max(s, axis=0, keepdims=True) for s in scores]
        weights = [jnp.exp(s - top) for s, top in zip(scores, tops)]
        totals = [jnp.sum(w, axis=0, keepdims=True) for w in weights]
        for head, p in enumerate(parts):
            values = mem_ref[there, local + p.start : local + p.stop]
            mixed = dot(values, weights[head].astype(bf16), 1, 0)
            o_ref[at + p.start : at + p.stop] = (mixed * (1.0 / totals[head])).astype(bf16)
            l_ref[group * len(parts) + head] = tops[head] + jnp.log(totals[head])
    weight = get_whole(1)
    second = first
    for k in range(groups):
        second = second + dot(o_ref[k * local : (k + 1) * local], weight[k], 0, 1)
    second_ref[...] = second
    three_ref[...] = norm_forward(second, norm_ref[2:3], norm_ref[3:4])[0].astype(bf16)


def local_specs(clip, count, rows, width, memory):
    groups, depth, slots = memory.shape
    heads = groups * depth // 2 // HEAD_DIM
    wide = pl.BlockSpec((rows, width), lambda i: (0, 0))
    turned = pl.BlockSpec((width, rows), lambda i: (0, 0))
    sums = pl.BlockSpec((heads, 1, rows), lambda i: (0, 0, 0))
    norms = pl.BlockSpec((4, width), lambda i: (0, 0))
    mem = pl.BlockSpec((groups, depth, slots // count), lambda i: (0, 0, clip))
    return (wide, turned, sums, norms, mem, heads)


def local_forward(clip, count, lengths, core, order, mixed, frames, norms, memory, weights):
    rows, width = frames.shape
    wide, turned, sums, norm_spec, mem, heads = local_specs(clip, count, rows, width, memory)
    return pl.pallas_call(
        functools.partial(local_forward_kernel, clip),
        grid=(1,),
        in_specs=[pl.BlockSpec(memory_space=pltpu.SMEM)] * 3
        + [turned, wide, norm_spec, mem]
        + [pl.BlockSpec(memory_space=pl.ANY)] * 4,
        out_specs=[wide, wide, wide, turned, turned, sums, wide],
        out_shape=[
            shape_of((rows, width), f32),
            shape_of((rows, width), f32),
            shape_of((rows, width), bf16),
            shape_of((width, rows), bf16),
            shape_of((width, rows), bf16),
            shape_of((heads, 1, rows), f32),
            shape_of((rows, width), bf16),
        ],
        scratch_shapes=[pltpu.VMEM((width, width), bf16)]
        + [pltpu.VMEM(weights[2].shape, bf16)] * 2
        + [pltpu.SemaphoreType.DMA((2 * memory.shape[0] + 2,))],
        compiler_params=params(),
        cost_estimate=cost(11.3),
        name="local_forward",
    )(lengths, core, order, mixed, frames, norms, memory, *weights)


def local_backward_kernel(
    clip,
    n_ref,
    core_ref,
    order_ref,
    b_ref,
    cot_ref,
    first_ref,
    second_ref,
    q_ref,
    o_ref,
    l_ref,
    norm_ref,
    mem_ref,
    wo_mine,
    wo_other,
    cq_hbm,
    co_hbm,
    *refs,
):
    cross_ref, self_ref, one_ref, dq_ref, d_ref, g_ref, term_ref, grads_ref, wo, cq, co, sems = refs
    start_out, start_whole, get_out, get_whole = fetch(
        core_ref[0], (wo_mine, wo_other), wo, (cq_hbm, co_hbm), (cq, co), sems
    )
    start_whole(1)
    start_whole(0)
    start_out()
    groups, depth, slots = mem_ref.shape
    local = depth // 2
    heads = local // HEAD_DIM
    live = lax.broadcasted_iota(jnp.int32, (slots, 1), 0) < n_ref[clip]

    back = total([b_ref[k] for k in range(b_ref.shape[0])])
    _, normal, scale = norm_forward(second_ref[...], norm_ref[2:3], norm_ref[3:4])
    term_ref[2:3] = jnp.sum(back * normal, axis=0, keepdims=True)
    term_ref[3:4] = jnp.sum(back, axis=0, keepdims=True)
    grad_two = cot_ref[...].astype(f32) + norm_backward(back, normal, scale, norm_ref[2:3])
    cross_in = grad_two.astype(bf16)
    cross_ref[...] = cross_in
    weight = get_whole(1)
    for k in range(groups):
        grads_ref[k * local : (k + 1) * local] = dot(cross_in, weight[k], 1, 0).astype(bf16).T
    for group in range(groups):
        for head, part in enumerate(head_parts(local)):
            there = slice(group * local + part.start, group * local + part.stop)
            queries = q_ref[there]
            keys = mem_ref[order_ref[group], part]
            grads = grads_ref[there]
            mixsum = jnp.sum(o_ref[there].astype(f32) * grads.astype(f32), axis=0, keepdims=True)
            scores = jnp.where(live, dot(keys, queries, 0, 0), -1e30)
            probs = jnp.exp(scores - l_ref[group * heads + head])
            values = slice(local + part.start, local + part.stop)
            grad_probs = dot(mem_ref[order_ref[group], values], grads, 0, 0)
            grad_scores = (probs * (grad_probs - mixsum)).astype(bf16)
            dq_ref[there] = (dot(keys, grad_scores, 1, 0) * FACTOR).astype(bf16)
            d_ref[group, part] = dot(queries, grad_scores, 1, 1).astype(bf16)
            d_ref[group, values] = dot(grads, probs.astype(bf16), 1, 1).astype(bf16)
    weight = get_whole(0)
    back = jnp.zeros(grad_two.shape, f32)
    for k in range(groups):
        back = back + dot(dq_ref[k * local : (k + 1) * local], weight[k], 0, 1)
    _, normal, scale = norm_forward(first_ref[...], norm_ref[0:1], norm_ref[1:2])
    term_ref[0:1] = jnp.sum(back * normal, axis=0, keepdims=True)
    term_ref[1:2] = jnp.sum(back, axis=0, keepdims=True)
    grad_one = grad_two + norm_backward(back, normal, scale, norm_ref[0:1])
    one_ref[...] = grad_one
    self_in = grad_one.astype(bf16)
    self_ref[...] = self_in
    g_ref[...] = dot(get_out(), self_in, 1, 1).astype(bf16)


def local_backward(
    clip, count, lengths, core, order, back, cotangent, first, second, cross, norms, memory, weights
):
    rows, width = cotangent.shape
    wide, turned, sums, norm_spec, mem, heads = local_specs(clip, count, rows, width, memory)
    groups, depth, slots = memory.shape
    slots = slots // count
    return pl.pallas_call(
        functools.partial(local_backward_kernel, clip),
        grid=(1,),
        in_specs=[
            pl.BlockSpec(memory_space=pltpu.SMEM),
            pl.BlockSpec(memory_space=pltpu.SMEM),
            pl.BlockSpec(memory_space=pltpu.SMEM),
            pl.BlockSpec(back.shape, lambda i: (0, 0, 0)),
            wide,
            wide,
            wide,
            turned,
            turned,
            sums,
            norm_spec,
            mem,
        ]
        + [pl.BlockSpec(memory_space=pl.ANY)] * 4,
        out_specs=[
            wide,
            wide,
            wide,
            turned,
            pl.BlockSpec((groups, depth, slots), lambda i: (0, 0, 0)),
            turned,
            norm_spec,
        ],
        out_shape=[
            shape_of((rows, width), bf16),
            shape_of((rows, width), bf16),
            shape_of((rows, width), f32),
            shape_of((width, rows), bf16),
            shape_of((groups, depth, slots), bf16),
            shape_of((width, rows), bf16),
            shape_of((4, width), f32),
        ],
        scratch_shapes=[pltpu.VMEM((width, rows), bf16)]
        + [pltpu.VMEM((width, width), bf16)]
        + [pltpu.VMEM(weights[2].shape, bf16)] * 2
        + [pltpu.SemaphoreType.DMA((2 * groups + 2,))],
        compiler_params=params(),
        cost_estimate=cost(40),
        name="local_backward",
    )(lengths, core, order, back, cotangent, first, second, *cross, norms, memory, *weights)


def cost(micros):
    micros = 0.4 * micros
    return pl.CostEstimate(
        flops=int(micros * 1.15e9), bytes_accessed=int(micros * 3.6e6), transcendentals=0
    )


def shape_of(shape, kind):
    return jax.ShapeDtypeStruct(shape, kind)


def params():
    return pltpu.CompilerParams(vmem_limit_bytes=58 * 2**20)


def self_forward(turned, front_keys, front_values):
    size = lax.axis_size("mp")
    heads = front_keys.shape[0] // HEAD_DIM
    frames = turned.shape[1]
    step = 3 if heads % 3 == 0 else 1
    rows = step * HEAD_DIM
    steps = heads // step

    def at(third):
        return pl.BlockSpec((rows, frames), lambda h: (third * steps + h, 0))

    column = pl.BlockSpec((rows, 1), lambda h: (h, 0))
    return pl.pallas_call(
        self_forward_kernel,
        grid=(steps,),
        in_specs=[at(0), at(1), at(2), column, column],
        out_specs=[
            pl.BlockSpec((size, rows, frames // size), lambda h: (0, h, 0)),
            pl.BlockSpec((step, 1, frames), lambda h: (h, 0, 0)),
        ],
        out_shape=[
            shape_of((size, heads * HEAD_DIM, frames // size), bf16),
            shape_of((heads, 1, frames), f32),
        ],
        compiler_params=params(),
        cost_estimate=cost(8.7),
        name="self_forward",
    )(turned, turned, turned, front_keys, front_values)


def self_backward(turned, grads, mixed, logsum, front_keys, front_values, cosine, sine):
    heads = front_keys.shape[0] // HEAD_DIM
    frames = turned.shape[1]

    def at(third):
        return pl.BlockSpec((HEAD_DIM, frames), lambda h: (third * heads + h, 0))

    column = pl.BlockSpec((HEAD_DIM, 1), lambda h: (h, 0))
    size = lax.axis_size("mp")
    blocks = pl.BlockSpec((size, HEAD_DIM, frames // size), lambda h: (0, h, 0))
    angles = pl.BlockSpec((HALF, frames), lambda h: (0, 0))
    return pl.pallas_call(
        functools.partial(self_backward_kernel, min(256, frames)),
        grid=(heads,),
        in_specs=[
            at(0),
            at(1),
            at(2),
            blocks,
            blocks,
            pl.BlockSpec((1, 1, frames), lambda h: (h, 0, 0)),
            column,
            column,
            angles,
            angles,
        ],
        out_specs=[
            pl.BlockSpec((3, HEAD_DIM, frames), lambda h: (0, h, 0)),
            column,
            column,
        ],
        out_shape=[
            shape_of((3, heads * HEAD_DIM, frames), bf16),
            shape_of((heads * HEAD_DIM, 1), bf16),
            shape_of((heads * HEAD_DIM, 1), bf16),
        ],
        compiler_params=params(),
        cost_estimate=cost(45),
        name="self_backward",
    )(turned, turned, turned, grads, mixed, logsum, front_keys, front_values, cosine, sine)


def block_refs(refs, size):
    if len(refs) == size:
        return [[ref] for ref in refs]
    return [refs[0:1], refs[1:2], refs[2:3], refs[3:5]]


def block_value(refs):
    parts = [ref[...] for ref in refs]
    return parts[0] if len(parts) == 1 else jnp.concatenate(parts, axis=0)


def whole_specs(arrays):
    return [pl.BlockSpec(array.shape, lambda j, *_: (0, 0)) for array in arrays]


def project_kernel(
    size, given, heads, n_ref, p_ref, norm_ref, wq_ref, wk_ref, wv_ref, cos_ref, sin_ref, *refs
):
    d_ref, x_ref, front_ref, w_ref = refs[-4:]
    blocks = block_refs(refs[:given], size)
    local = heads * HEAD_DIM

    @pl.when(pl.program_id(0) == 0)
    def _():
        for third, ref in enumerate((wq_ref, wk_ref, wv_ref)):
            w_ref[third * local : (third + 1) * local] = ref[...].T
        prefix = norm_forward(p_ref[...], norm_ref[0:1], norm_ref[1:2])[0].astype(bf16)
        front_ref[...] = dot(w_ref[local:], prefix, 1, 1).astype(bf16)

    for k in range(size):

        @pl.when(pl.program_id(0) == k)
        def _(k=k):
            frames = block_value(blocks[k])
            x_ref[0] = frames
            raw = dot(w_ref[...], frames, 1, 1)
            cosine = cos_ref[...]
            sine = sin_ref[...]
            for head in range(2 * heads):
                at = head * HEAD_DIM
                upper = raw[at : at + HALF]
                lower = raw[at + HALF : at + HEAD_DIM]
                first = upper * cosine - lower * sine
                second = lower * cosine + upper * sine
                if head < heads:
                    first, second = first * FACTOR, second * FACTOR
                d_ref[at : at + HALF] = first.astype(bf16)
                d_ref[at + HALF : at + HEAD_DIM] = second.astype(bf16)
            d_ref[2 * local :] = raw[2 * local :].astype(bf16)


def project(clip, count, order, picked, norms, pieces, weights, cosine, sine, earlier):
    size = lax.axis_size("mp")
    width, local = weights[0].shape
    depth = 3 * local
    rows = pieces[0].shape[0]
    angles = pl.BlockSpec((HALF, rows), lambda k, n: (0, n[k]))
    return pl.pallas_call(
        functools.partial(project_kernel, size, len(pieces), local // HEAD_DIM),
        grid_spec=pltpu.PrefetchScalarGridSpec(
            num_scalar_prefetch=1,
            grid=(size,),
            in_specs=whole_specs([picked, norms] + weights)
            + [angles, angles]
            + whole_specs(pieces)
            + [pl.BlockSpec(memory_space=pl.ANY)] * len(earlier),
            out_specs=[
                pl.BlockSpec((depth, rows), lambda k, n: (0, n[k])),
                pl.BlockSpec((1, rows, width), lambda k, n: (clip, n[k], 0)),
                pl.BlockSpec((2 * local, picked.shape[0]), lambda k, n: (0, 0)),
            ],
            scratch_shapes=[pltpu.VMEM((depth, width), bf16)],
        ),
        out_shape=[
            shape_of((depth, size * rows), bf16),
            shape_of((count, size * rows, width), bf16),
            shape_of((2 * local, picked.shape[0]), bf16),
        ],
        input_output_aliases={8 + len(pieces): 1} if earlier else {},
        compiler_params=params(),
        cost_estimate=cost(8),
        name="project",
    )(order, picked, norms, *weights, cosine, sine, *pieces, *earlier)


def glu_kernel(size, given, n_ref, gate_ref, up_ref, down_ref, *refs):
    h_ref, dg_ref, du_ref, x_ref, c_ref = refs[-5:]
    blocks = block_refs(refs[:given], size)
    grads = block_refs(refs[given : 2 * given], size)
    rows = h_ref.shape[1] // size

    @pl.when(pl.program_id(0) == 0)
    def _():
        for k in range(size):
            there = pl.ds(pl.multiple_of(n_ref[k] * rows, rows), rows)
            x_ref[0, there] = block_value(blocks[k])
            c_ref[0, there] = block_value(grads[k])

    for k in range(size):
        frames = block_value(blocks[k])
        there = pl.ds(pl.multiple_of(n_ref[k] * rows, rows), rows)
        gate = dot(frames, gate_ref[...], 1, 0)
        upper = dot(frames, up_ref[...], 1, 0)
        grad_hidden = dot(block_value(grads[k]), down_ref[...], 1, 1)
        sigma = 1.0 / (1.0 + jnp.exp(-gate))
        silu = gate * sigma
        h_ref[0, there] = (silu * upper).astype(bf16)
        dg_ref[0, there] = (grad_hidden * upper * (sigma + silu * (1.0 - sigma))).astype(bf16)
        du_ref[0, there] = (grad_hidden * silu).astype(bf16)


def glu(clip, count, order, pieces, grads, w_gate, w_up, w_down, earlier):
    size = lax.axis_size("mp")
    width, hidden = w_gate.shape
    rows = size * pieces[0].shape[0]
    block = 256
    columns = pl.BlockSpec((width, block), lambda j: (0, j))
    out = pl.BlockSpec((1, rows, block), lambda j: (clip, 0, j))
    whole = pl.BlockSpec((1, rows, width), lambda j: (clip, 0, 0))
    return pl.pallas_call(
        functools.partial(glu_kernel, size, len(pieces)),
        grid=(hidden // block,),
        in_specs=[
            pl.BlockSpec(memory_space=pltpu.SMEM),
            columns,
            columns,
            pl.BlockSpec((block, width), lambda j: (j, 0)),
        ]
        + whole_specs(pieces)
        + whole_specs(grads)
        + [pl.BlockSpec(memory_space=pl.ANY)] * len(earlier),
        out_specs=[out, out, out, whole, whole],
        out_shape=[shape_of((count, rows, hidden), bf16)] * 3
        + [shape_of((count, rows, width), bf16)] * 2,
        input_output_aliases={4 + 2 * len(pieces) + i: i for i in range(len(earlier))},
        compiler_params=params(),
        cost_estimate=cost(22),
        name="glu",
    )(order, w_gate, w_up, w_down, *pieces, *grads, *earlier)


def glu_back_kernel(dg_ref, du_ref, gate_ref, up_ref, o_ref):
    size, rows, _ = o_ref.shape
    for k in range(size):
        part = slice(k * rows, (k + 1) * rows)
        back = dot(dg_ref[0, part], gate_ref[...], 1, 1) + dot(du_ref[0, part], up_ref[...], 1, 1)
        o_ref[k] = back.astype(bf16)


def glu_back(clip, grad_gate, grad_upper, w_gate, w_up):
    size = lax.axis_size("mp")
    _, frames, hidden = grad_gate.shape
    rows = frames // size
    width = w_gate.shape[0]
    block = 256
    whole = pl.BlockSpec((1, frames, hidden), lambda j: (clip, 0, 0))
    part = pl.BlockSpec((block, hidden), lambda j: (j, 0))
    return pl.pallas_call(
        glu_back_kernel,
        grid=(width // block,),
        in_specs=[whole, whole, part, part],
        out_specs=pl.BlockSpec((size, rows, block), lambda j: (0, 0, j)),
        out_shape=shape_of((size, rows, width), bf16),
        compiler_params=params(),
        cost_estimate=cost(14.5),
        name="glu_back",
    )(grad_gate, grad_upper, w_gate, w_up)


def whole_grad_kernel(chips, n, count, given, core_ref, *refs):
    o_ref = refs[-2] if not given else refs[-1]
    turned_ref = refs[-1] if not given else refs[0]
    y_refs = refs[1:] if given else refs[n * count :]
    depth = o_ref.shape[3]

    if not given:

        @pl.when(pl.program_id(0) == 0)
        def _():
            for w in range(n):
                parts = [ref[...] for ref in refs[w * count : (w + 1) * count]]
                turned_ref[w] = jnp.concatenate(parts, axis=0).T

    for w in range(n):
        right = jnp.concatenate([ref[...] for ref in y_refs[w * count : (w + 1) * count]], axis=1)
        for z in range(chips):
            at = pl.multiple_of((2 * z + core_ref[0]) * depth, depth)
            result = dot(turned_ref[w, pl.ds(at, depth)], right, 1, 1)
            if given:
                result = result + refs[1 + n * count][0, z, w].astype(f32)
            o_ref[0, z, w] = result.astype(bf16)


def whole_grad(core, groups, lefts, rights, earlier):
    size = lax.axis_size("mp")
    n = len(rights)
    count = len(rights[0])
    rows = rights[0][0].shape[1]
    local = rights[0][0].shape[0] // size
    width = lefts.shape[1] if earlier else lefts[0][0].shape[1]
    chips = groups // 2
    depth = width // groups
    out = pl.BlockSpec((1, chips, n, depth, local), lambda m: (m, 0, 0, 0, 0))
    turned = pl.BlockSpec((n, width, count * rows), lambda m: (0, 0, 0))
    right = pl.BlockSpec((local, rows), lambda m: (m, 0))
    left = pl.BlockSpec((rows, width), lambda m: (0, 0))
    out_shape = shape_of((size, chips, n, depth, local), bf16)
    turned_shape = shape_of((n, width, count * rows), bf16)
    rights = [array for pair in rights for array in pair]
    lefts = [lefts] if earlier else [array for pair in lefts for array in pair]
    return pl.pallas_call(
        functools.partial(whole_grad_kernel, chips, n, count, len(earlier)),
        grid=(size,),
        in_specs=[pl.BlockSpec(memory_space=pltpu.SMEM)]
        + [turned if earlier else left] * len(lefts)
        + [right] * len(rights)
        + [out] * len(earlier),
        out_specs=out if earlier else [out, turned],
        out_shape=out_shape if earlier else [out_shape, turned_shape],
        compiler_params=params(),
        cost_estimate=cost(30),
        name="whole_grad",
    )(core, *lefts, *rights, *earlier)


def branch_kernel(x_ref, w_ref, o_ref):
    o_ref[0, 0] = dot(x_ref[0], w_ref[...], 1, 0).astype(bf16)


def branch_blocks(hidden, w_down):
    size = lax.axis_size("mp")
    count, frames, depth = hidden.shape
    width = w_down.shape[1]
    rows = frames // size
    return pl.pallas_call(
        branch_kernel,
        grid=(count, size),
        in_specs=[
            pl.BlockSpec((1, rows, depth), lambda b, k: (b, k, 0)),
            pl.BlockSpec((depth, width), lambda b, k: (0, 0)),
        ],
        out_specs=pl.BlockSpec((1, 1, rows, width), lambda b, k: (k, b, 0, 0)),
        out_shape=shape_of((size, count, rows, width), bf16),
        compiler_params=params(),
        cost_estimate=cost(13.2),
        name="branch",
    )(hidden, w_down)


def weight_grad_kernel(x_ref, g_ref, o_ref):
    o_ref[...] = dot(x_ref[...], g_ref[...], 0, 0).astype(bf16)


def weight_grad(frames, grads):
    frames = frames.reshape(-1, frames.shape[-1])
    grads = grads.reshape(-1, grads.shape[-1])
    rows, width = frames.shape
    hidden = grads.shape[1]
    block = 256
    return pl.pallas_call(
        weight_grad_kernel,
        grid=(width // block,),
        in_specs=[
            pl.BlockSpec((rows, block), lambda i: (0, i)),
            pl.BlockSpec((rows, hidden), lambda i: (0, 0)),
        ],
        out_specs=pl.BlockSpec((block, hidden), lambda i: (i, 0)),
        out_shape=shape_of((width, hidden), bf16),
        compiler_params=params(),
        cost_estimate=cost(10),
        name="weight_grad",
    )(frames, grads)


def self_weight_grad_kernel(count, x_ref, p_ref, f_ref, *refs):
    d_refs = refs[:count]
    w_refs = refs[count : count + 3]
    o_ref, gain_ref, shift_ref, sum_ref = refs[count + 3 :]
    local = w_refs[0].shape[1]

    @pl.when(pl.program_id(0) == 0)
    def _():
        ones = jnp.ones((8, x_ref.shape[1]), bf16)
        for third in range(3):
            part = slice(third * local, (third + 1) * local)
            sums = jnp.zeros((8, local), f32)
            for b in range(count):
                sums = sums + dot(ones, d_refs[b][third], 1, 1) + f_ref[b : b + 1, part]
            sum_ref[:, part] = sums

    gain = jnp.zeros(gain_ref.shape, f32)
    shift = jnp.zeros(shift_ref.shape, f32)
    result = jnp.zeros((x_ref.shape[2], 3 * local), f32)
    for b in range(count):
        grads = d_refs[b][...].reshape(3 * local, -1)
        result = result + dot(x_ref[b], grads, 0, 1) + p_ref[:, b : b + 1] * f_ref[b : b + 1]
    o_ref[...] = result.astype(bf16)
    for third in range(3):
        part = slice(third * local, (third + 1) * local)
        weight = w_refs[third][...].astype(f32)
        gain = gain + jnp.sum(weight * result[:, part], axis=1, keepdims=True)
        shift = shift + jnp.sum(weight * sum_ref[0:1, part], axis=1, keepdims=True)
    gain_ref[...] = gain
    shift_ref[...] = shift


def self_weight_grad(frames, prefix, grads, front, weights):
    count, rows, width = frames.shape
    local = grads[0].shape[1]
    depth = 3 * local
    block = 256
    weight = pl.BlockSpec((block, local), lambda i: (i, 0))
    column = pl.BlockSpec((block, 1), lambda i: (i, 0))
    return pl.pallas_call(
        functools.partial(self_weight_grad_kernel, count),
        grid=(width // block,),
        in_specs=[
            pl.BlockSpec((count, rows, block), lambda i: (0, 0, i)),
            pl.BlockSpec((block, count), lambda i: (i, 0)),
            pl.BlockSpec((count, depth), lambda i: (0, 0)),
        ]
        + [pl.BlockSpec((3, local, rows), lambda i: (0, 0, 0))] * count
        + [weight] * 3,
        out_specs=[pl.BlockSpec((block, depth), lambda i: (i, 0)), column, column],
        out_shape=[shape_of((width, depth), bf16)] + [shape_of((width, 1), f32)] * 2,
        scratch_shapes=[pltpu.VMEM((8, depth), f32)],
        compiler_params=params(),
        cost_estimate=cost(12),
        name="self_weight_grad",
    )(frames, prefix.T.astype(f32), front.astype(f32), *grads, *weights)


def self_back_kernel(d_ref, wq_ref, wk_ref, wv_ref, o_ref):
    local = wq_ref.shape[1]
    back = jnp.zeros(o_ref.shape[1:], f32)
    for third, ref in enumerate((wq_ref, wk_ref, wv_ref)):
        back = back + dot(d_ref[third], ref[...], 0, 1)
    o_ref[0] = back.astype(bf16)


def self_back(grads, weights):
    size = lax.axis_size("mp")
    _, local, frames = grads.shape
    width = weights[0].shape[0]
    rows = frames // size
    return pl.pallas_call(
        self_back_kernel,
        grid=(size,),
        in_specs=[pl.BlockSpec((3, local, rows), lambda k: (0, 0, k))] + whole_specs(weights),
        out_specs=pl.BlockSpec((1, rows, width), lambda k: (k, 0, 0)),
        out_shape=shape_of((size, rows, width), bf16),
        compiler_params=params(),
        cost_estimate=cost(7),
        name="self_back",
    )(grads, *weights)


def turning(frames):
    places = (jnp.arange(frames) + 1).astype(f32)
    rates = jnp.exp(jnp.arange(HALF).astype(f32) * (-2.0 * math.log(10000.0) / HEAD_DIM))
    angles = rates[:, None] * places[None, :]
    return (jnp.cos(angles), jnp.sin(angles))


def sum_over_clips(values, axis):
    return lax.psum_scatter(values.astype(bf16), "dp", scatter_dimension=axis, tiled=True)


def shards(
    frames_in,
    prompt,
    lengths,
    tsteps,
    table,
    gain_one,
    shift_one,
    gain_two,
    shift_two,
    gain_three,
    shift_three,
    w_query,
    w_key,
    w_value,
    w_out,
    c_query,
    c_key,
    c_value,
    c_out,
    w_gate,
    w_up,
    w_down,
    cotangent,
):
    size = lax.axis_size("mp")
    groups = lax.axis_size("dp")
    count, rows, width = frames_in.shape
    clips = range(count)
    local = w_query.shape[1]
    here = lax.axis_index("mp")
    there = lax.axis_index("dp")
    core = there & 1
    chain = Chain()
    hold, mark, arrive = chain.hold, chain.mark, chain.arrive

    def joined(parts, axis):
        return jnp.concatenate(parts, axis=axis)

    order = jnp.stack([here ^ k for k in range(size)]).astype(jnp.int32)
    this_core = jnp.stack([core]).astype(jnp.int32)
    depth = width // groups
    side = jnp.stack(
        [
            lax.dynamic_slice_in_dim(c_query, there * depth, depth, 0),
            lax.dynamic_slice_in_dim(c_out, there * depth, depth, 1).T,
        ]
    )
    side = lax.all_gather(side, "mp", axis=0)
    ones, low = [], []
    for b in clips:
        ones.append(norm_forward(hold(frames_in[b]).astype(f32), gain_one, shift_one))
        low.append(ones[b][0].astype(bf16))
        mark(low[b])
        if b == 0:
            spread_one = [Spread(low[0])]
            spread_one[0].first = arrive(spread_one[0].first)
            spread_one[0].second_step()
        else:
            spread_one.append(Spread(low[b]))
    tokens = prompt.reshape(-1, prompt.shape[-1])
    memory = [dot(hold(part), tokens, 0, 1).astype(bf16) for part in (c_key, c_value)]
    mark(*memory)
    memory = joined(memory, 0)
    side = arrive(side)
    c_query_all = lax.all_gather(side[:, 0], "dp", axis=1, tiled=True)
    c_out_all = lax.all_gather(side[:, 1], "dp", axis=1, tiled=True)
    cosine, sine = turning(size * rows)
    picked = [lax.dynamic_slice_in_dim(hold(table), tsteps[b], 1, 0) for b in clips]
    mark(*picked)
    picked = joined(picked + [jnp.ones((8 - count, width), f32)], 0)
    norm_one = jnp.stack([gain_one, shift_one])
    half = lax.dynamic_slice_in_dim(hold(w_out), core * (local // 2), local // 2, 0)
    mark(half)
    spread_one[0].last = arrive(spread_one[0].last)
    for later in spread_one[1:]:
        later.first = arrive(later.first)
        later.second_step()
        later.last = arrive(later.last)
    halves = gathered(hold(half))

    turned, mixed_part, logsum, mixed = [], [], [], []
    frames_one = ()
    weights = [w_query, w_key, w_value]
    for b in clips:
        pieces = hold(spread_one[b].pieces())
        out, frames_one, front = project(
            b, count, order, picked, norm_one, pieces, weights, cosine, sine, list(frames_one)
        )
        frames_one = (frames_one,)
        turned.append(out)
        mark(out)
        if b == 0:
            front_keys = [front[:local, c : c + 1] for c in clips]
            front_values = [front[local:, c : c + 1] for c in clips]
        else:
            memory = hold(memory)
            memory = [memory] + [swap(memory, "mp", k) for k in range(1, size)]
            halves = arrive(halves)
            other = swap(halves, "dp", 1)
            mixed[0] = exchange(hold(mixed[0]))
        out, sums = self_forward(hold(turned[b]), front_keys[b], front_values[b])
        mixed_part.append(out)
        logsum.append(sums)
        mixed.append(out)
        mark(out)
    frames_one = frames_one[0]
    mixed[0] = arrive(mixed[0])
    for b in clips[1:]:
        mixed[b] = exchange(hold(mixed[b]))
    memory = jnp.stack(arrive(memory))
    mark(memory)
    spread_down = [Spread(hold(cotangent[0]))]
    other = arrive(other)
    local_weights = (halves, other, c_query_all, c_out_all)

    norms = jnp.stack([gain_two, shift_two, gain_three, shift_three])
    first, normed_two, cross, second, low, spread_three = [], [], [], [], [], []
    for b in clips:
        mixed[b] = hold(mixed[b]).reshape(size * local, rows)
        parts = local_forward(
            b, count, lengths, this_core, order, mixed[b], frames_in[b], norms, memory, local_weights
        )
        first.append(parts[0])
        second.append(parts[1])
        normed_two.append(parts[2])
        cross.append(parts[3:6])
        low.append(parts[6])
        mark(low[b])
        if b == 0:
            spread_three.append(Spread(low[b]))
            spread_down[0].first = arrive(spread_down[0].first)
            spread_down[0].second_step()

    back_three = []
    parts = ()
    spread_down[0].last = arrive(spread_down[0].last)
    spread_three[0].first = arrive(spread_three[0].first)
    spread_three[0].second_step()
    spread_three.extend(Spread(hold(later)) for later in low[1:])
    spread_three[0].last = arrive(spread_three[0].last)
    spread_down.extend(Spread(hold(later)) for later in cotangent[1:])
    for b in clips:
        pieces = hold(spread_three[b].pieces())
        parts = glu(
            b, count, order, pieces, spread_down[b].pieces(), w_gate, w_up, w_down, list(parts)
        )
        mark(parts[1])
        if b == 0:
            for later in spread_three[1:] + spread_down[1:]:
                later.first = arrive(later.first)
                later.second_step()
        grad_gate, grad_upper = hold((parts[1], parts[2]))
        back = glu_back(b, grad_gate, grad_upper, w_gate, w_up)
        mark(back)
        if b == 0:
            for later in spread_three[1:] + spread_down[1:]:
                later.last = arrive(later.last)
        else:
            back_three[b - 1] = arrive(back_three[b - 1])
        back_three.append(exchange(hold(back)))

    hidden, grad_gate, grad_upper, frames_three, down_in = parts
    raw_w_down = weight_grad(hold(down_in), hidden)
    grad_w_down = sum_over_clips(raw_w_down, 0)
    mark(raw_w_down)
    branch = branch_blocks(hold(hidden), w_down)
    mark(branch)
    branch = lax.psum_scatter(branch, "mp", scatter_dimension=0, tiled=True)[0]
    raw_w_gate = weight_grad(hold(frames_three), grad_gate)
    grad_w_gate = sum_over_clips(raw_w_gate, 0)
    mark(raw_w_gate)

    grad_one, cross_in, self_in = [], [], []
    grad_cross_query, grad_memory, grad_mixed, norm_terms = [], [], [], []
    for b in clips:
        if b:
            back_three[b] = arrive(back_three[b])
            grad_mixed[b - 1] = exchange(hold(grad_mixed[b - 1]))
        parts = local_backward(
            b,
            count,
            lengths,
            this_core,
            order,
            hold(back_three[b]),
            cotangent[b],
            first[b],
            second[b],
            cross[b],
            norms,
            memory,
            local_weights,
        )
        cross_in.append(parts[0])
        self_in.append(parts[1])
        grad_one.append(parts[2])
        grad_cross_query.append(parts[3])
        grad_memory.append(parts[4])
        norm_terms.append(parts[6])
        mark(parts[5])
        grad_mixed.append(parts[5].reshape(size, local, rows))
    for b in clips[:-1]:
        grad_mixed[b] = arrive(grad_mixed[b])
    grad_mixed[-1] = exchange(hold(grad_mixed[-1]))

    grad_memory = Settle(joined(hold(grad_memory), 2))
    mark(*grad_memory.mine)
    grad_memory = grad_memory.second_step()
    rights = (grad_cross_query, [part[1] for part in cross], mixed)
    other_raws, lefts = whole_grad(
        1 - this_core, groups, (normed_two, hold(cross_in), self_in), rights, []
    )
    mark(other_raws)
    other_raws = swap(other_raws, "dp", 1)
    raw_w_up = weight_grad(hold(frames_three), grad_upper)
    grad_w_up = sum_over_clips(raw_w_up, 0)
    mark(raw_w_up)
    raws = whole_grad(this_core, groups, lefts, rights, [arrive(other_raws)])
    mark(raws)
    raws = Settle(hold(raws).reshape(size, -1, local))
    mark(*raws.mine)
    raws.first_step()

    grad_self, grad_front, back_one = [], [], []
    for b in clips:
        grads, grad_front_key, grad_front_value = self_backward(
            turned[b],
            hold(grad_mixed[b]),
            mixed_part[b],
            logsum[b],
            front_keys[b],
            front_values[b],
            cosine,
            sine,
        )
        grad_self.append(grads)
        grad_front.append(joined([grad_front_key, grad_front_value], 0))
        mark(grads)
        if b + 1 < count:
            grad_mixed[b + 1] = arrive(grad_mixed[b + 1])
            raws.came = arrive(raws.came)
            raws.add()
            mark(*raws.mine)
            raws = raws.second_step()
            back = self_back(hold(grad_self[b]), weights)
            mark(back)
            back_one.append(exchange(hold(back)))
            grad_memory = total(arrive(grad_memory)).astype(bf16)
            low_memory = [
                dot(tokens, part, 0, 1).astype(bf16) for part in jnp.split(grad_memory, 2, axis=0)
            ]
            mark(*low_memory)
            low_memory = [part.reshape(groups, -1, local) for part in low_memory]
            mine, other = core_half(joined(low_memory, 1))

    raws = total(arrive(raws)).astype(bf16).reshape(groups // 2, 3, -1, local)
    memory_half = plus(mine, arrive(other))
    mark(raws, memory_half)
    raws = joined([raws, memory_half[:, None]], 1)
    cores = [list(range(c, groups, 2)) for c in range(2)]
    raws = lax.psum_scatter(raws, "dp", scatter_dimension=0, axis_index_groups=cores, tiled=True)[0]
    prefix_normed, prefix_normal, prefix_scale = norm_forward(
        picked[:count], gain_one, shift_one
    )
    prefix_low = prefix_normed.astype(bf16)
    grad_front = joined(grad_front, 1)
    wide_front = joined([jnp.zeros((count, local), bf16), grad_front.T], 1)
    low_w_self, gain_term, shift_term = self_weight_grad(
        frames_one, prefix_low, hold(grad_self), wide_front, weights
    )
    grad_w_self = sum_over_clips(low_w_self, 0)
    mark(low_w_self)
    back = self_back(hold(grad_self[-1]), weights)
    mark(back)
    back_one = arrive(back_one)
    back_one.append(exchange(hold(back)))

    def wide(value):
        return value.astype(f32)

    small = []
    gain_term, shift_term = gain_term[:, 0], shift_term[:, 0]
    small.append((gain_term - shift_one * shift_term) / gain_one)
    small.append(shift_term)
    norm_terms = sum(norm_terms[1:], norm_terms[0])
    steps = jnp.where(here == 0, tsteps, 0).astype(f32)
    steps = lax.dynamic_update_slice(jnp.zeros((width,), f32), steps, (there * count,))

    back_prefix = dot(grad_front[:local], w_key, 0, 1) + dot(grad_front[local:], w_value, 0, 1)
    grad_picked = norm_backward(back_prefix, prefix_normal, prefix_scale, gain_one)
    spots = jnp.arange(groups)[:, None, None] == there
    spots = jnp.where(spots, grad_picked[None], 0.0).reshape(groups * count, width)
    small = hold(joined([jnp.stack(small), norm_terms, steps[None], spots], 0))
    small = all_sum(small)
    all_steps = small[6, : groups * count]
    matches = jnp.arange(table.shape[0])[:, None].astype(f32) == all_steps[None, :]
    grad_table = jnp.dot(matches.astype(f32), small[7:], precision=lax.Precision.HIGHEST)

    mark(small)
    back_one[-1] = arrive(back_one[-1])
    back_one = [total(terms) for terms in back_one]
    grad_frames = [
        grad_one[b] + norm_backward(back_one[b], ones[b][1], ones[b][2], gain_one) for b in clips
    ]
    mark(grad_table, *grad_frames)
    grad_w_down = wide(arrive(grad_w_down).T)
    branch = arrive(branch)
    output = [second[b] + branch[b].astype(f32) for b in clips]
    grad_w_gate = wide(arrive(grad_w_gate))
    grad_w_up = arrive(grad_w_up)
    raws = arrive(raws).astype(f32)
    grad_w_self = arrive(grad_w_self)

    depth_c = prompt.shape[-1] // groups

    return (
        jnp.stack(output),
        jnp.stack(grad_frames),
        grad_table,
        small[0],
        small[1],
        small[2],
        small[3],
        small[4],
        small[5],
        wide(grad_w_self[:, :local]),
        wide(grad_w_self[:, local : 2 * local]),
        wide(grad_w_self[:, 2 * local :]),
        raws[2].T,
        raws[0],
        raws[3, :depth_c],
        raws[3, depth_c:],
        raws[1].T,
        grad_w_gate,
        wide(grad_w_up),
        grad_w_down,
    )


def solution(mesh):
    placed = (
        P("dp", "mp", None),
        P("dp", None, None),
        P("dp"),
        P("dp"),
        P(),
        P(),
        P(),
        P(),
        P(),
        P(),
        P(),
        P(None, "mp"),
        P(None, "mp"),
        P(None, "mp"),
        P("mp", None),
        P(None, "mp"),
        P(None, "mp"),
        P(None, "mp"),
        P("mp", None),
        P(None, "mp"),
        P(None, "mp"),
        P("mp", None),
        P("dp", "mp", None),
    )
    return jax.shard_map(
        shards,
        mesh=mesh,
        in_specs=placed,
        out_specs=(
            P("dp", "mp", None),
            P("dp", "mp", None),
            P(),
            P(),
            P(),
            P(),
            P(),
            P(),
            P(),
            P("dp", "mp"),
            P("dp", "mp"),
            P("dp", "mp"),
            P("mp", "dp"),
            P("dp", "mp"),
            P("dp", "mp"),
            P("dp", "mp"),
            P("mp", "dp"),
            P("dp", "mp"),
            P("dp", "mp"),
            P("mp", "dp"),
        ),
        check_vma=False,
    )
```

```python
import functools
import math

import jax
import jax.numpy as jnp
from jax import lax
from jax.experimental import pallas as pl
from jax.experimental.pallas import tpu as pltpu
from jax.sharding import PartitionSpec as P

HEAD_DIM = 64
HALF = HEAD_DIM // 2
FACTOR = 1.0 / math.sqrt(HEAD_DIM)

norm_eps = 1e-05

f32 = jnp.float32
bf16 = jnp.bfloat16


def dot(left, right, left_axis, right_axis):
    return lax.dot_general(
        left, right, (((left_axis,), (right_axis,)), ((), ())), preferred_element_type=f32
    )


def norm_forward(values, gain, shift):
    center = values - jnp.mean(values, axis=-1, keepdims=True)
    scale = lax.rsqrt(jnp.mean(center * center, axis=-1, keepdims=True) + norm_eps)
    normal = center * scale
    return (normal * gain + shift, normal, scale)


def norm_backward(grad, normal, scale, gain):
    inner = grad * gain
    return scale * (
        inner
        - jnp.mean(inner, axis=-1, keepdims=True)
        - normal * jnp.mean(inner * normal, axis=-1, keepdims=True)
    )


def bits_of(size):
    return [1 << place for place in range(size.bit_length() - 1)]


def swap(values, axis, k):
    return lax.ppermute(values, axis, [(i, i ^ k) for i in range(lax.axis_size(axis))])


def after(values, *others):
    return lax.optimization_barrier((values,) + others)[0]


class Spread:
    def __init__(self, values):
        self.values = values
        self.last = ()
        size = lax.axis_size("mp")
        partners = (1, 2) if size == 4 else range(1, size)
        self.first = tuple(swap(values, "mp", k) for k in partners)

    def second_step(self):
        if lax.axis_size("mp") == 4:
            one, two = self.first
            half = one.shape[0] // 2
            self.last = (swap(one[:half], "mp", 2), swap(two[half:], "mp", 1))

    def pieces(self):
        return [self.values, *self.first, *self.last]


def place(blocks, axis):
    here = lax.axis_index("mp")
    step = blocks[0].shape[axis]
    shape = list(blocks[0].shape)
    shape[axis] = step * len(blocks)
    result = jnp.zeros(shape, blocks[0].dtype)
    for k, block in enumerate(blocks):
        result = lax.dynamic_update_slice_in_dim(result, block, (here ^ k) * step, axis)
    return result


def gathered(values):
    return exchange(jnp.broadcast_to(values[None], (lax.axis_size("mp"),) + values.shape))


def exchange(blocks):
    return lax.all_to_all(blocks, "mp", 0, 0)


class Settle:
    def __init__(self, blocks):
        here = lax.axis_index("mp")
        size = blocks.shape[0]
        self.mine = [lax.dynamic_index_in_dim(blocks, here ^ k, 0, False) for k in range(size)]
        self.came = ()

    def first_step(self):
        if len(self.mine) == 4:
            half = self.mine[3].shape[0] // 2
            self.came = (swap(self.mine[3][:half], "mp", 2), swap(self.mine[3][half:], "mp", 1))

    def add(self):
        if len(self.mine) == 4:
            _, one, two, _ = self.mine
            high, low = self.came
            half = high.shape[0]
            one = jnp.concatenate([plus(one[:half], high), one[half:]], axis=0)
            two = jnp.concatenate([two[:half], plus(two[half:], low)], axis=0)
            self.mine = [self.mine[0], one, two]

    def second_step(self):
        return [self.mine[0]] + [swap(self.mine[k], "mp", k) for k in range(1, len(self.mine))]


def plus(left, right):
    return (left.astype(f32) + right.astype(f32)).astype(bf16)


def total(terms):
    result = terms[0].astype(f32)
    for k in range(1, len(terms)):
        result = result + terms[k].astype(f32)
    return result


def all_sum(values):
    for axis in ("dp", "mp"):
        for bit in bits_of(lax.axis_size(axis)):
            values = values + swap(values, axis, bit)
    return values


def core_half(blocks):
    core = lax.axis_index("dp") & 1
    pairs = blocks.reshape((blocks.shape[0] // 2, 2) + blocks.shape[1:])
    mine = lax.dynamic_index_in_dim(pairs, core, 1, False)
    other = lax.dynamic_index_in_dim(pairs, 1 - core, 1, False)
    return (mine, swap(other, "dp", 1))


class Chain:
    def __init__(self):
        self.last = ()

    def hold(self, values):
        return after(values, *self.last) if self.last else values

    def mark(self, *values):
        self.last = values

    def arrive(self, values):
        values = self.hold(values)
        self.mark(values)
        return values


def plus(left, right):
    return (left.astype(f32) + right.astype(f32)).astype(bf16)


def total(terms):
    result = terms[0].astype(f32)
    for term in terms[1:]:
        result = result + term.astype(f32)
    return result


def all_sum(values):
    for axis in ("dp", "mp"):
        for bit in bits_of(lax.axis_size(axis)):
            values = values + swap(values, axis, bit)
    return values


def core_half(blocks):
    core = lax.axis_index("dp") & 1
    pairs = blocks.reshape((blocks.shape[0] // 2, 2) + blocks.shape[1:])
    mine = lax.dynamic_index_in_dim(pairs, core, 1, False)
    other = lax.dynamic_index_in_dim(pairs, 1 - core, 1, False)
    return (mine, swap(other, "dp", 1))


def chips_sum(blocks):
    here = lax.axis_index("dp") >> 1
    mine = [
        lax.dynamic_index_in_dim(blocks, here ^ k, 0, False) for k in range(blocks.shape[0])
    ]
    return total([mine[0]] + [swap(mine[k], "dp", 2 * k) for k in range(1, len(mine))])


def self_forward_kernel(q_ref, k_ref, v_ref, pk_ref, pv_ref, o_ref, l_ref):
    parts = head_parts(q_ref.shape[0])
    scores = [dot(k_ref[part], q_ref[part], 0, 0) for part in parts]
    for head, part in enumerate(parts):
        front = q_ref[part].astype(f32) * pk_ref[part].astype(f32)
        front = jnp.sum(front, axis=0, keepdims=True)
        top = jnp.maximum(jnp.max(scores[head], axis=0, keepdims=True), front)
        weights = jnp.exp(scores[head] - top)
        front_weight = jnp.exp(front - top)
        total = jnp.sum(weights, axis=0, keepdims=True) + front_weight
        mixed = dot(v_ref[part], weights.astype(bf16), 1, 0)
        mixed = mixed + pv_ref[part].astype(f32) * front_weight.astype(bf16).astype(f32)
        mixed = (mixed * (1.0 / total)).astype(bf16)
        frames = o_ref.shape[2]
        for k in range(o_ref.shape[0]):
            o_ref[k, part] = mixed[:, k * frames : (k + 1) * frames]
        l_ref[head] = top + jnp.log(total)


def self_backward_kernel(
    block,
    q_ref,
    k_ref,
    v_ref,
    g_ref,
    o_ref,
    l_ref,
    pk_ref,
    pv_ref,
    cos_ref,
    sin_ref,
    d_ref,
    dpk_ref,
    dpv_ref,
):
    frames = q_ref.shape[1]
    keys = k_ref[...]
    values = v_ref[...]
    front_key = pk_ref[...].astype(f32)
    front_value = pv_ref[...].astype(f32)
    grad_keys = jnp.zeros((HEAD_DIM, frames), f32)
    grad_values = jnp.zeros((HEAD_DIM, frames), f32)
    grad_front_key = jnp.zeros((HEAD_DIM, 1), f32)
    grad_front_value = jnp.zeros((HEAD_DIM, 1), f32)
    whole_grads = jnp.concatenate([g_ref[k] for k in range(g_ref.shape[0])], axis=1)
    whole_mixed = jnp.concatenate([o_ref[k] for k in range(o_ref.shape[0])], axis=1)
    for start in range(0, frames, block):
        part = slice(start, start + block)
        queries = q_ref[:, part]
        grads = whole_grads[:, part]
        wide_queries = queries.astype(f32)
        wide_grads = grads.astype(f32)
        logsum = l_ref[0, :, part]
        mixsum = jnp.sum(whole_mixed[:, part].astype(f32) * wide_grads, axis=0, keepdims=True)
        probs = jnp.exp(dot(keys, queries, 0, 0) - logsum)
        grad_probs = dot(values, grads, 0, 0)
        grad_scores = (probs * (grad_probs - mixsum)).astype(bf16)
        grad_values = grad_values + dot(grads, probs.astype(bf16), 1, 1)
        grad_keys = grad_keys + dot(queries, grad_scores, 1, 1)
        grad_queries = dot(keys, grad_scores, 1, 0)
        front = jnp.exp(jnp.sum(wide_queries * front_key, axis=0, keepdims=True) - logsum)
        grad_front = jnp.sum(wide_grads * front_value, axis=0, keepdims=True)
        grad_front = (front * (grad_front - mixsum)).astype(bf16).astype(f32)
        front = front.astype(bf16).astype(f32)
        grad_front_key += jnp.sum(wide_queries * grad_front, axis=1, keepdims=True)
        grad_front_value += jnp.sum(wide_grads * front, axis=1, keepdims=True)
        grad_queries = (grad_queries + front_key * grad_front) * FACTOR
        cosine = cos_ref[:, part]
        sine = sin_ref[:, part]
        upper, lower = grad_queries[:HALF], grad_queries[HALF:]
        d_ref[0, :HALF, part] = (upper * cosine + lower * sine).astype(bf16)
        d_ref[0, HALF:, part] = (lower * cosine - upper * sine).astype(bf16)
    cosine = cos_ref[...]
    sine = sin_ref[...]
    upper, lower = grad_keys[:HALF], grad_keys[HALF:]
    d_ref[1, :HALF, :] = (upper * cosine + lower * sine).astype(bf16)
    d_ref[1, HALF:, :] = (lower * cosine - upper * sine).astype(bf16)
    d_ref[2] = grad_values.astype(bf16)
    dpk_ref[...] = grad_front_key.astype(bf16)
    dpv_ref[...] = grad_front_value.astype(bf16)


def head_parts(rows):
    return [slice(at, at + HEAD_DIM) for at in range(0, rows, HEAD_DIM)]


def fetch(core, out_halves, out, wholes, targets, sems):
    mine, other = out_halves
    size, half, _ = mine.shape
    copies = []
    for k in range(size):
        for source, part in ((mine, core), (other, 1 - core)):
            at = pl.multiple_of((2 * k + part) * half, 16)
            target = out.at[pl.ds(at, half)]
            copies.append(pltpu.make_async_copy(source.at[k], target, sems.at[len(copies)]))
    first = len(copies)
    for source, target in zip(wholes, targets):
        copies.append(pltpu.make_async_copy(source, target, sems.at[len(copies)]))

    def start_out():
        for copy in copies[:first]:
            copy.start()

    def start_whole(k):
        copies[first + k].start()

    def get_out():
        for copy in copies[:first]:
            copy.wait()
        return out[...]

    def get_whole(k):
        copies[first + k].wait()
        return targets[k]

    return start_out, start_whole, get_out, get_whole


def local_forward_kernel(
    clip, n_ref, core_ref, order_ref, mixed_ref, x_ref, norm_ref, mem_ref, wo_mine, wo_other, cq_hbm, co_hbm, *refs
):
    first_ref, second_ref, two_ref, q_ref, o_ref, l_ref, three_ref, wo, cq, co, sems = refs
    start_out, start_whole, get_out, get_whole = fetch(
        core_ref[0], (wo_mine, wo_other), wo, (cq_hbm, co_hbm), (cq, co), sems
    )
    start_out()
    start_whole(0)
    start_whole(1)
    groups, depth, slots = mem_ref.shape
    local = depth // 2
    live = lax.broadcasted_iota(jnp.int32, (slots, 1), 0) < n_ref[clip]
    first = x_ref[...].astype(f32) + dot(mixed_ref[...], get_out(), 0, 0)
    first_ref[...] = first
    two = norm_forward(first, norm_ref[0:1], norm_ref[1:2])[0].astype(bf16)
    two_ref[...] = two
    weight = get_whole(0)
    for k in range(groups):
        q_ref[k * local : (k + 1) * local] = (dot(two, weight[k], 1, 0) * FACTOR).astype(bf16).T
    for group in range(groups):
        parts = head_parts(local)
        there = order_ref[group]
        at = group * local
        queries = [q_ref[at + p.start : at + p.stop] for p in parts]
        scores = [dot(mem_ref[there, p], q, 0, 0) for p, q in zip(parts, queries)]
        scores = [jnp.where(live, s, -1e30) for s in scores]
        tops = [jnp.max(s, axis=0, keepdims=True) for s in scores]
        weights = [jnp.exp(s - top) for s, top in zip(scores, tops)]
        totals = [jnp.sum(w, axis=0, keepdims=True) for w in weights]
        for head, p in enumerate(parts):
            values = mem_ref[there, local + p.start : local + p.stop]
            mixed = dot(values, weights[head].astype(bf16), 1, 0)
            o_ref[at + p.start : at + p.stop] = (mixed * (1.0 / totals[head])).astype(bf16)
            l_ref[group * len(parts) + head] = tops[head] + jnp.log(totals[head])
    weight = get_whole(1)
    second = first
    for k in range(groups):
        second = second + dot(o_ref[k * local : (k + 1) * local], weight[k], 0, 1)
    second_ref[...] = second
    three_ref[...] = norm_forward(second, norm_ref[2:3], norm_ref[3:4])[0].astype(bf16)


def local_specs(clip, count, rows, width, memory):
    groups, depth, slots = memory.shape
    heads = groups * depth // 2 // HEAD_DIM
    wide = pl.BlockSpec((rows, width), lambda i: (0, 0))
    turned = pl.BlockSpec((width, rows), lambda i: (0, 0))
    sums = pl.BlockSpec((heads, 1, rows), lambda i: (0, 0, 0))
    norms = pl.BlockSpec((4, width), lambda i: (0, 0))
    mem = pl.BlockSpec((groups, depth, slots // count), lambda i: (0, 0, clip))
    return (wide, turned, sums, norms, mem, heads)


def local_forward(clip, count, lengths, core, order, mixed, frames, norms, memory, weights):
    rows, width = frames.shape
    wide, turned, sums, norm_spec, mem, heads = local_specs(clip, count, rows, width, memory)
    return pl.pallas_call(
        functools.partial(local_forward_kernel, clip),
        grid=(1,),
        in_specs=[pl.BlockSpec(memory_space=pltpu.SMEM)] * 3
        + [turned, wide, norm_spec, mem]
        + [pl.BlockSpec(memory_space=pl.ANY)] * 4,
        out_specs=[wide, wide, wide, turned, turned, sums, wide],
        out_shape=[
            shape_of((rows, width), f32),
            shape_of((rows, width), f32),
            shape_of((rows, width), bf16),
            shape_of((width, rows), bf16),
            shape_of((width, rows), bf16),
            shape_of((heads, 1, rows), f32),
            shape_of((rows, width), bf16),
        ],
        scratch_shapes=[pltpu.VMEM((width, width), bf16)]
        + [pltpu.VMEM(weights[2].shape, bf16)] * 2
        + [pltpu.SemaphoreType.DMA((2 * memory.shape[0] + 2,))],
        compiler_params=params(),
        cost_estimate=cost(11.3),
        name="local_forward",
    )(lengths, core, order, mixed, frames, norms, memory, *weights)


def local_backward_kernel(
    clip,
    n_ref,
    core_ref,
    order_ref,
    b_ref,
    cot_ref,
    first_ref,
    second_ref,
    q_ref,
    o_ref,
    l_ref,
    norm_ref,
    mem_ref,
    wo_mine,
    wo_other,
    cq_hbm,
    co_hbm,
    *refs,
):
    cross_ref, self_ref, one_ref, dq_ref, d_ref, g_ref, term_ref, grads_ref, wo, cq, co, sems = refs
    start_out, start_whole, get_out, get_whole = fetch(
        core_ref[0], (wo_mine, wo_other), wo, (cq_hbm, co_hbm), (cq, co), sems
    )
    start_whole(1)
    start_whole(0)
    start_out()
    groups, depth, slots = mem_ref.shape
    local = depth // 2
    heads = local // HEAD_DIM
    live = lax.broadcasted_iota(jnp.int32, (slots, 1), 0) < n_ref[clip]

    back = total([b_ref[k] for k in range(b_ref.shape[0])])
    _, normal, scale = norm_forward(second_ref[...], norm_ref[2:3], norm_ref[3:4])
    term_ref[2:3] = jnp.sum(back * normal, axis=0, keepdims=True)
    term_ref[3:4] = jnp.sum(back, axis=0, keepdims=True)
    grad_two = cot_ref[...].astype(f32) + norm_backward(back, normal, scale, norm_ref[2:3])
    cross_in = grad_two.astype(bf16)
    cross_ref[...] = cross_in
    weight = get_whole(1)
    for k in range(groups):
        grads_ref[k * local : (k + 1) * local] = dot(cross_in, weight[k], 1, 0).astype(bf16).T
    for group in range(groups):
        for head, part in enumerate(head_parts(local)):
            there = slice(group * local + part.start, group * local + part.stop)
            queries = q_ref[there]
            keys = mem_ref[order_ref[group], part]
            grads = grads_ref[there]
            mixsum = jnp.sum(o_ref[there].astype(f32) * grads.astype(f32), axis=0, keepdims=True)
            scores = jnp.where(live, dot(keys, queries, 0, 0), -1e30)
            probs = jnp.exp(scores - l_ref[group * heads + head])
            values = slice(local + part.start, local + part.stop)
            grad_probs = dot(mem_ref[order_ref[group], values], grads, 0, 0)
            grad_scores = (probs * (grad_probs - mixsum)).astype(bf16)
            dq_ref[there] = (dot(keys, grad_scores, 1, 0) * FACTOR).astype(bf16)
            d_ref[group, part] = dot(queries, grad_scores, 1, 1).astype(bf16)
            d_ref[group, values] = dot(grads, probs.astype(bf16), 1, 1).astype(bf16)
    weight = get_whole(0)
    back = jnp.zeros(grad_two.shape, f32)
    for k in range(groups):
        back = back + dot(dq_ref[k * local : (k + 1) * local], weight[k], 0, 1)
    _, normal, scale = norm_forward(first_ref[...], norm_ref[0:1], norm_ref[1:2])
    term_ref[0:1] = jnp.sum(back * normal, axis=0, keepdims=True)
    term_ref[1:2] = jnp.sum(back, axis=0, keepdims=True)
    grad_one = grad_two + norm_backward(back, normal, scale, norm_ref[0:1])
    one_ref[...] = grad_one
    self_in = grad_one.astype(bf16)
    self_ref[...] = self_in
    g_ref[...] = dot(get_out(), self_in, 1, 1).astype(bf16)


def local_backward(
    clip, count, lengths, core, order, back, cotangent, first, second, cross, norms, memory, weights
):
    rows, width = cotangent.shape
    wide, turned, sums, norm_spec, mem, heads = local_specs(clip, count, rows, width, memory)
    groups, depth, slots = memory.shape
    slots = slots // count
    return pl.pallas_call(
        functools.partial(local_backward_kernel, clip),
        grid=(1,),
        in_specs=[
            pl.BlockSpec(memory_space=pltpu.SMEM),
            pl.BlockSpec(memory_space=pltpu.SMEM),
            pl.BlockSpec(memory_space=pltpu.SMEM),
            pl.BlockSpec(back.shape, lambda i: (0, 0, 0)),
            wide,
            wide,
            wide,
            turned,
            turned,
            sums,
            norm_spec,
            mem,
        ]
        + [pl.BlockSpec(memory_space=pl.ANY)] * 4,
        out_specs=[
            wide,
            wide,
            wide,
            turned,
            pl.BlockSpec((groups, depth, slots), lambda i: (0, 0, 0)),
            turned,
            norm_spec,
        ],
        out_shape=[
            shape_of((rows, width), bf16),
            shape_of((rows, width), bf16),
            shape_of((rows, width), f32),
            shape_of((width, rows), bf16),
            shape_of((groups, depth, slots), bf16),
            shape_of((width, rows), bf16),
            shape_of((4, width), f32),
        ],
        scratch_shapes=[pltpu.VMEM((width, rows), bf16)]
        + [pltpu.VMEM((width, width), bf16)]
        + [pltpu.VMEM(weights[2].shape, bf16)] * 2
        + [pltpu.SemaphoreType.DMA((2 * groups + 2,))],
        compiler_params=params(),
        cost_estimate=cost(40),
        name="local_backward",
    )(lengths, core, order, back, cotangent, first, second, *cross, norms, memory, *weights)


def cost(micros):
    micros = 0.4 * micros
    return pl.CostEstimate(
        flops=int(micros * 1.15e9), bytes_accessed=int(micros * 3.6e6), transcendentals=0
    )


def shape_of(shape, kind):
    return jax.ShapeDtypeStruct(shape, kind)


def params():
    return pltpu.CompilerParams(vmem_limit_bytes=60 * 2**20)


def self_forward(turned, front_keys, front_values):
    size = lax.axis_size("mp")
    heads = front_keys.shape[0] // HEAD_DIM
    frames = turned.shape[1]
    step = 3 if heads % 3 == 0 else 1
    rows = step * HEAD_DIM
    steps = heads // step

    def at(third):
        return pl.BlockSpec((rows, frames), lambda h: (third * steps + h, 0))

    column = pl.BlockSpec((rows, 1), lambda h: (h, 0))
    return pl.pallas_call(
        self_forward_kernel,
        grid=(steps,),
        in_specs=[at(0), at(1), at(2), column, column],
        out_specs=[
            pl.BlockSpec((size, rows, frames // size), lambda h: (0, h, 0)),
            pl.BlockSpec((step, 1, frames), lambda h: (h, 0, 0)),
        ],
        out_shape=[
            shape_of((size, heads * HEAD_DIM, frames // size), bf16),
            shape_of((heads, 1, frames), f32),
        ],
        compiler_params=params(),
        cost_estimate=cost(8.7),
        name="self_forward",
    )(turned, turned, turned, front_keys, front_values)


def self_backward(turned, grads, mixed, logsum, front_keys, front_values, cosine, sine):
    heads = front_keys.shape[0] // HEAD_DIM
    frames = turned.shape[1]

    def at(third):
        return pl.BlockSpec((HEAD_DIM, frames), lambda h: (third * heads + h, 0))

    column = pl.BlockSpec((HEAD_DIM, 1), lambda h: (h, 0))
    size = lax.axis_size("mp")
    blocks = pl.BlockSpec((size, HEAD_DIM, frames // size), lambda h: (0, h, 0))
    angles = pl.BlockSpec((HALF, frames), lambda h: (0, 0))
    return pl.pallas_call(
        functools.partial(self_backward_kernel, min(256, frames)),
        grid=(heads,),
        in_specs=[
            at(0),
            at(1),
            at(2),
            blocks,
            blocks,
            pl.BlockSpec((1, 1, frames), lambda h: (h, 0, 0)),
            column,
            column,
            angles,
            angles,
        ],
        out_specs=[
            pl.BlockSpec((3, HEAD_DIM, frames), lambda h: (0, h, 0)),
            column,
            column,
        ],
        out_shape=[
            shape_of((3, heads * HEAD_DIM, frames), bf16),
            shape_of((heads * HEAD_DIM, 1), bf16),
            shape_of((heads * HEAD_DIM, 1), bf16),
        ],
        compiler_params=params(),
        cost_estimate=cost(45),
        name="self_backward",
    )(turned, turned, turned, grads, mixed, logsum, front_keys, front_values, cosine, sine)


def block_refs(refs, size):
    if len(refs) == size:
        return [[ref] for ref in refs]
    return [refs[0:1], refs[1:2], refs[2:3], refs[3:5]]


def block_value(refs):
    parts = [ref[...] for ref in refs]
    return parts[0] if len(parts) == 1 else jnp.concatenate(parts, axis=0)


def whole_specs(arrays):
    return [pl.BlockSpec(array.shape, lambda j, *_: (0, 0)) for array in arrays]


def project_kernel(
    size, given, heads, n_ref, p_ref, norm_ref, wq_ref, wk_ref, wv_ref, cos_ref, sin_ref, *refs
):
    d_ref, x_ref, front_ref, w_ref = refs[-4:]
    blocks = block_refs(refs[:given], size)
    local = heads * HEAD_DIM

    @pl.when(pl.program_id(0) == 0)
    def _():
        for third, ref in enumerate((wq_ref, wk_ref, wv_ref)):
            w_ref[third * local : (third + 1) * local] = ref[...].T
        prefix = norm_forward(p_ref[...], norm_ref[0:1], norm_ref[1:2])[0].astype(bf16)
        front_ref[...] = dot(w_ref[local:], prefix, 1, 1).astype(bf16)

    for k in range(size):

        @pl.when(pl.program_id(0) == k)
        def _(k=k):
            frames = block_value(blocks[k])
            x_ref[0] = frames
            raw = dot(w_ref[...], frames, 1, 1)
            cosine = cos_ref[...]
            sine = sin_ref[...]
            for head in range(2 * heads):
                at = head * HEAD_DIM
                upper = raw[at : at + HALF]
                lower = raw[at + HALF : at + HEAD_DIM]
                first = upper * cosine - lower * sine
                second = lower * cosine + upper * sine
                if head < heads:
                    first, second = first * FACTOR, second * FACTOR
                d_ref[at : at + HALF] = first.astype(bf16)
                d_ref[at + HALF : at + HEAD_DIM] = second.astype(bf16)
            d_ref[2 * local :] = raw[2 * local :].astype(bf16)


def project(clip, count, order, picked, norms, pieces, weights, cosine, sine, earlier):
    size = lax.axis_size("mp")
    width, local = weights[0].shape
    depth = 3 * local
    rows = pieces[0].shape[0]
    angles = pl.BlockSpec((HALF, rows), lambda k, n: (0, n[k]))
    return pl.pallas_call(
        functools.partial(project_kernel, size, len(pieces), local // HEAD_DIM),
        grid_spec=pltpu.PrefetchScalarGridSpec(
            num_scalar_prefetch=1,
            grid=(size,),
            in_specs=whole_specs([picked, norms] + weights)
            + [angles, angles]
            + whole_specs(pieces)
            + [pl.BlockSpec(memory_space=pl.ANY)] * len(earlier),
            out_specs=[
                pl.BlockSpec((depth, rows), lambda k, n: (0, n[k])),
                pl.BlockSpec((1, rows, width), lambda k, n: (clip, n[k], 0)),
                pl.BlockSpec((2 * local, picked.shape[0]), lambda k, n: (0, 0)),
            ],
            scratch_shapes=[pltpu.VMEM((depth, width), bf16)],
        ),
        out_shape=[
            shape_of((depth, size * rows), bf16),
            shape_of((count, size * rows, width), bf16),
            shape_of((2 * local, picked.shape[0]), bf16),
        ],
        input_output_aliases={8 + len(pieces): 1} if earlier else {},
        compiler_params=params(),
        cost_estimate=cost(8),
        name="project",
    )(order, picked, norms, *weights, cosine, sine, *pieces, *earlier)


def glu_kernel(size, given, n_ref, gate_ref, up_ref, down_ref, *refs):
    h_ref, dg_ref, du_ref, x_ref, c_ref = refs[-5:]
    blocks = block_refs(refs[:given], size)
    grads = block_refs(refs[given : 2 * given], size)
    rows = h_ref.shape[1] // size

    @pl.when(pl.program_id(0) == 0)
    def _():
        for k in range(size):
            there = pl.ds(pl.multiple_of(n_ref[k] * rows, rows), rows)
            x_ref[0, there] = block_value(blocks[k])
            c_ref[0, there] = block_value(grads[k])

    for k in range(size):
        frames = block_value(blocks[k])
        there = pl.ds(pl.multiple_of(n_ref[k] * rows, rows), rows)
        gate = dot(frames, gate_ref[...], 1, 0)
        upper = dot(frames, up_ref[...], 1, 0)
        grad_hidden = dot(block_value(grads[k]), down_ref[...], 1, 1)
        sigma = 1.0 / (1.0 + jnp.exp(-gate))
        silu = gate * sigma
        h_ref[0, there] = (silu * upper).astype(bf16)
        dg_ref[0, there] = (grad_hidden * upper * (sigma + silu * (1.0 - sigma))).astype(bf16)
        du_ref[0, there] = (grad_hidden * silu).astype(bf16)


def glu(clip, count, order, pieces, grads, w_gate, w_up, w_down, earlier):
    size = lax.axis_size("mp")
    width, hidden = w_gate.shape
    rows = size * pieces[0].shape[0]
    block = 256
    columns = pl.BlockSpec((width, block), lambda j: (0, j))
    out = pl.BlockSpec((1, rows, block), lambda j: (clip, 0, j))
    whole = pl.BlockSpec((1, rows, width), lambda j: (clip, 0, 0))
    return pl.pallas_call(
        functools.partial(glu_kernel, size, len(pieces)),
        grid=(hidden // block,),
        in_specs=[
            pl.BlockSpec(memory_space=pltpu.SMEM),
            columns,
            columns,
            pl.BlockSpec((block, width), lambda j: (j, 0)),
        ]
        + whole_specs(pieces)
        + whole_specs(grads)
        + [pl.BlockSpec(memory_space=pl.ANY)] * len(earlier),
        out_specs=[out, out, out, whole, whole],
        out_shape=[shape_of((count, rows, hidden), bf16)] * 3
        + [shape_of((count, rows, width), bf16)] * 2,
        input_output_aliases={4 + 2 * len(pieces) + i: i for i in range(len(earlier))},
        compiler_params=params(),
        cost_estimate=cost(22),
        name="glu",
    )(order, w_gate, w_up, w_down, *pieces, *grads, *earlier)


def glu_back_kernel(dg_ref, du_ref, gate_ref, up_ref, o_ref):
    size, rows, _ = o_ref.shape
    for k in range(size):
        part = slice(k * rows, (k + 1) * rows)
        back = dot(dg_ref[0, part], gate_ref[...], 1, 1) + dot(du_ref[0, part], up_ref[...], 1, 1)
        o_ref[k] = back.astype(bf16)


def glu_back(clip, grad_gate, grad_upper, w_gate, w_up):
    size = lax.axis_size("mp")
    _, frames, hidden = grad_gate.shape
    rows = frames // size
    width = w_gate.shape[0]
    block = 256
    whole = pl.BlockSpec((1, frames, hidden), lambda j: (clip, 0, 0))
    part = pl.BlockSpec((block, hidden), lambda j: (j, 0))
    return pl.pallas_call(
        glu_back_kernel,
        grid=(width // block,),
        in_specs=[whole, whole, part, part],
        out_specs=pl.BlockSpec((size, rows, block), lambda j: (0, 0, j)),
        out_shape=shape_of((size, rows, width), bf16),
        compiler_params=params(),
        cost_estimate=cost(14.5),
        name="glu_back",
    )(grad_gate, grad_upper, w_gate, w_up)


def whole_grad_kernel(chips, n, count, given, core_ref, *refs):
    o_ref = refs[-2] if not given else refs[-1]
    turned_ref = refs[-1] if not given else refs[0]
    y_refs = refs[1:] if given else refs[n * count :]
    depth = o_ref.shape[3]

    if not given:

        @pl.when(pl.program_id(0) == 0)
        def _():
            for w in range(n):
                parts = [ref[...] for ref in refs[w * count : (w + 1) * count]]
                turned_ref[w] = jnp.concatenate(parts, axis=0).T

    for w in range(n):
        right = jnp.concatenate([ref[...] for ref in y_refs[w * count : (w + 1) * count]], axis=1)
        for z in range(chips):
            at = pl.multiple_of((2 * z + core_ref[0]) * depth, depth)
            result = dot(turned_ref[w, pl.ds(at, depth)], right, 1, 1)
            if given:
                result = result + refs[1 + n * count][0, z, w].astype(f32)
            o_ref[0, z, w] = result.astype(bf16)


def whole_grad(core, groups, lefts, rights, earlier):
    size = lax.axis_size("mp")
    n = len(rights)
    count = len(rights[0])
    rows = rights[0][0].shape[1]
    local = rights[0][0].shape[0] // size
    width = lefts.shape[1] if earlier else lefts[0][0].shape[1]
    chips = groups // 2
    depth = width // groups
    out = pl.BlockSpec((1, chips, n, depth, local), lambda m: (m, 0, 0, 0, 0))
    turned = pl.BlockSpec((n, width, count * rows), lambda m: (0, 0, 0))
    right = pl.BlockSpec((local, rows), lambda m: (m, 0))
    left = pl.BlockSpec((rows, width), lambda m: (0, 0))
    out_shape = shape_of((size, chips, n, depth, local), bf16)
    turned_shape = shape_of((n, width, count * rows), bf16)
    rights = [array for pair in rights for array in pair]
    lefts = [lefts] if earlier else [array for pair in lefts for array in pair]
    return pl.pallas_call(
        functools.partial(whole_grad_kernel, chips, n, count, len(earlier)),
        grid=(size,),
        in_specs=[pl.BlockSpec(memory_space=pltpu.SMEM)]
        + [turned if earlier else left] * len(lefts)
        + [right] * len(rights)
        + [out] * len(earlier),
        out_specs=out if earlier else [out, turned],
        out_shape=out_shape if earlier else [out_shape, turned_shape],
        compiler_params=params(),
        cost_estimate=cost(30),
        name="whole_grad",
    )(core, *lefts, *rights, *earlier)


def branch_kernel(x_ref, w_ref, o_ref):
    o_ref[0, 0] = dot(x_ref[0], w_ref[...], 1, 0).astype(bf16)


def branch_blocks(hidden, w_down):
    size = lax.axis_size("mp")
    count, frames, depth = hidden.shape
    width = w_down.shape[1]
    rows = frames // size
    return pl.pallas_call(
        branch_kernel,
        grid=(count, size),
        in_specs=[
            pl.BlockSpec((1, rows, depth), lambda b, k: (b, k, 0)),
            pl.BlockSpec((depth, width), lambda b, k: (0, 0)),
        ],
        out_specs=pl.BlockSpec((1, 1, rows, width), lambda b, k: (k, b, 0, 0)),
        out_shape=shape_of((size, count, rows, width), bf16),
        compiler_params=params(),
        cost_estimate=cost(13.2),
        name="branch",
    )(hidden, w_down)


def weight_grad_kernel(x_ref, g_ref, o_ref):
    o_ref[...] = dot(x_ref[...], g_ref[...], 0, 0).astype(bf16)


def weight_grad(frames, grads):
    frames = frames.reshape(-1, frames.shape[-1])
    grads = grads.reshape(-1, grads.shape[-1])
    rows, width = frames.shape
    hidden = grads.shape[1]
    block = 256
    return pl.pallas_call(
        weight_grad_kernel,
        grid=(width // block,),
        in_specs=[
            pl.BlockSpec((rows, block), lambda i: (0, i)),
            pl.BlockSpec((rows, hidden), lambda i: (0, 0)),
        ],
        out_specs=pl.BlockSpec((block, hidden), lambda i: (i, 0)),
        out_shape=shape_of((width, hidden), bf16),
        compiler_params=params(),
        cost_estimate=cost(10),
        name="weight_grad",
    )(frames, grads)


def self_weight_grad_kernel(count, x_ref, p_ref, f_ref, *refs):
    d_refs = refs[:count]
    w_refs = refs[count : count + 3]
    o_ref, gain_ref, shift_ref, sum_ref = refs[count + 3 :]
    local = w_refs[0].shape[1]

    @pl.when(pl.program_id(0) == 0)
    def _():
        ones = jnp.ones((8, x_ref.shape[1]), bf16)
        for third in range(3):
            part = slice(third * local, (third + 1) * local)
            sums = jnp.zeros((8, local), f32)
            for b in range(count):
                sums = sums + dot(ones, d_refs[b][third], 1, 1) + f_ref[b : b + 1, part]
            sum_ref[:, part] = sums

    gain = jnp.zeros(gain_ref.shape, f32)
    shift = jnp.zeros(shift_ref.shape, f32)
    result = jnp.zeros((x_ref.shape[2], 3 * local), f32)
    for b in range(count):
        grads = d_refs[b][...].reshape(3 * local, -1)
        result = result + dot(x_ref[b], grads, 0, 1) + p_ref[:, b : b + 1] * f_ref[b : b + 1]
    o_ref[...] = result.astype(bf16)
    for third in range(3):
        part = slice(third * local, (third + 1) * local)
        weight = w_refs[third][...].astype(f32)
        gain = gain + jnp.sum(weight * result[:, part], axis=1, keepdims=True)
        shift = shift + jnp.sum(weight * sum_ref[0:1, part], axis=1, keepdims=True)
    gain_ref[...] = gain
    shift_ref[...] = shift


def self_weight_grad(frames, prefix, grads, front, weights):
    count, rows, width = frames.shape
    local = grads[0].shape[1]
    depth = 3 * local
    block = 256
    weight = pl.BlockSpec((block, local), lambda i: (i, 0))
    column = pl.BlockSpec((block, 1), lambda i: (i, 0))
    return pl.pallas_call(
        functools.partial(self_weight_grad_kernel, count),
        grid=(width // block,),
        in_specs=[
            pl.BlockSpec((count, rows, block), lambda i: (0, 0, i)),
            pl.BlockSpec((block, count), lambda i: (i, 0)),
            pl.BlockSpec((count, depth), lambda i: (0, 0)),
        ]
        + [pl.BlockSpec((3, local, rows), lambda i: (0, 0, 0))] * count
        + [weight] * 3,
        out_specs=[pl.BlockSpec((block, depth), lambda i: (i, 0)), column, column],
        out_shape=[shape_of((width, depth), bf16)] + [shape_of((width, 1), f32)] * 2,
        scratch_shapes=[pltpu.VMEM((8, depth), f32)],
        compiler_params=params(),
        cost_estimate=cost(12),
        name="self_weight_grad",
    )(frames, prefix.T.astype(f32), front.astype(f32), *grads, *weights)


def self_back_kernel(d_ref, wq_ref, wk_ref, wv_ref, o_ref):
    local = wq_ref.shape[1]
    back = jnp.zeros(o_ref.shape[1:], f32)
    for third, ref in enumerate((wq_ref, wk_ref, wv_ref)):
        back = back + dot(d_ref[third], ref[...], 0, 1)
    o_ref[0] = back.astype(bf16)


def self_back(grads, weights):
    size = lax.axis_size("mp")
    _, local, frames = grads.shape
    width = weights[0].shape[0]
    rows = frames // size
    return pl.pallas_call(
        self_back_kernel,
        grid=(size,),
        in_specs=[pl.BlockSpec((3, local, rows), lambda k: (0, 0, k))] + whole_specs(weights),
        out_specs=pl.BlockSpec((1, rows, width), lambda k: (k, 0, 0)),
        out_shape=shape_of((size, rows, width), bf16),
        compiler_params=params(),
        cost_estimate=cost(7),
        name="self_back",
    )(grads, *weights)


def turning(frames):
    places = (jnp.arange(frames) + 1).astype(f32)
    rates = jnp.exp(jnp.arange(HALF).astype(f32) * (-2.0 * math.log(10000.0) / HEAD_DIM))
    angles = rates[:, None] * places[None, :]
    return (jnp.cos(angles), jnp.sin(angles))


def sum_over_clips(values, axis):
    return lax.psum_scatter(values.astype(bf16), "dp", scatter_dimension=axis, tiled=True)


def shards(
    frames_in,
    prompt,
    lengths,
    tsteps,
    table,
    gain_one,
    shift_one,
    gain_two,
    shift_two,
    gain_three,
    shift_three,
    w_query,
    w_key,
    w_value,
    w_out,
    c_query,
    c_key,
    c_value,
    c_out,
    w_gate,
    w_up,
    w_down,
    cotangent,
):
    size = lax.axis_size("mp")
    groups = lax.axis_size("dp")
    count, rows, width = frames_in.shape
    clips = range(count)
    local = w_query.shape[1]
    here = lax.axis_index("mp")
    there = lax.axis_index("dp")
    core = there & 1
    chain = Chain()
    hold, mark, arrive = chain.hold, chain.mark, chain.arrive

    def joined(parts, axis):
        return jnp.concatenate(parts, axis=axis)

    order = jnp.stack([here ^ k for k in range(size)]).astype(jnp.int32)
    this_core = jnp.stack([core]).astype(jnp.int32)
    depth = width // groups
    side = jnp.stack(
        [
            lax.dynamic_slice_in_dim(c_query, there * depth, depth, 0),
            lax.dynamic_slice_in_dim(c_out, there * depth, depth, 1).T,
        ]
    )
    side = lax.all_gather(side, "mp", axis=0)
    ones, low = [], []
    for b in clips:
        ones.append(norm_forward(hold(frames_in[b]).astype(f32), gain_one, shift_one))
        low.append(ones[b][0].astype(bf16))
        mark(low[b])
        if b == 0:
            spread_one = [Spread(low[0])]
            spread_one[0].first = arrive(spread_one[0].first)
            spread_one[0].second_step()
        else:
            spread_one.append(Spread(low[b]))
    tokens = prompt.reshape(-1, prompt.shape[-1])
    memory = [dot(hold(part), tokens, 0, 1).astype(bf16) for part in (c_key, c_value)]
    mark(*memory)
    memory = joined(memory, 0)
    side = arrive(side)
    c_query_all = lax.all_gather(side[:, 0], "dp", axis=1, tiled=True)
    c_out_all = lax.all_gather(side[:, 1], "dp", axis=1, tiled=True)
    cosine, sine = turning(size * rows)
    picked = [lax.dynamic_slice_in_dim(hold(table), tsteps[b], 1, 0) for b in clips]
    mark(*picked)
    picked = joined(picked + [jnp.ones((8 - count, width), f32)], 0)
    norm_one = jnp.stack([gain_one, shift_one])
    half = lax.dynamic_slice_in_dim(hold(w_out), core * (local // 2), local // 2, 0)
    mark(half)
    spread_one[0].last = arrive(spread_one[0].last)
    for later in spread_one[1:]:
        later.first = arrive(later.first)
        later.second_step()
        later.last = arrive(later.last)
    halves = gathered(hold(half))

    turned, mixed_part, logsum, mixed = [], [], [], []
    frames_one = ()
    weights = [w_query, w_key, w_value]
    for b in clips:
        pieces = hold(spread_one[b].pieces())
        out, frames_one, front = project(
            b, count, order, picked, norm_one, pieces, weights, cosine, sine, list(frames_one)
        )
        frames_one = (frames_one,)
        turned.append(out)
        mark(out)
        if b == 0:
            front_keys = [front[:local, c : c + 1] for c in clips]
            front_values = [front[local:, c : c + 1] for c in clips]
        else:
            memory = hold(memory)
            memory = [memory] + [swap(memory, "mp", k) for k in range(1, size)]
            halves = arrive(halves)
            other = swap(halves, "dp", 1)
            mixed[0] = exchange(hold(mixed[0]))
        out, sums = self_forward(hold(turned[b]), front_keys[b], front_values[b])
        mixed_part.append(out)
        logsum.append(sums)
        mixed.append(out)
        mark(out)
    frames_one = frames_one[0]
    mixed[0] = arrive(mixed[0])
    for b in clips[1:]:
        mixed[b] = exchange(hold(mixed[b]))
    memory = jnp.stack(arrive(memory))
    mark(memory)
    spread_down = [Spread(hold(cotangent[0]))]
    other = arrive(other)
    local_weights = (halves, other, c_query_all, c_out_all)

    norms = jnp.stack([gain_two, shift_two, gain_three, shift_three])
    first, normed_two, cross, second, low, spread_three = [], [], [], [], [], []
    for b in clips:
        mixed[b] = hold(mixed[b]).reshape(size * local, rows)
        parts = local_forward(
            b, count, lengths, this_core, order, mixed[b], frames_in[b], norms, memory, local_weights
        )
        first.append(parts[0])
        second.append(parts[1])
        normed_two.append(parts[2])
        cross.append(parts[3:6])
        low.append(parts[6])
        mark(low[b])
        if b == 0:
            spread_three.append(Spread(low[b]))
            spread_down[0].first = arrive(spread_down[0].first)
            spread_down[0].second_step()

    back_three = []
    parts = ()
    spread_down[0].last = arrive(spread_down[0].last)
    spread_three[0].first = arrive(spread_three[0].first)
    spread_three[0].second_step()
    spread_three.extend(Spread(hold(later)) for later in low[1:])
    spread_three[0].last = arrive(spread_three[0].last)
    spread_down.extend(Spread(hold(later)) for later in cotangent[1:])
    for b in clips:
        pieces = hold(spread_three[b].pieces())
        parts = glu(
            b, count, order, pieces, spread_down[b].pieces(), w_gate, w_up, w_down, list(parts)
        )
        mark(parts[1])
        if b == 0:
            for later in spread_three[1:] + spread_down[1:]:
                later.first = arrive(later.first)
                later.second_step()
        grad_gate, grad_upper = hold((parts[1], parts[2]))
        back = glu_back(b, grad_gate, grad_upper, w_gate, w_up)
        mark(back)
        if b == 0:
            for later in spread_three[1:] + spread_down[1:]:
                later.last = arrive(later.last)
        else:
            back_three[b - 1] = arrive(back_three[b - 1])
        back_three.append(exchange(hold(back)))

    hidden, grad_gate, grad_upper, frames_three, down_in = parts
    raw_w_down = weight_grad(hold(down_in), hidden)
    grad_w_down = sum_over_clips(raw_w_down, 0)
    mark(raw_w_down)
    branch = branch_blocks(hold(hidden), w_down)
    mark(branch)
    branch = lax.psum_scatter(branch, "mp", scatter_dimension=0, tiled=True)[0]
    raw_w_gate = weight_grad(hold(frames_three), grad_gate)
    grad_w_gate = sum_over_clips(raw_w_gate, 0)
    mark(raw_w_gate)

    grad_one, cross_in, self_in = [], [], []
    grad_cross_query, grad_memory, grad_mixed, norm_terms = [], [], [], []
    for b in clips:
        if b:
            back_three[b] = arrive(back_three[b])
            grad_mixed[b - 1] = exchange(hold(grad_mixed[b - 1]))
        parts = local_backward(
            b,
            count,
            lengths,
            this_core,
            order,
            hold(back_three[b]),
            cotangent[b],
            first[b],
            second[b],
            cross[b],
            norms,
            memory,
            local_weights,
        )
        cross_in.append(parts[0])
        self_in.append(parts[1])
        grad_one.append(parts[2])
        grad_cross_query.append(parts[3])
        grad_memory.append(parts[4])
        norm_terms.append(parts[6])
        mark(parts[5])
        grad_mixed.append(parts[5].reshape(size, local, rows))
    for b in clips[:-1]:
        grad_mixed[b] = arrive(grad_mixed[b])
    grad_mixed[-1] = exchange(hold(grad_mixed[-1]))

    grad_memory = Settle(joined(hold(grad_memory), 2))
    mark(*grad_memory.mine)
    grad_memory = grad_memory.second_step()
    rights = (grad_cross_query, [part[1] for part in cross], mixed)
    other_raws, lefts = whole_grad(
        1 - this_core, groups, (normed_two, hold(cross_in), self_in), rights, []
    )
    mark(other_raws)
    other_raws = swap(other_raws, "dp", 1)
    raw_w_up = weight_grad(hold(frames_three), grad_upper)
    grad_w_up = sum_over_clips(raw_w_up, 0)
    mark(raw_w_up)
    raws = whole_grad(this_core, groups, lefts, rights, [arrive(other_raws)])
    mark(raws)
    raws = Settle(hold(raws).reshape(size, -1, local))
    mark(*raws.mine)
    raws.first_step()

    grad_self, grad_front, back_one = [], [], []
    for b in clips:
        grads, grad_front_key, grad_front_value = self_backward(
            turned[b],
            hold(grad_mixed[b]),
            mixed_part[b],
            logsum[b],
            front_keys[b],
            front_values[b],
            cosine,
            sine,
        )
        grad_self.append(grads)
        grad_front.append(joined([grad_front_key, grad_front_value], 0))
        mark(grads)
        if b + 1 < count:
            grad_mixed[b + 1] = arrive(grad_mixed[b + 1])
            raws.came = arrive(raws.came)
            raws.add()
            mark(*raws.mine)
            raws = raws.second_step()
            back = self_back(hold(grad_self[b]), weights)
            mark(back)
            back_one.append(exchange(hold(back)))
            grad_memory = total(arrive(grad_memory)).astype(bf16)
            low_memory = [
                dot(tokens, part, 0, 1).astype(bf16) for part in jnp.split(grad_memory, 2, axis=0)
            ]
            mark(*low_memory)
            low_memory = [part.reshape(groups, -1, local) for part in low_memory]
            mine, other = core_half(joined(low_memory, 1))

    raws = total(arrive(raws)).astype(bf16).reshape(groups // 2, 3, -1, local)
    memory_half = plus(mine, arrive(other))
    mark(raws, memory_half)
    raws = joined([raws, memory_half[:, None]], 1)
    cores = [list(range(c, groups, 2)) for c in range(2)]
    raws = lax.psum_scatter(raws, "dp", scatter_dimension=0, axis_index_groups=cores, tiled=True)[0]
    prefix_normed, prefix_normal, prefix_scale = norm_forward(
        picked[:count], gain_one, shift_one
    )
    prefix_low = prefix_normed.astype(bf16)
    grad_front = joined(grad_front, 1)
    wide_front = joined([jnp.zeros((count, local), bf16), grad_front.T], 1)
    low_w_self, gain_term, shift_term = self_weight_grad(
        frames_one, prefix_low, hold(grad_self), wide_front, weights
    )
    grad_w_self = sum_over_clips(low_w_self, 0)
    mark(low_w_self)
    back = self_back(hold(grad_self[-1]), weights)
    mark(back)
    back_one = arrive(back_one)
    back_one.append(exchange(hold(back)))

    def wide(value):
        return value.astype(f32)

    small = []
    gain_term, shift_term = gain_term[:, 0], shift_term[:, 0]
    small.append((gain_term - shift_one * shift_term) / gain_one)
    small.append(shift_term)
    norm_terms = sum(norm_terms[1:], norm_terms[0])
    steps = jnp.where(here == 0, tsteps, 0).astype(f32)
    steps = lax.dynamic_update_slice(jnp.zeros((width,), f32), steps, (there * count,))

    back_prefix = dot(grad_front[:local], w_key, 0, 1) + dot(grad_front[local:], w_value, 0, 1)
    grad_picked = norm_backward(back_prefix, prefix_normal, prefix_scale, gain_one)
    spots = jnp.arange(groups)[:, None, None] == there
    spots = jnp.where(spots, grad_picked[None], 0.0).reshape(groups * count, width)
    small = hold(joined([jnp.stack(small), norm_terms, steps[None], spots], 0))
    small = all_sum(small)
    all_steps = small[6, : groups * count]
    matches = jnp.arange(table.shape[0])[:, None].astype(f32) == all_steps[None, :]
    grad_table = jnp.dot(matches.astype(f32), small[7:], precision=lax.Precision.HIGHEST)

    mark(small)
    back_one[-1] = arrive(back_one[-1])
    back_one = [total(terms) for terms in back_one]
    grad_frames = [
        grad_one[b] + norm_backward(back_one[b], ones[b][1], ones[b][2], gain_one) for b in clips
    ]
    mark(grad_table, *grad_frames)
    grad_w_down = wide(arrive(grad_w_down).T)
    branch = arrive(branch)
    output = [second[b] + branch[b].astype(f32) for b in clips]
    grad_w_gate = wide(arrive(grad_w_gate))
    grad_w_up = arrive(grad_w_up)
    raws = arrive(raws).astype(f32)
    grad_w_self = arrive(grad_w_self)

    depth_c = prompt.shape[-1] // groups

    return (
        jnp.stack(output),
        jnp.stack(grad_frames),
        grad_table,
        small[0],
        small[1],
        small[2],
        small[3],
        small[4],
        small[5],
        wide(grad_w_self[:, :local]),
        wide(grad_w_self[:, local : 2 * local]),
        wide(grad_w_self[:, 2 * local :]),
        raws[2].T,
        raws[0],
        raws[3, :depth_c],
        raws[3, depth_c:],
        raws[1].T,
        grad_w_gate,
        wide(grad_w_up),
        grad_w_down,
    )


def solution(mesh):
    placed = (
        P("dp", "mp", None),
        P("dp", None, None),
        P("dp"),
        P("dp"),
        P(),
        P(),
        P(),
        P(),
        P(),
        P(),
        P(),
        P(None, "mp"),
        P(None, "mp"),
        P(None, "mp"),
        P("mp", None),
        P(None, "mp"),
        P(None, "mp"),
        P(None, "mp"),
        P("mp", None),
        P(None, "mp"),
        P(None, "mp"),
        P("mp", None),
        P("dp", "mp", None),
    )
    return jax.shard_map(
        shards,
        mesh=mesh,
        in_specs=placed,
        out_specs=(
            P("dp", "mp", None),
            P("dp", "mp", None),
            P(),
            P(),
            P(),
            P(),
            P(),
            P(),
            P(),
            P("dp", "mp"),
            P("dp", "mp"),
            P("dp", "mp"),
            P("mp", "dp"),
            P("dp", "mp"),
            P("dp", "mp"),
            P("dp", "mp"),
            P("mp", "dp"),
            P("dp", "mp"),
            P("dp", "mp"),
            P("mp", "dp"),
        ),
        check_vma=False,
    )
```
